32 devices in a mesh: groups: 2 (over x), expert: 16 (over z, y, core).
Axes of the slice: x: 2, y: 2, z: 4, core: 2. Of those that a mesh axis runs over, the one named last changes fastest.
Arguments:
- resid: bfloat16 [2048, 4096], P(('groups', 'expert')), parts along dimension 0, may hold values from -6 to 6
- queries: bfloat16 [2048, 4096], P(('groups', 'expert')), parts along dimension 0, may hold values from -120 to 120
- keys: bfloat16 [2048, 4096], P(('groups', 'expert')), parts along dimension 0, may hold values from -6 to 6
- values: bfloat16 [2048, 4096], P(('groups', 'expert')), parts along dimension 0, may hold values from -6 to 6
- segment_ids: int32 [2048], P(('groups', 'expert')), parts along dimension 0, may hold values from 0 to 3, never falling along the last dimension, each value on 1 to 512 neighbouring positions
- norm_gain: float32 [4096], replicated, may hold values from 0.1 to 1.9
- routes: int32 [2048, 2], P(('groups', 'expert')), parts along dimension 0, may hold values from 0 to 7, all different within a row; in each aligned block of 64 rows (0 to 63, 64 to 127, ...) at most 20 rows name the same one
- route_gates: bfloat16 [2048, 2], P(('groups', 'expert')), parts along dimension 0, may hold values from 0.19921875 to 1
- w_gate: bfloat16 [4096, 16384], P(None, 'expert'), may hold values from -0.09375 to 0.09375
- w_up: bfloat16 [4096, 16384], P(None, 'expert'), may hold values from -0.09375 to 0.09375
- w_down: bfloat16 [16384, 4096], P('expert'), may hold values from -0.0625 to 0.0625
Outputs:
- layer_out: bfloat16 [2048, 4096], P(('groups', 'expert')), parts along dimension 0
The draws below stay inside these ranges and needn't reach their ends.
There are 2 independent parts, one for each index of `groups`. The reference program is written for one: setup_inputs(seed, part) draws one part's arguments, and reference() takes and returns one part's arrays. A program takes and returns all parts, laid end to end along the dimension named above; an argument that names none is the same for every part. Nothing has to cross between parts.
Inputs may be any that keep to these rules, and one draw needn't show every extreme that they name: `routes`: in each token's row the experts differ; in the rows of one device no expert is named more than 20 times, a bound that some block reaches.
All inputs are finite; a program needn't handle non-finite values.
Results may differ from the reference program's by a relative error of at most 0.0037.
Values may be sent and summed in bfloat16 or wider, within the bound.
No kernel may reach another device: no remote copies, remote signals or barrier semaphores. Data moves between devices by JAX's collectives and lax.ppermute only.
A program may use at most 128 MiB of HBM per device.

```python
import math
import jax
import jax.numpy as jnp
import numpy as np
from jax import lax

D = 4096
HEADS = 32
HEAD_DIM = 128
FF = 8192
EXPERTS = 8
E_WIN = 2
TOP = 2
TOK_DEV = 64
CAP = 20
SPAN = 192
TOKENS = 1024
N_EXPERT = 16


def shared_keys(key):
    return jax.random.truncated_normal(key, -6.0, 6.0, (TOKENS, D), jnp.float32)


def draw_keys(key, part):
    base = shared_keys(key)
    return base.astype(jnp.bfloat16)


def draw_queries(key, part):
    key = jax.random.fold_in(key, 11)
    fresh = jax.random.truncated_normal(key, -6.0, 6.0, (TOKENS, D), jnp.float32)
    return fresh.astype(jnp.bfloat16)


def block_levels(key, shape, cuts, least, top_value):
    loudness = 1.0
    for axis_at, shards_of in cuts:
        steps = jax.random.uniform(jax.random.fold_in(jax.random.fold_in(key, 6), axis_at), (shards_of,), jnp.float32, least / len(cuts), top_value / len(cuts))
        loudness = loudness * jnp.repeat(jnp.exp(steps), shape[axis_at] // shards_of).reshape((-1,) + (1,) * (len(shape) - 1 - axis_at))
    return loudness


def length_profile(number_of, total, most, skew):
    portions = [(1 << 20) // math.isqrt(standing ** skew) + 1 for standing in range(2, number_of + 1)]
    surplus, holding = total - most - (number_of - 1), [1] * (number_of - 1)
    while surplus > 0:
        free = [i for i in range(number_of - 1) if holding[i] < most]
        whole, left = sum([portions[i] for i in free]), surplus
        for i in free:
            more = min(most - holding[i], max(1, left * portions[i] // whole), surplus)
            holding[i] = holding[i] + more
            surplus = surplus - more
    return np.array([most] + holding)


def ragged_sizes(stream_key, number_of, total, reach, lean):
    if number_of == 2:
        one = jax.random.randint(stream_key, (), max(1, total - reach), min(reach, total - 1) + 1)
        return jnp.stack([one, total - one])
    lengths = jnp.asarray(length_profile(number_of, total, reach, lean), jnp.int32)
    twos = (number_of - 1) // 2
    source_of, receiver = lengths[1:1 + 2 * twos:2], lengths[2:2 + 2 * twos:2]
    slack = jnp.minimum(source_of - 1, reach - receiver)
    passed = jax.random.randint(jax.random.fold_in(stream_key, 1), (twos,), 0, 1 << 20) % (slack + 1)
    lengths = lengths.at[1:1 + 2 * twos:2].set(source_of - passed).at[2:2 + 2 * twos:2].set(receiver + passed)
    return lengths[jax.random.permutation(jax.random.fold_in(stream_key, 2), number_of)]


def shared_out(own_key, own, number, rows, number_of, top, most, skew):
    ranking = jax.random.permutation(own_key, number_of)
    heavy_load, ordinary = portions_of(number_of, rows * top, most, skew, True), portions_of(number_of, rows * top, most, skew, False)
    places = jnp.arange(number_of)

    def named(sizes, turn):
        used = int((sizes > 0).sum())
        fixed = max(1, used // 4)
        passed = fixed + (places - fixed + turn * (used - fixed)) % max(1, number_of - fixed)
        return jnp.zeros((number_of,), jnp.int32).at[ranking[jnp.where(places < fixed, places, passed)]].set(jnp.asarray(sizes, jnp.int32))

    sizes = jnp.where(number % 4 == 0, named(heavy_load, number // 4), named(ordinary, number - number // 4 - 1))
    mixed = jax.random.permutation(jax.random.fold_in(own, 3), number_of)
    donor, taker = mixed[0:number_of // 2 * 2:2], mixed[1:number_of // 2 * 2:2]
    room = jnp.minimum(sizes[donor] - 1, most - sizes[taker]) // 2
    room = jnp.where((donor == ranking[0]) | (taker == ranking[0]) | (sizes[taker] == 0), 0, jnp.maximum(room, 0))
    passed = jax.random.randint(jax.random.fold_in(own, 4), (number_of // 2,), 0, 1 << 20) % (room + 1)
    sizes = sizes.at[donor].add(-passed).at[taker].add(passed)
    members = jnp.searchsorted(jnp.cumsum(sizes), jnp.arange(rows * top), side="right").astype(jnp.int32)
    table = members.reshape(top, rows).T
    table = table[jax.random.permutation(jax.random.fold_in(own, 1), rows)]
    turn = jax.random.randint(jax.random.fold_in(own, 2), (rows, 1), 0, top)
    return jnp.take_along_axis(table, (jnp.arange(top)[None, :] + turn) % top, axis=1)


def portions_of(count, total, reach, slope, full):
    weights = [(1 << 20) // math.isqrt(standing ** slope) + 1 for standing in range(1, count + 1)]
    largest = reach if full else min(reach, max(-(-total // count), total * weights[0] // sum(weights)))
    least = 1 if total - largest >= count - 1 else 0
    holding, surplus = [largest] + [least] * (count - 1), total - largest - least * (count - 1)
    while surplus > 0:
        movable = [i for i in range(1, count) if holding[i] < largest] or [i for i in range(1, count) if holding[i] < reach]
        whole, budget = sum([weights[i] for i in movable]), surplus
        for i in movable:
            more = min(reach - holding[i], max(1, budget * weights[i] // whole), surplus)
            holding[i] = holding[i] + more
            surplus = surplus - more
    return np.array(holding)


def bell_draw(rng, extent, scale, most, cuts=(), held_as=jnp.bfloat16):
    values = jax.random.normal(rng, extent, jnp.float32) * scale
    if len(cuts) > 0:
        values = block_levels(rng, extent, cuts, -0.22, 0.18) * values
    return jnp.clip(values, min=-most, max=most).astype(held_as)


def setup_inputs(seed: int = 0, part: int = 0) -> dict:
    key_list = jax.random.split(jax.random.key(seed), 12)
    part_keys = jax.random.split(jax.random.fold_in(key_list[11], part), 12)
    resid = bell_draw(part_keys[0], (TOKENS, D), 1.0, 6.0, ((0, 16),))
    queries = draw_queries(jax.random.fold_in(jax.random.fold_in(key_list[11], part), 71), part)
    keys = draw_keys(jax.random.fold_in(jax.random.fold_in(key_list[11], part), 71), part)
    values = bell_draw(part_keys[3], (TOKENS, D), 1.0, 6.0, ((0, 16),))
    segment_ids = jnp.searchsorted(jnp.cumsum(ragged_sizes(part_keys[4], 4, TOKENS, TOKENS // 2, 1)), jnp.arange(TOKENS), side="right").astype(jnp.int32)
    norm_gain = jnp.clip(1.0 + 0.18 * jax.random.normal(key_list[5], (D,), jnp.float32), 0.1, 1.9)
    routes_keys = jax.random.split(jax.random.fold_in(part_keys[6], 1), TOKENS // TOK_DEV)
    routes_turns = jax.random.permutation(jax.random.fold_in(part_keys[6], 3), TOKENS // TOK_DEV)
    routes = jax.vmap(lambda own, number: shared_out(jax.random.fold_in(part_keys[6], 2), own, number, TOK_DEV, EXPERTS, TOP, CAP, 2))(routes_keys, routes_turns).reshape((TOKENS, TOP))
    route_gates = jnp.clip(0.19921875 + 0.80078125 * jax.random.uniform(part_keys[7], (TOKENS, TOP), jnp.float32) ** block_levels(part_keys[7], (TOKENS, TOP), ((0, 16),), -0.2, 0.2), 0.19921875, 1.0).astype(jnp.bfloat16)
    w_gate = bell_draw(key_list[8], (D, E_WIN * FF), D ** -0.5, 0.09375, ((1, 16),))
    w_up = bell_draw(key_list[9], (D, E_WIN * FF), D ** -0.5, 0.09375, ((1, 16),))
    w_down = bell_draw(key_list[10], (E_WIN * FF, D), FF ** -0.5, 0.0625, ((0, 16),))
    return {"resid": resid, "queries": queries, "keys": keys, "values": values, "segment_ids": segment_ids, "norm_gain": norm_gain, "routes": routes, "route_gates": route_gates, "w_gate": w_gate, "w_up": w_up, "w_down": w_down}


def reference(resid, queries, keys, values, segment_ids, norm_gain, routes, route_gates, w_gate, w_up, w_down):
    softmax_scale = 1.0 / HEAD_DIM ** 0.5
    positions = jnp.arange(TOKENS)
    distance = positions[:, None] - positions[None, :]
    allowed = (distance >= 0) & (distance <= SPAN) & (segment_ids[:, None] == segment_ids[None, :])
    query_heads = queries.reshape(TOKENS, HEADS, HEAD_DIM).transpose(1, 0, 2)
    key_heads = keys.reshape(TOKENS, HEADS, HEAD_DIM).transpose(1, 0, 2)
    value_heads = values.reshape(TOKENS, HEADS, HEAD_DIM).transpose(1, 0, 2)

    def one_head(operands):
        query_h, key_h, value_h = operands
        scores = jnp.dot(query_h, key_h.T, preferred_element_type=jnp.float32) * softmax_scale
        scores = jnp.where(allowed, scores, -1e+30)
        rowmax = lax.optimization_barrier(jnp.max(scores, axis=1, keepdims=True))
        expo = jnp.where(allowed, jnp.exp(scores - rowmax), 0.0)
        denom = lax.optimization_barrier(jnp.sum(expo, axis=1, keepdims=True))
        numer = jnp.dot(expo.astype(jnp.bfloat16), value_h, preferred_element_type=jnp.float32)
        return numer / denom
    attended = lax.map(one_head, (query_heads, key_heads, value_heads))
    attended = attended.transpose(1, 0, 2).reshape(TOKENS, D)
    mixed = resid.astype(jnp.float32) + attended
    normed = (mixed * lax.rsqrt(lax.optimization_barrier(jnp.mean(mixed * mixed, axis=1, keepdims=True)) + 1e-05) * norm_gain).astype(jnp.bfloat16)
    shard_count = N_EXPERT // E_WIN
    ff_local = FF // shard_count
    limit = N_EXPERT * CAP
    result = mixed
    for expert_id in range(E_WIN):
        chosen_slot = routes == expert_id
        weighting = lax.optimization_barrier(jnp.sum(jnp.where(chosen_slot, route_gates.astype(jnp.float32), 0.0), axis=1))
        chosen = jnp.any(chosen_slot, axis=1)
        picked = jnp.nonzero(chosen, size=limit, fill_value=0)[0].astype(jnp.int32)
        live = jnp.sum(chosen.astype(jnp.int32))
        is_valid = jnp.arange(limit) < live
        in_rows = normed[picked]

        def shard_step(shard, accum):
            column = (expert_id * FF + shard * ff_local).astype(jnp.int32)
            gate_slice = lax.dynamic_slice_in_dim(w_gate, column, ff_local, 1)
            up_slice = lax.dynamic_slice_in_dim(w_up, column, ff_local, 1)
            down_slice = lax.dynamic_slice_in_dim(w_down, column, ff_local, 0)
            gate_proj = jnp.dot(in_rows, gate_slice, preferred_element_type=jnp.float32)
            up_proj = jnp.dot(in_rows, up_slice, preferred_element_type=jnp.float32)
            hidden = (jax.nn.silu(gate_proj) * up_proj).astype(jnp.bfloat16)
            partial_out = jnp.dot(hidden, down_slice, preferred_element_type=jnp.float32).astype(jnp.bfloat16)
            return accum + partial_out.astype(jnp.float32)
        expert_out = lax.fori_loop(0, shard_count, shard_step, jnp.zeros((limit, D), jnp.float32))
        scaling = jnp.where(is_valid, weighting[picked], 0.0)
        result = result.at[picked].add(expert_out * scaling[:, None])
    return result.astype(jnp.bfloat16)
```

```python
import functools

import jax
import jax.numpy as jnp
from jax import lax
from jax.experimental import pallas as pl
from jax.experimental.pallas import tpu as pltpu
from jax.sharding import PartitionSpec as P

HEAD_DIM = 128
E_WIN = 2
WIN_DEV = 3
CAP = 20
HEADS_STEP = 4
MASKED = -1e30


def attention_kernel(
    deltas, q, k0, v0, k1, v1, k2, v2, k3, v3, segs, resid, gain, routes, gates,
    mixed_out, keep_out, send_out, weight_out, mask,
):
    step = pl.program_id(0)
    steps = pl.num_programs(0)
    rows = q.shape[0]
    keys = (WIN_DEV + 1) * rows

    @pl.when(step == 0)
    def _():
        seg_row = segs[...]
        eye = lax.broadcasted_iota(jnp.int32, (rows, rows), 0) == lax.broadcasted_iota(
            jnp.int32, (rows, rows), 1
        )
        seg_col = jnp.sum(jnp.where(eye, seg_row[:, :rows], 0), axis=1, keepdims=True)
        lane = lax.broadcasted_iota(jnp.int32, (rows, keys), 1)
        sub = lax.broadcasted_iota(jnp.int32, (rows, keys), 0)
        block = lane // rows
        back = jnp.where(
            block == 0,
            deltas[0],
            jnp.where(block == 1, deltas[1], jnp.where(block == 2, deltas[2], deltas[3])),
        )
        distance = sub - (lane - block * rows) + back * rows
        allowed = (distance >= 0) & (distance <= WIN_DEV * rows) & (seg_col == seg_row)
        mask[...] = jnp.where(allowed, 1.0, 0.0)

    allowed = mask[...] > 0.5
    scale = 1.0 / HEAD_DIM**0.5
    outs = []
    for head in range(HEADS_STEP):
        cols = slice(head * HEAD_DIM, (head + 1) * HEAD_DIM)
        key_h = jnp.concatenate([k0[:, cols], k1[:, cols], k2[:, cols], k3[:, cols]], axis=0)
        value_h = jnp.concatenate([v0[:, cols], v1[:, cols], v2[:, cols], v3[:, cols]], axis=0)
        scores = (
            lax.dot_general(
                q[:, cols], key_h, (((1,), (1,)), ((), ())), preferred_element_type=jnp.float32
            )
            * scale
        )
        scores = jnp.where(allowed, scores, MASKED)
        rowmax = jnp.max(scores, axis=1, keepdims=True)
        expo = jnp.where(allowed, jnp.exp(scores - rowmax), 0.0)
        denom = jnp.sum(expo, axis=1, keepdims=True)
        numer = jnp.dot(expo.astype(jnp.bfloat16), value_h, preferred_element_type=jnp.float32)
        outs.append(numer / denom)
    attended = jnp.concatenate(outs, axis=1)
    width = HEADS_STEP * HEAD_DIM
    at = pl.ds(pl.multiple_of(step * width, width), width)
    mixed_out[:, at] = resid[...].astype(jnp.float32) + attended

    @pl.when(step == steps - 1)
    def _():
        mixed = mixed_out[...]
        normed = (
            mixed * lax.rsqrt(jnp.mean(mixed * mixed, axis=1, keepdims=True) + 1e-05) * gain[...]
        ).astype(jnp.bfloat16)
        upper = (
            lax.broadcasted_iota(jnp.int32, (rows, rows), 0)
            < lax.broadcasted_iota(jnp.int32, (rows, rows), 1)
        ).astype(jnp.float32).astype(jnp.bfloat16)
        slot = lax.broadcasted_iota(jnp.int32, (CAP, rows), 0)
        for place, out in ((0, keep_out), (1, send_out)):
            expert = jnp.where(place == 0, deltas[4], 1 - deltas[4])
            hit = routes[...] == expert
            member = jnp.max(jnp.where(hit, 1.0, 0.0), axis=0, keepdims=True)
            weight = jnp.sum(
                jnp.where(hit, gates[...].astype(jnp.float32), 0.0), axis=0, keepdims=True
            )
            rank = jnp.dot(
                jnp.broadcast_to(member, (8, rows)).astype(jnp.bfloat16),
                upper,
                preferred_element_type=jnp.float32,
            )[0:1].astype(jnp.int32)
            pick = jnp.where((slot == rank) & (member > 0.5), 1.0, 0.0)
            out[...] = jnp.dot(
                pick.astype(jnp.bfloat16), normed, preferred_element_type=jnp.float32
            ).astype(jnp.bfloat16)
            weight_out[place] = (pick * weight).astype(jnp.bfloat16)


def attention(deltas, q, k_own, v_own, arrived, segs, resid, gain, routes, gates):
    rows, width = q.shape
    cols = HEADS_STEP * HEAD_DIM
    steps = width // cols
    top = routes.shape[0]
    first = pl.BlockSpec((rows, cols), lambda j, *_: (0, j))
    second = pl.BlockSpec((rows, cols), lambda j, *_: (1, j))

    def whole(shape):
        return pl.BlockSpec(shape, lambda j, *_: (0,) * len(shape))

    pairs = []
    pair_specs = []
    for block in arrived:
        pairs += [block, block]
        pair_specs += [first, second]
    return pl.pallas_call(
        attention_kernel,
        grid_spec=pltpu.PrefetchScalarGridSpec(
            num_scalar_prefetch=1,
            grid=(steps,),
            in_specs=[first, first, first]
            + pair_specs
            + [
                whole((1, (WIN_DEV + 1) * rows)),
                first,
                whole((1, width)),
                whole((top, rows)),
                whole((top, rows)),
            ],
            out_specs=[
                whole((rows, width)),
                whole((CAP, width)),
                whole((CAP, width)),
                whole((E_WIN, CAP, rows)),
            ],
            scratch_shapes=[pltpu.VMEM((rows, (WIN_DEV + 1) * rows), jnp.float32)],
        ),
        out_shape=[
            jax.ShapeDtypeStruct((rows, width), jnp.float32),
            jax.ShapeDtypeStruct((CAP, width), jnp.bfloat16),
            jax.ShapeDtypeStruct((CAP, width), jnp.bfloat16),
            jax.ShapeDtypeStruct((E_WIN, CAP, rows), jnp.bfloat16),
        ],
        compiler_params=pltpu.CompilerParams(vmem_limit_bytes=24 * 1024 * 1024),
        cost_estimate=pl.CostEstimate(
            flops=4 * rows * 4 * rows * width, bytes_accessed=8 * rows * width * 4,
            transcendentals=rows * 4 * rows * (width // HEAD_DIM),
        ),
        name="attention",
    )(deltas, q, k_own, v_own, *pairs, segs, resid, gain, routes, gates)


def experts_kernel(first_steps, x, w_gate, w_up, w_down, out, hidden):
    step = pl.program_id(0)
    cols = w_gate.shape[1]

    @pl.when(step < first_steps)
    def _():
        rows = x[...]
        gate = jnp.dot(rows, w_gate[...], preferred_element_type=jnp.float32)
        up = jnp.dot(rows, w_up[...], preferred_element_type=jnp.float32)
        at = pl.ds(pl.multiple_of(step * cols, cols), cols)
        hidden[:, at] = (jax.nn.silu(gate) * up).astype(jnp.bfloat16)

    @pl.when(step >= first_steps)
    def _():
        out[...] = jnp.dot(
            hidden[...], w_down[...], preferred_element_type=jnp.float32
        ).astype(jnp.bfloat16)


def experts(x, w_gate, w_up, w_down):
    rows, width = x.shape
    units = w_gate.shape[1]
    cols = min(256, units)
    first_steps = units // cols
    out_cols = 1024
    second_steps = width // out_cols
    return pl.pallas_call(
        functools.partial(experts_kernel, first_steps),
        grid=(first_steps + second_steps,),
        in_specs=[
            pl.BlockSpec((rows, width), lambda j: (0, 0)),
            pl.BlockSpec((width, cols), lambda j: (0, jnp.minimum(j, first_steps - 1))),
            pl.BlockSpec((width, cols), lambda j: (0, jnp.minimum(j, first_steps - 1))),
            pl.BlockSpec((units, out_cols), lambda j: (0, jnp.maximum(j - first_steps, 0))),
        ],
        out_specs=pl.BlockSpec((rows, out_cols), lambda j: (0, jnp.maximum(j - first_steps, 0))),
        out_shape=jax.ShapeDtypeStruct((rows, width), jnp.bfloat16),
        scratch_shapes=[pltpu.VMEM((rows, units), jnp.bfloat16)],
        compiler_params=pltpu.CompilerParams(vmem_limit_bytes=48 * 1024 * 1024),
        cost_estimate=pl.CostEstimate(
            flops=6 * rows * width * units,
            bytes_accessed=6 * width * units + 4 * rows * width,
            transcendentals=rows * units,
        ),
        name="experts",
    )(x, w_gate, w_up, w_down)


def combine_kernel(mixed, weight, own, other, out):
    total = mixed[...]
    for place, part in ((0, own[...][:CAP]), (1, other[...])):
        total = total + lax.dot_general(
            weight[place], part, (((0,), (0,)), ((), ())), preferred_element_type=jnp.float32
        )
    out[...] = total.astype(jnp.bfloat16)


def combine(mixed, weight, own, other):
    rows, width = mixed.shape
    cols = 1024
    return pl.pallas_call(
        combine_kernel,
        grid=(width // cols,),
        in_specs=[
            pl.BlockSpec((rows, cols), lambda j: (0, j)),
            pl.BlockSpec(weight.shape, lambda j: (0, 0, 0)),
            pl.BlockSpec((own.shape[0], cols), lambda j: (0, j)),
            pl.BlockSpec((other.shape[0], cols), lambda j: (0, j)),
        ],
        out_specs=pl.BlockSpec((rows, cols), lambda j: (0, j)),
        out_shape=jax.ShapeDtypeStruct((rows, width), jnp.bfloat16),
        name="combine",
    )(mixed, weight, own, other)


def shards(
    resid, queries, keys, values, segment_ids, norm_gain, routes, route_gates, w_gate, w_up, w_down
):
    tok_rows = resid.shape[0]
    count = lax.axis_size("expert")
    own = lax.axis_index("expert")
    shard_count = count // E_WIN
    odd = own % 2

    both = jnp.concatenate([keys, values], axis=0)
    two_back = lax.ppermute(both, "expert", [(i, i + 2) for i in range(count - 2)])
    crossing = [(i, i + 1) for i in range(0, count, 2)]
    crossing += [(i, i + 3) for i in range(1, count - 3, 2)]
    crossed = lax.ppermute(both, "expert", crossing)
    mirrored = lax.ppermute(two_back, "expert", [(i, i ^ 1) for i in range(count)])
    delta_list = [0 * own, 0 * own + 2, 3 - 2 * odd, 1 + 2 * odd]

    seg_all = lax.all_gather(segment_ids, "expert", axis=0, tiled=True)
    segs = [
        lax.dynamic_slice_in_dim(seg_all, jnp.maximum(own - delta, 0) * tok_rows, tok_rows)
        for delta in delta_list
    ]
    segs = jnp.concatenate(segs).reshape(1, -1)
    far = 2 * WIN_DEV + 2
    my_expert = own // shard_count
    scalars = jnp.stack(
        [jnp.where(own >= delta, delta, far) for delta in delta_list] + [my_expert]
    ).astype(jnp.int32)

    mixed, keep, send, weight = attention(
        scalars, queries, keys, values, [two_back, crossed, mirrored], segs, resid,
        norm_gain.reshape(1, -1), routes.T, route_gates.T,
    )
    partner = [(i, (i + shard_count) % count) for i in range(count)]
    got = lax.ppermute(send, "expert", partner)
    pair_rows = jnp.concatenate([keep, got], axis=0)
    halves = [list(range(e * shard_count, (e + 1) * shard_count)) for e in range(E_WIN)]
    in_rows = lax.all_gather(pair_rows, "expert", axis=0, tiled=True, axis_index_groups=halves)
    partial_out = experts(in_rows, w_gate, w_up, w_down)
    summed = lax.psum_scatter(
        partial_out, "expert", scatter_dimension=0, tiled=True, axis_index_groups=halves
    )
    back = lax.ppermute(summed[CAP:], "expert", partner)
    return combine(mixed, weight, summed, back)


def solution(mesh):
    placed = (
        P(("groups", "expert"), None),
        P(("groups", "expert"), None),
        P(("groups", "expert"), None),
        P(("groups", "expert"), None),
        P(("groups", "expert")),
        P(),
        P(("groups", "expert"), None),
        P(("groups", "expert"), None),
        P(None, "expert"),
        P(None, "expert"),
        P("expert", None),
    )
    return jax.shard_map(
        shards, mesh=mesh, in_specs=placed, out_specs=P(("groups", "expert"), None), check_vma=False
    )
```

```python
import functools

import jax
import jax.numpy as jnp
from jax import lax
from jax.experimental import pallas as pl
from jax.experimental.pallas import tpu as pltpu
from jax.sharding import PartitionSpec as P

HEAD_DIM = 128
E_WIN = 2
WIN_DEV = 3
CAP = 20
EARLY = 16
LATE = 2 * CAP - EARLY
HEADS_STEP = 8
MASKED = -1e30
MIB = 1024 * 1024


def attention_kernel(
    deltas, q, k0, v0, k1, v1, k2, v2, k3, v3, segs, resid, gain, routes, gates,
    mixed_out, early_out, rest_out, send_out, weight_out, bias,
):
    step = pl.program_id(0)
    steps = pl.num_programs(0)
    rows = q.shape[0]
    keys = (WIN_DEV + 1) * rows

    @pl.when(step == 0)
    def _():
        seg_row = segs[...]
        eye = lax.broadcasted_iota(jnp.int32, (rows, rows), 0) == lax.broadcasted_iota(
            jnp.int32, (rows, rows), 1
        )
        seg_col = jnp.sum(jnp.where(eye, seg_row[:, :rows], 0), axis=1, keepdims=True)
        lane = lax.broadcasted_iota(jnp.int32, (rows, keys), 1)
        sub = lax.broadcasted_iota(jnp.int32, (rows, keys), 0)
        block = lane // rows
        back = jnp.where(
            block == 0,
            deltas[0],
            jnp.where(block == 1, deltas[1], jnp.where(block == 2, deltas[2], deltas[3])),
        )
        distance = sub - (lane - block * rows) + back * rows
        allowed = (distance >= 0) & (distance <= WIN_DEV * rows) & (seg_col == seg_row)
        bias[...] = jnp.where(allowed, 0.0, MASKED)

    scale = 1.0 / HEAD_DIM**0.5
    heads = [slice(head * HEAD_DIM, (head + 1) * HEAD_DIM) for head in range(HEADS_STEP)]
    scores = jnp.stack(
        [
            lax.dot_general(
                q[:, cols],
                jnp.concatenate([k0[:, cols], k1[:, cols], k2[:, cols], k3[:, cols]], axis=0),
                (((1,), (1,)), ((), ())),
                preferred_element_type=jnp.float32,
            )
            for cols in heads
        ]
    )
    scores = scores * scale + bias[...][None]
    expo = jnp.exp(scores - jnp.max(scores, axis=2, keepdims=True))
    denom = jnp.sum(expo, axis=2, keepdims=True)
    probs = expo.astype(jnp.bfloat16)
    outs = [
        jnp.dot(
            probs[head],
            jnp.concatenate([v0[:, cols], v1[:, cols], v2[:, cols], v3[:, cols]], axis=0),
            preferred_element_type=jnp.float32,
        )
        / denom[head]
        for head, cols in enumerate(heads)
    ]
    width = HEADS_STEP * HEAD_DIM
    at = pl.ds(pl.multiple_of(step * width, width), width)
    mixed_out[:, at] = resid[...].astype(jnp.float32) + jnp.concatenate(outs, axis=1)

    @pl.when(step == steps - 1)
    def _():
        mixed = mixed_out[...]
        normed = (
            mixed * lax.rsqrt(jnp.mean(mixed * mixed, axis=1, keepdims=True) + 1e-05) * gain[...]
        ).astype(jnp.bfloat16)
        across = lax.broadcasted_iota(jnp.int32, (rows, rows), 1)
        down = lax.broadcasted_iota(jnp.int32, (rows, rows), 0)
        upper = jnp.where(down < across, 1.0, 0.0).astype(jnp.bfloat16)
        eye = jnp.where(down == across, 1.0, 0.0).astype(jnp.bfloat16)
        slot = lax.broadcasted_iota(jnp.int32, (32, rows), 0)

        def picks(expert):
            hit = routes[...] == expert
            member = jnp.max(jnp.where(hit, 1.0, 0.0), axis=0, keepdims=True)
            weight = jnp.sum(
                jnp.where(hit, gates[...].astype(jnp.float32), 0.0), axis=0, keepdims=True
            )
            rank = jnp.dot(
                jnp.broadcast_to(member, (8, rows)).astype(jnp.bfloat16),
                upper,
                preferred_element_type=jnp.float32,
            )[0:1].astype(jnp.int32)
            return member > 0.5, weight, rank

        def spread(pick, weight):
            return lax.dot_general(
                eye,
                jnp.where(pick, weight, 0.0).astype(jnp.bfloat16),
                (((1,), (1,)), ((), ())),
                preferred_element_type=jnp.float32,
            ).astype(jnp.bfloat16)

        def packed(pick):
            return jnp.dot(
                jnp.where(pick, 1.0, 0.0).astype(jnp.bfloat16),
                normed,
                preferred_element_type=jnp.float32,
            ).astype(jnp.bfloat16)

        member, weight, rank = picks(deltas[4])
        pick = (slot == rank) & member
        mine = packed(pick)
        early_out[...] = mine[:EARLY]
        rest_out[...] = mine[EARLY:CAP]
        weight_out[0] = spread(pick & (slot < EARLY), weight)
        weight_out[1] = spread((slot - CAP + EARLY == rank) & (slot >= CAP) & member, weight)
        member, weight, rank = picks(1 - deltas[4])
        pick = (slot == rank) & member
        send_out[...] = packed(pick)[:CAP]
        weight_out[2] = spread(pick, weight)


def attention(deltas, q, pairs, segs, resid, gain, routes, gates):
    rows, width = q.shape
    cols = HEADS_STEP * HEAD_DIM
    top = routes.shape[0]
    piece = pl.BlockSpec((rows, cols), lambda j, *_: (0, j))

    def whole(shape):
        return pl.BlockSpec(shape, lambda j, *_: (0,) * len(shape))

    return pl.pallas_call(
        attention_kernel,
        grid_spec=pltpu.PrefetchScalarGridSpec(
            num_scalar_prefetch=1,
            grid=(width // cols,),
            in_specs=[piece] * (1 + len(pairs))
            + [
                whole((1, (WIN_DEV + 1) * rows)),
                piece,
                whole((1, width)),
                whole((top, rows)),
                whole((top, rows)),
            ],
            out_specs=[
                whole((rows, width)),
                whole((EARLY, width)),
                whole((CAP - EARLY, width)),
                whole((CAP, width)),
                whole((3, rows, 32)),
            ],
            scratch_shapes=[pltpu.VMEM((rows, (WIN_DEV + 1) * rows), jnp.float32)],
        ),
        out_shape=[
            jax.ShapeDtypeStruct((rows, width), jnp.float32),
            jax.ShapeDtypeStruct((EARLY, width), jnp.bfloat16),
            jax.ShapeDtypeStruct((CAP - EARLY, width), jnp.bfloat16),
            jax.ShapeDtypeStruct((CAP, width), jnp.bfloat16),
            jax.ShapeDtypeStruct((3, rows, 32), jnp.bfloat16),
        ],
        compiler_params=pltpu.CompilerParams(vmem_limit_bytes=56 * MIB),
        cost_estimate=pl.CostEstimate(
            flops=4 * rows * 4 * rows * width, bytes_accessed=8 * rows * width * 4,
            transcendentals=rows * 4 * rows * (width // HEAD_DIM),
        ),
        name="attention",
    )(deltas, q, *pairs, segs, resid, gain, routes, gates)


def experts_kernel(
    depth, out_cols, x, w_gate, w_up, w_down, out,
    gate_held, up_held, down_held, gate_sum, up_sum, hidden, first_sems, second_sems,
):
    width, units = gate_held.shape
    first = []
    for part in range(width // depth):
        at = pl.ds(part * depth, depth)
        first.append(
            (
                pltpu.make_async_copy(w_gate.at[at], gate_held.at[at], first_sems.at[0, part]),
                pltpu.make_async_copy(w_up.at[at], up_held.at[at], first_sems.at[1, part]),
            )
        )
    second = []
    for part in range(width // out_cols):
        at = pl.ds(part * out_cols, out_cols)
        second.append(
            pltpu.make_async_copy(w_down.at[:, at], down_held.at[:, at], second_sems.at[part])
        )
    for gate_copy, up_copy in first:
        gate_copy.start()
        up_copy.start()
    for copy in second:
        copy.start()
    for part, (gate_copy, up_copy) in enumerate(first):
        at = slice(part * depth, (part + 1) * depth)
        piece = x[:, at]
        gate_copy.wait()
        gate = jnp.dot(piece, gate_held[at], preferred_element_type=jnp.float32)
        up_copy.wait()
        up = jnp.dot(piece, up_held[at], preferred_element_type=jnp.float32)
        if part == 0:
            gate_sum[...] = gate
            up_sum[...] = up
        else:
            gate_sum[...] += gate
            up_sum[...] += up
    hidden[...] = (jax.nn.silu(gate_sum[...]) * up_sum[...]).astype(jnp.bfloat16)
    for part, copy in enumerate(second):
        at = slice(part * out_cols, (part + 1) * out_cols)
        copy.wait()
        out[:, at] = jnp.dot(
            hidden[...], down_held[:, at], preferred_element_type=jnp.float32
        ).astype(jnp.bfloat16)


def experts(x, w_gate, w_up, w_down):
    rows, width = x.shape
    units = w_gate.shape[1]
    depth = 512
    out_cols = 512
    in_place = pl.BlockSpec(memory_space=pl.ANY)
    near = pl.BlockSpec(memory_space=pltpu.VMEM)
    return pl.pallas_call(
        functools.partial(experts_kernel, depth, out_cols),
        in_specs=[near, in_place, in_place, in_place],
        out_specs=near,
        out_shape=jax.ShapeDtypeStruct((rows, width), jnp.bfloat16),
        scratch_shapes=[
            pltpu.VMEM((width, units), jnp.bfloat16),
            pltpu.VMEM((width, units), jnp.bfloat16),
            pltpu.VMEM((units, width), jnp.bfloat16),
            pltpu.VMEM((rows, units), jnp.float32),
            pltpu.VMEM((rows, units), jnp.float32),
            pltpu.VMEM((rows, units), jnp.bfloat16),
            pltpu.SemaphoreType.DMA((2, width // depth)),
            pltpu.SemaphoreType.DMA((width // out_cols,)),
        ],
        compiler_params=pltpu.CompilerParams(vmem_limit_bytes=56 * MIB),
        cost_estimate=pl.CostEstimate(
            flops=6 * rows * width * units,
            bytes_accessed=6 * width * units + 4 * rows * width,
            transcendentals=rows * units,
        ),
        name="experts",
    )(x, w_gate, w_up, w_down)


def combine_kernel(mixed, weight, early, late, other, out):
    total = mixed[...]
    for place, part in enumerate((early, late, other)):
        total = total + jnp.dot(
            weight[place][:, : part.shape[0]], part[...], preferred_element_type=jnp.float32
        )
    out[...] = total.astype(jnp.bfloat16)


def combine(mixed, weight, early, late, other):
    rows, width = mixed.shape
    cols = 2048

    def piece(count):
        return pl.BlockSpec((count, cols), lambda j: (0, j))

    return pl.pallas_call(
        combine_kernel,
        grid=(width // cols,),
        in_specs=[
            piece(rows),
            pl.BlockSpec(weight.shape, lambda j: (0, 0, 0)),
            piece(early.shape[0]),
            piece(late.shape[0]),
            piece(other.shape[0]),
        ],
        out_specs=piece(rows),
        out_shape=jax.ShapeDtypeStruct((rows, width), jnp.bfloat16),
        compiler_params=pltpu.CompilerParams(vmem_limit_bytes=56 * MIB),
        name="combine",
    )(mixed, weight, early, late, other)


def shards(
    resid, queries, keys, values, segment_ids, norm_gain, routes, route_gates, w_gate, w_up, w_down
):
    tok_rows = resid.shape[0]
    count = lax.axis_size("expert")
    own = lax.axis_index("expert")
    shard_count = count // E_WIN
    odd = own % 2

    next_chip = [(i, i + 2) for i in range(count - 2)]
    crossing = [(i, i + 1) for i in range(0, count, 2)]
    crossing += [(i, i + 3) for i in range(1, count - 3, 2)]
    mirror = [(i, i ^ 1) for i in range(count)]
    key_two = lax.ppermute(keys, "expert", next_chip)
    value_two = lax.ppermute(values, "expert", next_chip)
    key_cross = lax.ppermute(keys, "expert", crossing)
    value_cross = lax.ppermute(values, "expert", crossing)
    key_two, seg_held = lax.optimization_barrier((key_two, segment_ids))
    key_mirror = lax.ppermute(key_two, "expert", mirror)
    value_mirror = lax.ppermute(value_two, "expert", mirror)
    seg_two = lax.ppermute(seg_held, "expert", next_chip)
    seg_cross = lax.ppermute(seg_held, "expert", crossing)
    seg_mirror = lax.ppermute(seg_two, "expert", mirror)
    segs = jnp.concatenate([segment_ids, seg_two, seg_cross, seg_mirror]).reshape(1, -1)

    far = 2 * WIN_DEV + 2
    delta_list = [0 * own, 0 * own + 2, 3 - 2 * odd, 1 + 2 * odd]
    my_expert = own // shard_count
    scalars = jnp.stack(
        [jnp.where(own >= delta, delta, far) for delta in delta_list] + [my_expert]
    ).astype(jnp.int32)

    mixed, early, rest, send, weight = attention(
        scalars,
        queries,
        [keys, values, key_two, value_two, key_cross, value_cross, key_mirror, value_mirror],
        segs, resid, norm_gain.reshape(1, -1), routes.T, route_gates.T,
    )
    partner = [(i, (i + shard_count) % count) for i in range(count)]
    halves = [list(range(e * shard_count, (e + 1) * shard_count)) for e in range(E_WIN)]

    def gathered(block):
        return lax.all_gather(block, "expert", axis=0, tiled=True, axis_index_groups=halves)

    def scattered(block):
        return lax.psum_scatter(
            block, "expert", scatter_dimension=0, tiled=True, axis_index_groups=halves
        )

    early_rows = gathered(early)
    got = lax.ppermute(send, "expert", partner)
    late_rows = gathered(jnp.concatenate([got, rest], axis=0))
    early_sum = scattered(experts(early_rows, w_gate, w_up, w_down))
    late_sum = scattered(experts(late_rows, w_gate, w_up, w_down))
    back = lax.ppermute(late_sum[:CAP], "expert", partner)
    return combine(mixed, weight, early_sum, late_sum, back)


def solution(mesh):
    placed = (
        P(("groups", "expert"), None),
        P(("groups", "expert"), None),
        P(("groups", "expert"), None),
        P(("groups", "expert"), None),
        P(("groups", "expert")),
        P(),
        P(("groups", "expert"), None),
        P(("groups", "expert"), None),
        P(None, "expert"),
        P(None, "expert"),
        P("expert", None),
    )
    return jax.shard_map(
        shards, mesh=mesh, in_specs=placed, out_specs=P(("groups", "expert"), None), check_vma=False
    )
```

```python
import functools

import jax
import jax.numpy as jnp
from jax import lax
from jax.experimental import pallas as pl
from jax.experimental.pallas import tpu as pltpu
from jax.sharding import PartitionSpec as P

HEAD_DIM = 128
E_WIN = 2
WIN_DEV = 3
CAP = 20
SPARE = 16
HEADS_STEP = 8
MASKED = -1e30
MIB = 1024 * 1024


def bundle_kernel(keys, segs, out, row, sems):
    rows = keys.shape[0]
    spare = out.shape[0] - rows
    body = pltpu.make_async_copy(keys, out.at[pl.ds(0, rows)], sems.at[0])
    body.start()
    row[...] = jnp.zeros_like(row)
    row[:, : segs.shape[1]] = jnp.broadcast_to(
        segs[...].astype(jnp.float32), (spare, segs.shape[1])
    ).astype(jnp.bfloat16)
    tail = pltpu.make_async_copy(row, out.at[pl.ds(rows, spare)], sems.at[1])
    tail.start()
    body.wait()
    tail.wait()


def bundle(keys, segs):
    rows, width = keys.shape
    anywhere = pl.BlockSpec(memory_space=pl.ANY)
    return pl.pallas_call(
        bundle_kernel,
        in_specs=[anywhere, pl.BlockSpec(memory_space=pltpu.VMEM)],
        out_specs=anywhere,
        out_shape=jax.ShapeDtypeStruct((rows + SPARE, width), keys.dtype),
        scratch_shapes=[
            pltpu.VMEM((SPARE, width), keys.dtype),
            pltpu.SemaphoreType.DMA((2,)),
        ],
        cost_estimate=pl.CostEstimate(
            flops=0, bytes_accessed=4 * rows * width, transcendentals=0
        ),
        name="bundle",
    )(keys, segs)


def attention_kernel(
    deltas, q, k0, v0, k1, v1, k2, v2, k3, v3, seg0, seg1, seg2, seg3, resid, gain, routes, gates,
    mixed_out, keep_out, send_out, weight_out, bias,
):
    step = pl.program_id(0)
    steps = pl.num_programs(0)
    rows = q.shape[0]
    keys = (WIN_DEV + 1) * rows

    @pl.when(step == 0)
    def _():
        seg_own = seg0[...].astype(jnp.float32)
        seg_row = jnp.concatenate(
            [seg_own] + [seg[0:1, :rows].astype(jnp.float32) for seg in (seg1, seg2, seg3)],
            axis=1,
        )
        eye = lax.broadcasted_iota(jnp.int32, (rows, rows), 0) == lax.broadcasted_iota(
            jnp.int32, (rows, rows), 1
        )
        seg_col = jnp.sum(jnp.where(eye, seg_own, 0.0), axis=1, keepdims=True)
        lane = lax.broadcasted_iota(jnp.int32, (rows, keys), 1)
        sub = lax.broadcasted_iota(jnp.int32, (rows, keys), 0)
        block = lane // rows
        back = jnp.where(
            block == 0,
            deltas[0],
            jnp.where(block == 1, deltas[1], jnp.where(block == 2, deltas[2], deltas[3])),
        )
        distance = sub - (lane - block * rows) + back * rows
        allowed = (distance >= 0) & (distance <= WIN_DEV * rows) & (seg_col == seg_row)
        bias[...] = jnp.where(allowed, 0.0, MASKED)

    scale = 1.0 / HEAD_DIM**0.5
    heads = [slice(head * HEAD_DIM, (head + 1) * HEAD_DIM) for head in range(HEADS_STEP)]
    scores = jnp.stack(
        [
            lax.dot_general(
                q[:, cols],
                jnp.concatenate([k0[:, cols], k1[:, cols], k2[:, cols], k3[:, cols]], axis=0),
                (((1,), (1,)), ((), ())),
                preferred_element_type=jnp.float32,
            )
            for cols in heads
        ]
    )
    scores = scores * scale + bias[...][None]
    expo = jnp.exp(scores - jnp.max(scores, axis=2, keepdims=True))
    denom = jnp.sum(expo, axis=2, keepdims=True)
    probs = expo.astype(jnp.bfloat16)
    outs = [
        jnp.dot(
            probs[head],
            jnp.concatenate([v0[:, cols], v1[:, cols], v2[:, cols], v3[:, cols]], axis=0),
            preferred_element_type=jnp.float32,
        )
        / denom[head]
        for head, cols in enumerate(heads)
    ]
    width = HEADS_STEP * HEAD_DIM
    at = pl.ds(pl.multiple_of(step * width, width), width)
    mixed_out[:, at] = resid[...].astype(jnp.float32) + jnp.concatenate(outs, axis=1)

    @pl.when(step == steps - 1)
    def _():
        mixed = mixed_out[...]
        normed = (
            mixed * lax.rsqrt(jnp.mean(mixed * mixed, axis=1, keepdims=True) + 1e-05) * gain[...]
        ).astype(jnp.bfloat16)
        across = lax.broadcasted_iota(jnp.int32, (rows, rows), 1)
        down = lax.broadcasted_iota(jnp.int32, (rows, rows), 0)
        upper = jnp.where(down < across, 1.0, 0.0).astype(jnp.bfloat16)
        eye = jnp.where(down == across, 1.0, 0.0).astype(jnp.bfloat16)
        slot = lax.broadcasted_iota(jnp.int32, (32, rows), 0)
        for place, out in ((0, keep_out), (1, send_out)):
            expert = deltas[4] if place == 0 else 1 - deltas[4]
            hit = routes[...] == expert
            member = jnp.max(jnp.where(hit, 1.0, 0.0), axis=0, keepdims=True)
            weight = jnp.sum(
                jnp.where(hit, gates[...].astype(jnp.float32), 0.0), axis=0, keepdims=True
            )
            rank = jnp.dot(
                jnp.broadcast_to(member, (8, rows)).astype(jnp.bfloat16),
                upper,
                preferred_element_type=jnp.float32,
            )[0:1].astype(jnp.int32)
            pick = (slot == rank) & (member > 0.5)
            out[...] = jnp.dot(
                jnp.where(pick, 1.0, 0.0).astype(jnp.bfloat16),
                normed,
                preferred_element_type=jnp.float32,
            )[:CAP].astype(jnp.bfloat16)
            weight_out[place] = lax.dot_general(
                eye,
                jnp.where(pick, weight, 0.0).astype(jnp.bfloat16),
                (((1,), (1,)), ((), ())),
                preferred_element_type=jnp.float32,
            ).astype(jnp.bfloat16)


def attention(deltas, q, pairs, seg_own, resid, gain, routes, gates):
    rows, width = q.shape
    cols = HEADS_STEP * HEAD_DIM
    top = routes.shape[0]
    piece = pl.BlockSpec((rows, cols), lambda j, *_: (0, j))
    tail = pl.BlockSpec((SPARE, HEAD_DIM), lambda j, *_: (rows // SPARE, 0))

    def whole(shape):
        return pl.BlockSpec(shape, lambda j, *_: (0,) * len(shape))

    bundles = pairs[2::2]
    return pl.pallas_call(
        attention_kernel,
        grid_spec=pltpu.PrefetchScalarGridSpec(
            num_scalar_prefetch=1,
            grid=(width // cols,),
            in_specs=[piece] * (1 + len(pairs))
            + [whole((1, rows))]
            + [tail] * len(bundles)
            + [
                piece,
                whole((1, width)),
                whole((top, rows)),
                whole((top, rows)),
            ],
            out_specs=[
                whole((rows, width)),
                whole((CAP, width)),
                whole((CAP, width)),
                whole((E_WIN, rows, 32)),
            ],
            scratch_shapes=[pltpu.VMEM((rows, (WIN_DEV + 1) * rows), jnp.float32)],
        ),
        out_shape=[
            jax.ShapeDtypeStruct((rows, width), jnp.float32),
            jax.ShapeDtypeStruct((CAP, width), jnp.bfloat16),
            jax.ShapeDtypeStruct((CAP, width), jnp.bfloat16),
            jax.ShapeDtypeStruct((E_WIN, rows, 32), jnp.bfloat16),
        ],
        compiler_params=pltpu.CompilerParams(vmem_limit_bytes=20 * MIB),
        cost_estimate=pl.CostEstimate(
            flops=4 * rows * 4 * rows * width, bytes_accessed=8 * rows * width * 4,
            transcendentals=rows * 4 * rows * (width // HEAD_DIM),
        ),
        name="attention",
    )(deltas, q, *pairs, seg_own, *bundles, resid, gain, routes, gates)


def fetch_kernel(parts, source, held, sems):
    depth = source.shape[0] // parts
    copies = []
    for part in range(parts):
        at = pl.ds(part * depth, depth)
        copies.append(pltpu.make_async_copy(source.at[at], held.at[at], sems.at[part]))
    for copy in copies:
        copy.start()
    for copy in copies:
        copy.wait()


def fetch(weights):
    parts = 4
    return pl.pallas_call(
        functools.partial(fetch_kernel, parts),
        in_specs=[pl.BlockSpec(memory_space=pl.ANY)],
        out_specs=pl.BlockSpec(memory_space=pltpu.VMEM),
        out_shape=pltpu.VMEM(weights.shape, weights.dtype),
        scratch_shapes=[pltpu.SemaphoreType.DMA((parts,))],
        compiler_params=pltpu.CompilerParams(vmem_limit_bytes=2 * MIB),
        cost_estimate=pl.CostEstimate(
            flops=0, bytes_accessed=4 * weights.size, transcendentals=0
        ),
        name="fetch",
    )(weights)


def experts_kernel(x, w_gate, w_up, w_down, out, hidden):
    width, units = w_gate.shape
    tile = min(256, units)

    @pl.loop(0, units // tile)
    def _(part):
        at = pl.ds(pl.multiple_of(part * tile, tile), tile)
        gate = jnp.dot(x[...], w_gate[:, at], preferred_element_type=jnp.float32)
        up = jnp.dot(x[...], w_up[:, at], preferred_element_type=jnp.float32)
        hidden[:, at] = (jax.nn.silu(gate) * up).astype(jnp.bfloat16)

    @pl.loop(0, width // 512)
    def _(part):
        at = pl.ds(pl.multiple_of(part * 512, 512), 512)
        out[:, at] = jnp.dot(
            hidden[...], w_down[:, at], preferred_element_type=jnp.float32
        ).astype(jnp.bfloat16)


def experts(x, w_gate, w_up, w_down):
    rows, width = x.shape
    units = w_gate.shape[1]
    near = pl.BlockSpec(memory_space=pltpu.VMEM)
    held = [
        pltpu.with_memory_space_constraint(w, pltpu.VMEM) for w in (w_gate, w_up, w_down)
    ]
    return pl.pallas_call(
        experts_kernel,
        in_specs=[near] * 4,
        out_specs=near,
        out_shape=jax.ShapeDtypeStruct((rows, width), jnp.bfloat16),
        scratch_shapes=[pltpu.VMEM((rows, units), jnp.bfloat16)],
        compiler_params=pltpu.CompilerParams(vmem_limit_bytes=20 * MIB),
        cost_estimate=pl.CostEstimate(
            flops=6 * rows * width * units,
            bytes_accessed=4 * rows * width,
            transcendentals=rows * units,
        ),
        name="experts",
    )(x, *held)


def join_kernel(first, second, out):
    out[...] = jnp.concatenate(
        [first[...].astype(jnp.float32), second[...].astype(jnp.float32)], axis=0
    ).astype(out.dtype)


def join(first, second):
    width = first.shape[1]
    near = pl.BlockSpec(memory_space=pltpu.VMEM)
    return pl.pallas_call(
        join_kernel,
        in_specs=[near, near],
        out_specs=near,
        out_shape=jax.ShapeDtypeStruct((first.shape[0] + second.shape[0], width), first.dtype),
        name="join",
    )(first, second)


def pile_kernel(*refs):
    blocks, out, sems = refs[:-2], refs[-2], refs[-1]
    rows = blocks[0].shape[0]
    copies = [
        pltpu.make_async_copy(block, out.at[pl.ds(at * rows, rows)], sems.at[at])
        for at, block in enumerate(blocks)
    ]
    for copy in copies:
        copy.start()
    for copy in copies:
        copy.wait()


def pile(blocks):
    rows, width = blocks[0].shape
    anywhere = pl.BlockSpec(memory_space=pl.ANY)
    return pl.pallas_call(
        pile_kernel,
        in_specs=[anywhere] * len(blocks),
        out_specs=anywhere,
        out_shape=jax.ShapeDtypeStruct((len(blocks) * rows, width), blocks[0].dtype),
        scratch_shapes=[pltpu.SemaphoreType.DMA((len(blocks),))],
        name="pile",
    )(*blocks)


def add_kernel(first, second, *outs):
    rows = outs[0].shape[0]
    for at, out in enumerate(outs):
        part = pl.ds(at * rows, rows)
        out[...] = (
            first[part].astype(jnp.float32) + second[part].astype(jnp.float32)
        ).astype(out.dtype)


def add_split(first, second, blocks):
    rows, width = first.shape
    each = rows // blocks
    cols = 1024
    piece = pl.BlockSpec((rows, cols), lambda j: (0, j))
    small = pl.BlockSpec((each, cols), lambda j: (0, j))
    return pl.pallas_call(
        add_kernel,
        grid=(width // cols,),
        in_specs=[piece, piece],
        out_specs=[small] * blocks,
        out_shape=[jax.ShapeDtypeStruct((each, width), first.dtype)] * blocks,
        name="add_split",
    )(first, second)


def total_kernel(*refs):
    blocks, own_out, back_out = refs[:-2], refs[-2], refs[-1]
    total = blocks[0][...].astype(jnp.float32)
    for block in blocks[1:]:
        total = total + block[...].astype(jnp.float32)
    own_out[...] = total[:CAP].astype(own_out.dtype)
    back_out[...] = total[CAP:].astype(back_out.dtype)


def total_of(blocks):
    width = blocks[0].shape[1]
    cols = 2048
    return pl.pallas_call(
        total_kernel,
        grid=(width // cols,),
        in_specs=[pl.BlockSpec((2 * CAP, cols), lambda j: (0, j))] * len(blocks),
        out_specs=[pl.BlockSpec((CAP, cols), lambda j: (0, j))] * 2,
        out_shape=[jax.ShapeDtypeStruct((CAP, width), blocks[0].dtype)] * 2,
        name="total",
    )(*blocks)


def combine_kernel(mixed, weight, own, other, out):
    total = mixed[...]
    for place, part in enumerate((own, other)):
        total = total + jnp.dot(
            weight[place][:, : part.shape[0]], part[...], preferred_element_type=jnp.float32
        )
    out[...] = total.astype(jnp.bfloat16)


def combine(mixed, weight, own, other):
    rows, width = mixed.shape
    cols = 2048

    def piece(count):
        return pl.BlockSpec((count, cols), lambda j: (0, j))

    return pl.pallas_call(
        combine_kernel,
        grid=(width // cols,),
        in_specs=[
            piece(rows),
            pl.BlockSpec(weight.shape, lambda j: (0, 0, 0)),
            piece(own.shape[0]),
            piece(other.shape[0]),
        ],
        out_specs=piece(rows),
        out_shape=jax.ShapeDtypeStruct((rows, width), jnp.bfloat16),
        name="combine",
    )(mixed, weight, own, other)


def shards(
    resid, queries, keys, values, segment_ids, norm_gain, routes, route_gates, w_gate, w_up, w_down
):
    count = lax.axis_size("expert")
    own = lax.axis_index("expert")
    shard_count = count // E_WIN
    odd = own % 2

    next_chip = [(i, i + 2) for i in range(count - 2)]
    crossing = [(i, i + 1) for i in range(0, count, 2)]
    crossing += [(i, i + 3) for i in range(1, count - 3, 2)]

    def swapped(block, mask):
        return lax.ppermute(block, "expert", [(i, i ^ mask) for i in range(count)])

    seg_own = segment_ids.reshape(1, -1)
    value_two = lax.ppermute(values, "expert", next_chip)
    key_block = bundle(keys, seg_own)
    key_two = lax.ppermute(key_block, "expert", next_chip)
    value_cross = lax.ppermute(values, "expert", crossing)
    key_cross = lax.ppermute(key_block, "expert", crossing)
    value_mirror = swapped(value_two, 1)
    key_mirror = swapped(key_two, 1)
    held = [fetch(w) for w in (w_gate, w_up, w_down)]

    far = 2 * WIN_DEV + 2
    delta_list = [0 * own, 0 * own + 2, 3 - 2 * odd, 1 + 2 * odd]
    my_expert = own // shard_count
    scalars = jnp.stack(
        [jnp.where(own >= delta, delta, far) for delta in delta_list] + [my_expert]
    ).astype(jnp.int32)

    mixed, keep, send, weight = attention(
        scalars,
        queries,
        [keys, values, key_two, value_two, key_cross, value_cross, key_mirror, value_mirror],
        seg_own, resid, norm_gain.reshape(1, -1), routes.T, route_gates.T,
    )
    partner = [(i, (i + shard_count) % count) for i in range(count)]
    masks = range(2, shard_count, 2)
    pair = join(keep, lax.ppermute(send, "expert", partner))
    local = pile([pair] + [swapped(pair, mask) for mask in masks])
    remote = swapped(local, 1)
    local_part = experts(local, *held)
    remote_part = experts(remote, *held)
    blocks = add_split(local_part, swapped(remote_part, 1), 1 + len(masks))
    own_sum, back = total_of(
        [blocks[0]] + [swapped(block, mask) for block, mask in zip(blocks[1:], masks)]
    )
    return combine(mixed, weight, own_sum, lax.ppermute(back, "expert", partner))


def solution(mesh):
    placed = (
        P(("groups", "expert"), None),
        P(("groups", "expert"), None),
        P(("groups", "expert"), None),
        P(("groups", "expert"), None),
        P(("groups", "expert")),
        P(),
        P(("groups", "expert"), None),
        P(("groups", "expert"), None),
        P(None, "expert"),
        P(None, "expert"),
        P("expert", None),
    )
    return jax.shard_map(
        shards, mesh=mesh, in_specs=placed, out_specs=P(("groups", "expert"), None), check_vma=False
    )
```

```python
import functools

import jax
import jax.numpy as jnp
from jax import lax
from jax.experimental import pallas as pl
from jax.experimental.pallas import tpu as pltpu
from jax.sharding import PartitionSpec as P

HEAD_DIM = 128
E_WIN = 2
WIN_DEV = 3
CAP = 20
SPARE = 16
HEADS_STEP = 8
MASKED = -1e30
MIB = 1024 * 1024


def far(x):
    return pltpu.with_memory_space_constraint(x, pltpu.HBM)


def close(x):
    return pltpu.with_memory_space_constraint(x, pltpu.VMEM)


NEAR = pl.BlockSpec(memory_space=pltpu.VMEM)


def bundle_kernel(keys, segs, out):
    rows = keys.shape[0]
    spare = out.shape[0] - rows
    out[:rows] = keys[...]
    out[rows:] = jnp.zeros((spare, keys.shape[1]), keys.dtype)
    out[rows:, : segs.shape[1]] = jnp.broadcast_to(
        segs[...].astype(jnp.float32), (spare, segs.shape[1])
    ).astype(keys.dtype)


def bundle(keys, segs):
    rows, width = keys.shape
    return pl.pallas_call(
        bundle_kernel,
        in_specs=[NEAR, NEAR],
        out_specs=NEAR,
        out_shape=jax.ShapeDtypeStruct((rows + SPARE, width), keys.dtype),
        cost_estimate=pl.CostEstimate(
            flops=0, bytes_accessed=4 * rows * width, transcendentals=0
        ),
        name="bundle",
    )(far(keys), far(segs))


def attention_kernel(
    deltas, q, k0, v0, k1, v1, k2, v2, k3, v3, seg0, seg1, seg2, seg3, resid, gain, routes, gates,
    mixed_out, keep_out, send_out, weight_out, bias,
):
    step = pl.program_id(0)
    steps = pl.num_programs(0)
    rows = q.shape[0]
    keys = (WIN_DEV + 1) * rows

    @pl.when(step == 0)
    def _():
        seg_own = seg0[...].astype(jnp.float32)
        seg_row = jnp.concatenate(
            [seg_own] + [seg[0:1, :rows].astype(jnp.float32) for seg in (seg1, seg2, seg3)],
            axis=1,
        )
        eye = lax.broadcasted_iota(jnp.int32, (rows, rows), 0) == lax.broadcasted_iota(
            jnp.int32, (rows, rows), 1
        )
        seg_col = jnp.sum(jnp.where(eye, seg_own, 0.0), axis=1, keepdims=True)
        lane = lax.broadcasted_iota(jnp.int32, (rows, keys), 1)
        sub = lax.broadcasted_iota(jnp.int32, (rows, keys), 0)
        block = lane // rows
        back = jnp.where(
            block == 0,
            deltas[0],
            jnp.where(block == 1, deltas[1], jnp.where(block == 2, deltas[2], deltas[3])),
        )
        distance = sub - (lane - block * rows) + back * rows
        allowed = (distance >= 0) & (distance <= WIN_DEV * rows) & (seg_col == seg_row)
        bias[...] = jnp.where(allowed, 0.0, MASKED)

    scale = 1.0 / HEAD_DIM**0.5
    heads = [slice(head * HEAD_DIM, (head + 1) * HEAD_DIM) for head in range(HEADS_STEP)]
    scores = jnp.stack(
        [
            lax.dot_general(
                q[:, cols],
                jnp.concatenate([k0[:, cols], k1[:, cols], k2[:, cols], k3[:, cols]], axis=0),
                (((1,), (1,)), ((), ())),
                preferred_element_type=jnp.float32,
            )
            for cols in heads
        ]
    )
    scores = scores * scale + bias[...][None]
    expo = jnp.exp(scores - jnp.max(scores, axis=2, keepdims=True))
    denom = jnp.sum(expo, axis=2, keepdims=True)
    probs = expo.astype(jnp.bfloat16)
    outs = [
        jnp.dot(
            probs[head],
            jnp.concatenate([v0[:, cols], v1[:, cols], v2[:, cols], v3[:, cols]], axis=0),
            preferred_element_type=jnp.float32,
        )
        / denom[head]
        for head, cols in enumerate(heads)
    ]
    width = HEADS_STEP * HEAD_DIM
    at = pl.ds(pl.multiple_of(step * width, width), width)
    mixed_out[:, at] = resid[...].astype(jnp.float32) + jnp.concatenate(outs, axis=1)

    @pl.when(step == steps - 1)
    def _():
        mixed = mixed_out[...]
        normed = (
            mixed * lax.rsqrt(jnp.mean(mixed * mixed, axis=1, keepdims=True) + 1e-05) * gain[...]
        ).astype(jnp.bfloat16)
        across = lax.broadcasted_iota(jnp.int32, (rows, rows), 1)
        down = lax.broadcasted_iota(jnp.int32, (rows, rows), 0)
        upper = jnp.where(down < across, 1.0, 0.0).astype(jnp.bfloat16)
        eye = jnp.where(down == across, 1.0, 0.0).astype(jnp.bfloat16)
        slot = lax.broadcasted_iota(jnp.int32, (32, rows), 0)
        for place, out in ((0, keep_out), (1, send_out)):
            expert = deltas[4] if place == 0 else 1 - deltas[4]
            hit = routes[...] == expert
            member = jnp.max(jnp.where(hit, 1.0, 0.0), axis=0, keepdims=True)
            weight = jnp.sum(
                jnp.where(hit, gates[...].astype(jnp.float32), 0.0), axis=0, keepdims=True
            )
            rank = jnp.dot(
                jnp.broadcast_to(member, (8, rows)).astype(jnp.bfloat16),
                upper,
                preferred_element_type=jnp.float32,
            )[0:1].astype(jnp.int32)
            pick = (slot == rank) & (member > 0.5)
            out[...] = jnp.dot(
                jnp.where(pick, 1.0, 0.0).astype(jnp.bfloat16),
                normed,
                preferred_element_type=jnp.float32,
            )[:CAP].astype(jnp.bfloat16)
            weight_out[place] = lax.dot_general(
                eye,
                jnp.where(pick, weight, 0.0).astype(jnp.bfloat16),
                (((1,), (1,)), ((), ())),
                preferred_element_type=jnp.float32,
            ).astype(jnp.bfloat16)


def attention(deltas, q, pairs, seg_own, resid, gain, routes, gates):
    rows, width = q.shape
    cols = HEADS_STEP * HEAD_DIM
    top = routes.shape[0]
    piece = pl.BlockSpec((rows, cols), lambda j, *_: (0, j))
    tail = pl.BlockSpec((SPARE, HEAD_DIM), lambda j, *_: (rows // SPARE, 0))

    def whole(shape):
        return pl.BlockSpec(shape, lambda j, *_: (0,) * len(shape))

    bundles = pairs[2::2]
    return pl.pallas_call(
        attention_kernel,
        grid_spec=pltpu.PrefetchScalarGridSpec(
            num_scalar_prefetch=1,
            grid=(width // cols,),
            in_specs=[piece] * (1 + len(pairs))
            + [whole((1, rows))]
            + [tail] * len(bundles)
            + [
                piece,
                whole((1, width)),
                whole((top, rows)),
                whole((top, rows)),
            ],
            out_specs=[
                whole((rows, width)),
                whole((CAP, width)),
                whole((CAP, width)),
                whole((E_WIN, rows, 32)),
            ],
            scratch_shapes=[pltpu.VMEM((rows, (WIN_DEV + 1) * rows), jnp.float32)],
        ),
        out_shape=[
            pltpu.VMEM((rows, width), jnp.float32),
            jax.ShapeDtypeStruct((CAP, width), jnp.bfloat16),
            jax.ShapeDtypeStruct((CAP, width), jnp.bfloat16),
            jax.ShapeDtypeStruct((E_WIN, rows, 32), jnp.bfloat16),
        ],
        compiler_params=pltpu.CompilerParams(vmem_limit_bytes=14 * MIB),
        cost_estimate=pl.CostEstimate(
            flops=4 * rows * 4 * rows * width, bytes_accessed=8 * rows * width * 4,
            transcendentals=rows * 4 * rows * (width // HEAD_DIM),
        ),
        name="attention",
    )(
        deltas, far(q), far(pairs[0]), far(pairs[1]), *pairs[2:], far(seg_own), *bundles,
        far(resid), far(gain), far(routes), far(gates),
    )


def fetch_kernel(parts, source, after, held, sems):
    depth = source.shape[0] // parts
    copies = []
    for part in range(parts):
        at = pl.ds(part * depth, depth)
        copies.append(pltpu.make_async_copy(source.at[at], held.at[at], sems.at[part]))
    for copy in copies:
        copy.start()
    for copy in copies:
        copy.wait()


def fetch(weights, after):
    parts = 4
    anywhere = pl.BlockSpec(memory_space=pl.ANY)
    return pl.pallas_call(
        functools.partial(fetch_kernel, parts),
        in_specs=[anywhere, anywhere],
        out_specs=NEAR,
        out_shape=pltpu.VMEM(weights.shape, weights.dtype),
        scratch_shapes=[pltpu.SemaphoreType.DMA((parts,))],
        compiler_params=pltpu.CompilerParams(vmem_limit_bytes=2 * MIB),
        cost_estimate=pl.CostEstimate(
            flops=0, bytes_accessed=4 * weights.size, transcendentals=0
        ),
        name="fetch",
    )(far(weights), after)


def experts_kernel(x, w_gate, w_up, w_down, out, hidden):
    width, units = w_gate.shape
    tile = min(256, units)

    @pl.loop(0, units // tile)
    def _(part):
        at = pl.ds(pl.multiple_of(part * tile, tile), tile)
        gate = jnp.dot(x[...], w_gate[:, at], preferred_element_type=jnp.float32)
        up = jnp.dot(x[...], w_up[:, at], preferred_element_type=jnp.float32)
        hidden[:, at] = (jax.nn.silu(gate) * up).astype(jnp.bfloat16)

    @pl.loop(0, width // 512)
    def _(part):
        at = pl.ds(pl.multiple_of(part * 512, 512), 512)
        out[:, at] = jnp.dot(
            hidden[...], w_down[:, at], preferred_element_type=jnp.float32
        ).astype(jnp.bfloat16)


def experts(x, w_gate, w_up, w_down):
    rows, width = x.shape
    units = w_gate.shape[1]
    return pl.pallas_call(
        experts_kernel,
        in_specs=[NEAR] * 4,
        out_specs=NEAR,
        out_shape=jax.ShapeDtypeStruct((rows, width), jnp.bfloat16),
        scratch_shapes=[pltpu.VMEM((rows, units), jnp.bfloat16)],
        compiler_params=pltpu.CompilerParams(vmem_limit_bytes=20 * MIB),
        cost_estimate=pl.CostEstimate(
            flops=6 * rows * width * units,
            bytes_accessed=4 * rows * width,
            transcendentals=rows * units,
        ),
        name="experts",
    )(x, close(w_gate), close(w_up), close(w_down))


def join_kernel(first, second, out):
    out[...] = jnp.concatenate(
        [first[...].astype(jnp.float32), second[...].astype(jnp.float32)], axis=0
    ).astype(out.dtype)


def join(first, second):
    width = first.shape[1]
    return pl.pallas_call(
        join_kernel,
        in_specs=[NEAR, NEAR],
        out_specs=NEAR,
        out_shape=jax.ShapeDtypeStruct((first.shape[0] + second.shape[0], width), first.dtype),
        name="join",
    )(first, second)


def pile_kernel(*refs):
    blocks, out = refs[:-1], refs[-1]
    rows = blocks[0].shape[0]
    for at, block in enumerate(blocks):
        out[pl.ds(at * rows, rows)] = block[...]


def pile(blocks):
    rows, width = blocks[0].shape
    return pl.pallas_call(
        pile_kernel,
        in_specs=[NEAR] * len(blocks),
        out_specs=NEAR,
        out_shape=jax.ShapeDtypeStruct((len(blocks) * rows, width), blocks[0].dtype),
        compiler_params=pltpu.CompilerParams(vmem_limit_bytes=24 * MIB),
        name="pile",
    )(*blocks)


def add_kernel(first, second, *outs):
    rows = outs[0].shape[0]
    for at, out in enumerate(outs):
        part = pl.ds(at * rows, rows)
        out[...] = (
            first[part].astype(jnp.float32) + second[part].astype(jnp.float32)
        ).astype(out.dtype)


def add_split(first, second, blocks):
    rows, width = first.shape
    each = rows // blocks
    return pl.pallas_call(
        add_kernel,
        in_specs=[NEAR, NEAR],
        out_specs=[NEAR] * blocks,
        out_shape=[jax.ShapeDtypeStruct((each, width), first.dtype)] * blocks,
        compiler_params=pltpu.CompilerParams(vmem_limit_bytes=24 * MIB),
        name="add_split",
    )(first, second)


def total_kernel(*refs):
    blocks, own_out, back_out = refs[:-2], refs[-2], refs[-1]
    total = blocks[0][...].astype(jnp.float32)
    for block in blocks[1:]:
        total = total + block[...].astype(jnp.float32)
    own_out[...] = total[:CAP].astype(own_out.dtype)
    back_out[...] = total[CAP:].astype(back_out.dtype)


def total_of(blocks):
    width = blocks[0].shape[1]
    return pl.pallas_call(
        total_kernel,
        in_specs=[NEAR] * len(blocks),
        out_specs=[NEAR] * 2,
        out_shape=[jax.ShapeDtypeStruct((CAP, width), blocks[0].dtype)] * 2,
        name="total",
    )(*blocks)


def combine_kernel(mixed, weight, own, other, out):
    total = mixed[...]
    for place, part in enumerate((own, other)):
        total = total + jnp.dot(
            weight[place][:, : part.shape[0]], part[...], preferred_element_type=jnp.float32
        )
    out[...] = total.astype(jnp.bfloat16)


def combine(mixed, weight, own, other):
    return pl.pallas_call(
        combine_kernel,
        in_specs=[NEAR] * 4,
        out_specs=NEAR,
        out_shape=jax.ShapeDtypeStruct(mixed.shape, jnp.bfloat16),
        name="combine",
    )(close(mixed), weight, own, other)


def shards(
    resid, queries, keys, values, segment_ids, norm_gain, routes, route_gates, w_gate, w_up, w_down
):
    count = lax.axis_size("expert")
    own = lax.axis_index("expert")
    shard_count = count // E_WIN
    odd = own % 2

    next_chip = [(i, i + 2) for i in range(count - 2)]
    crossing = [(i, i + 1) for i in range(0, count, 2)]
    crossing += [(i, i + 3) for i in range(1, count - 3, 2)]

    def swapped(block, mask):
        return lax.ppermute(block, "expert", [(i, i ^ mask) for i in range(count)])

    seg_own = segment_ids.reshape(1, -1)
    value_two = lax.ppermute(values, "expert", next_chip)
    key_block = bundle(keys, seg_own)
    key_two = lax.ppermute(key_block, "expert", next_chip)
    value_cross = lax.ppermute(values, "expert", crossing)
    key_cross = lax.ppermute(key_block, "expert", crossing)
    value_mirror = swapped(value_two, 1)
    key_mirror = swapped(key_two, 1)
    held = [fetch(w, value_two) for w in (w_gate, w_up, w_down)]
    key_cross, *held = lax.optimization_barrier((key_cross, *held))

    beyond = 2 * WIN_DEV + 2
    delta_list = [0 * own, 0 * own + 2, 3 - 2 * odd, 1 + 2 * odd]
    my_expert = own // shard_count
    scalars = jnp.stack(
        [jnp.where(own >= delta, delta, beyond) for delta in delta_list] + [my_expert]
    ).astype(jnp.int32)

    mixed, keep, send, weight = attention(
        scalars,
        queries,
        [keys, values, key_two, value_two, key_cross, value_cross, key_mirror, value_mirror],
        seg_own, resid, norm_gain.reshape(1, -1), routes.T, route_gates.T,
    )
    partner = [(i, (i + shard_count) % count) for i in range(count)]
    masks = range(2, shard_count, 2)
    pair = join(keep, lax.ppermute(send, "expert", partner))
    local = pile([pair] + [swapped(pair, mask) for mask in masks])
    remote = swapped(local, 1)
    local_part = experts(local, *held)
    remote_part = experts(remote, *held)
    blocks = add_split(local_part, swapped(remote_part, 1), 1 + len(masks))
    own_sum, back = total_of(
        [blocks[0]] + [swapped(block, mask) for block, mask in zip(blocks[1:], masks)]
    )
    return combine(mixed, weight, own_sum, lax.ppermute(back, "expert", partner))


def solution(mesh):
    placed = (
        P(("groups", "expert"), None),
        P(("groups", "expert"), None),
        P(("groups", "expert"), None),
        P(("groups", "expert"), None),
        P(("groups", "expert")),
        P(),
        P(("groups", "expert"), None),
        P(("groups", "expert"), None),
        P(None, "expert"),
        P(None, "expert"),
        P("expert", None),
    )
    return jax.shard_map(
        shards, mesh=mesh, in_specs=placed, out_specs=P(("groups", "expert"), None), check_vma=False
    )
```

```python
import functools

import jax
import jax.numpy as jnp
from jax import lax
from jax.experimental import pallas as pl
from jax.experimental.pallas import tpu as pltpu
from jax.sharding import PartitionSpec as P

HEAD_DIM = 128
E_WIN = 2
WIN_DEV = 3
CAP = 20
SPARE = 16
HEADS_STEP = 8
MASKED = -1e30
MIB = 1024 * 1024


def far(x):
    return pltpu.with_memory_space_constraint(x, pltpu.HBM)


def close(x):
    return pltpu.with_memory_space_constraint(x, pltpu.VMEM)


NEAR = pl.BlockSpec(memory_space=pltpu.VMEM)


def bundle_kernel(keys, segs, out):
    rows = keys.shape[0]
    spare = out.shape[0] - rows
    out[:rows] = keys[...]
    out[rows:] = jnp.zeros((spare, keys.shape[1]), keys.dtype)
    out[rows:, : segs.shape[1]] = jnp.broadcast_to(
        segs[...].astype(jnp.float32), (spare, segs.shape[1])
    ).astype(keys.dtype)


def bundle(keys, segs):
    rows, width = keys.shape
    return pl.pallas_call(
        bundle_kernel,
        in_specs=[NEAR, NEAR],
        out_specs=NEAR,
        out_shape=jax.ShapeDtypeStruct((rows + SPARE, width), keys.dtype),
        cost_estimate=pl.CostEstimate(
            flops=0, bytes_accessed=4 * rows * width, transcendentals=0
        ),
        compiler_params=pltpu.CompilerParams(vmem_limit_bytes=6 * MIB),
        name="bundle",
    )(far(keys), far(segs))


def attention_kernel(
    deltas, q, k0, v0, k1, v1, k2, v2, k3, v3, seg0, seg1, seg2, seg3, resid, gain, routes, gates,
    mixed_out, keep_out, send_out, weight_out, bias,
):
    step = pl.program_id(0)
    steps = pl.num_programs(0)
    rows = q.shape[0]
    keys = (WIN_DEV + 1) * rows

    @pl.when(step == 0)
    def _():
        seg_own = seg0[...].astype(jnp.float32)
        seg_row = jnp.concatenate(
            [seg_own] + [seg[0:1, :rows].astype(jnp.float32) for seg in (seg1, seg2, seg3)],
            axis=1,
        )
        eye = lax.broadcasted_iota(jnp.int32, (rows, rows), 0) == lax.broadcasted_iota(
            jnp.int32, (rows, rows), 1
        )
        seg_col = jnp.sum(jnp.where(eye, seg_own, 0.0), axis=1, keepdims=True)
        lane = lax.broadcasted_iota(jnp.int32, (rows, keys), 1)
        sub = lax.broadcasted_iota(jnp.int32, (rows, keys), 0)
        block = lane // rows
        back = jnp.where(
            block == 0,
            deltas[0],
            jnp.where(block == 1, deltas[1], jnp.where(block == 2, deltas[2], deltas[3])),
        )
        distance = sub - (lane - block * rows) + back * rows
        allowed = (distance >= 0) & (distance <= WIN_DEV * rows) & (seg_col == seg_row)
        bias[...] = jnp.where(allowed, 0.0, MASKED)

    scale = 1.0 / HEAD_DIM**0.5
    heads = [slice(head * HEAD_DIM, (head + 1) * HEAD_DIM) for head in range(HEADS_STEP)]
    scores = jnp.stack(
        [
            lax.dot_general(
                q[:, cols],
                jnp.concatenate([k0[:, cols], k1[:, cols], k2[:, cols], k3[:, cols]], axis=0),
                (((1,), (1,)), ((), ())),
                preferred_element_type=jnp.float32,
            )
            for cols in heads
        ]
    )
    scores = scores * scale + bias[...][None]
    expo = jnp.exp(scores - jnp.max(scores, axis=2, keepdims=True))
    denom = jnp.sum(expo, axis=2, keepdims=True)
    probs = expo.astype(jnp.bfloat16)
    outs = [
        jnp.dot(
            probs[head],
            jnp.concatenate([v0[:, cols], v1[:, cols], v2[:, cols], v3[:, cols]], axis=0),
            preferred_element_type=jnp.float32,
        )
        / denom[head]
        for head, cols in enumerate(heads)
    ]
    width = HEADS_STEP * HEAD_DIM
    at = pl.ds(pl.multiple_of(step * width, width), width)
    mixed_out[:, at] = resid[...].astype(jnp.float32) + jnp.concatenate(outs, axis=1)

    @pl.when(step == steps - 1)
    def _():
        mixed = mixed_out[...]
        normed = (
            mixed * lax.rsqrt(jnp.mean(mixed * mixed, axis=1, keepdims=True) + 1e-05) * gain[...]
        ).astype(jnp.bfloat16)
        across = lax.broadcasted_iota(jnp.int32, (rows, rows), 1)
        down = lax.broadcasted_iota(jnp.int32, (rows, rows), 0)
        upper = jnp.where(down < across, 1.0, 0.0).astype(jnp.bfloat16)
        eye = jnp.where(down == across, 1.0, 0.0).astype(jnp.bfloat16)
        slot = lax.broadcasted_iota(jnp.int32, (32, rows), 0)
        for place, out in ((0, keep_out), (1, send_out)):
            expert = deltas[4] if place == 0 else 1 - deltas[4]
            hit = routes[...] == expert
            member = jnp.max(jnp.where(hit, 1.0, 0.0), axis=0, keepdims=True)
            weight = jnp.sum(
                jnp.where(hit, gates[...].astype(jnp.float32), 0.0), axis=0, keepdims=True
            )
            rank = jnp.dot(
                jnp.broadcast_to(member, (8, rows)).astype(jnp.bfloat16),
                upper,
                preferred_element_type=jnp.float32,
            )[0:1].astype(jnp.int32)
            pick = (slot == rank) & (member > 0.5)
            out[...] = jnp.dot(
                jnp.where(pick, 1.0, 0.0).astype(jnp.bfloat16),
                normed,
                preferred_element_type=jnp.float32,
            )[:CAP].astype(jnp.bfloat16)
            weight_out[place] = lax.dot_general(
                eye,
                jnp.where(pick, weight, 0.0).astype(jnp.bfloat16),
                (((1,), (1,)), ((), ())),
                preferred_element_type=jnp.float32,
            ).astype(jnp.bfloat16)


def attention(deltas, q, pairs, seg_own, resid, gain, routes, gates):
    rows, width = q.shape
    cols = HEADS_STEP * HEAD_DIM
    top = routes.shape[0]
    piece = pl.BlockSpec((rows, cols), lambda j, *_: (0, j))
    tail = pl.BlockSpec((SPARE, HEAD_DIM), lambda j, *_: (rows // SPARE, 0))

    def whole(shape):
        return pl.BlockSpec(shape, lambda j, *_: (0,) * len(shape))

    bundles = pairs[2::2]
    return pl.pallas_call(
        attention_kernel,
        grid_spec=pltpu.PrefetchScalarGridSpec(
            num_scalar_prefetch=1,
            grid=(width // cols,),
            in_specs=[piece] * (1 + len(pairs))
            + [whole((1, rows))]
            + [tail] * len(bundles)
            + [
                piece,
                whole((1, width)),
                whole((top, rows)),
                whole((top, rows)),
            ],
            out_specs=[
                whole((rows, width)),
                whole((CAP, width)),
                whole((CAP, width)),
                whole((E_WIN, rows, 32)),
            ],
            scratch_shapes=[pltpu.VMEM((rows, (WIN_DEV + 1) * rows), jnp.float32)],
        ),
        out_shape=[
            pltpu.VMEM((rows, width), jnp.float32),
            jax.ShapeDtypeStruct((CAP, width), jnp.bfloat16),
            jax.ShapeDtypeStruct((CAP, width), jnp.bfloat16),
            jax.ShapeDtypeStruct((E_WIN, rows, 32), jnp.bfloat16),
        ],
        compiler_params=pltpu.CompilerParams(vmem_limit_bytes=14 * MIB),
        cost_estimate=pl.CostEstimate(
            flops=4 * rows * 4 * rows * width, bytes_accessed=8 * rows * width * 4,
            transcendentals=rows * 4 * rows * (width // HEAD_DIM),
        ),
        name="attention",
    )(
        deltas, far(q), far(pairs[0]), far(pairs[1]), *pairs[2:], far(seg_own), *bundles,
        far(resid), far(gain), far(routes), far(gates),
    )


def fetch_kernel(parts, source, held, sems):
    depth = source.shape[0] // parts
    copies = []
    for part in range(parts):
        at = pl.ds(part * depth, depth)
        copies.append(pltpu.make_async_copy(source.at[at], held.at[at], sems.at[part]))
    for copy in copies:
        copy.start()
    for copy in copies:
        copy.wait()


def fetch(weights):
    parts = 4
    anywhere = pl.BlockSpec(memory_space=pl.ANY)
    return pl.pallas_call(
        functools.partial(fetch_kernel, parts),
        in_specs=[anywhere],
        out_specs=NEAR,
        out_shape=pltpu.VMEM(weights.shape, weights.dtype),
        scratch_shapes=[pltpu.SemaphoreType.DMA((parts,))],
        compiler_params=pltpu.CompilerParams(vmem_limit_bytes=2 * MIB),
        cost_estimate=pl.CostEstimate(
            flops=0, bytes_accessed=4 * weights.size, transcendentals=0
        ),
        name="fetch",
    )(far(weights))


def experts_kernel(x, w_gate, w_up, w_down, out, hidden):
    width, units = w_gate.shape
    tile = min(256, units)

    @pl.loop(0, units // tile)
    def _(part):
        at = pl.ds(pl.multiple_of(part * tile, tile), tile)
        gate = jnp.dot(x[...], w_gate[:, at], preferred_element_type=jnp.float32)
        up = jnp.dot(x[...], w_up[:, at], preferred_element_type=jnp.float32)
        hidden[:, at] = (jax.nn.silu(gate) * up).astype(jnp.bfloat16)

    @pl.loop(0, width // 512)
    def _(part):
        at = pl.ds(pl.multiple_of(part * 512, 512), 512)
        out[:, at] = jnp.dot(
            hidden[...], w_down[:, at], preferred_element_type=jnp.float32
        ).astype(jnp.bfloat16)


def experts(x, w_gate, w_up, w_down):
    rows, width = x.shape
    units = w_gate.shape[1]
    return pl.pallas_call(
        experts_kernel,
        in_specs=[NEAR] * 4,
        out_specs=NEAR,
        out_shape=jax.ShapeDtypeStruct((rows, width), jnp.bfloat16),
        scratch_shapes=[pltpu.VMEM((rows, units), jnp.bfloat16)],
        compiler_params=pltpu.CompilerParams(vmem_limit_bytes=20 * MIB),
        cost_estimate=pl.CostEstimate(
            flops=6 * rows * width * units,
            bytes_accessed=4 * rows * width,
            transcendentals=rows * units,
        ),
        name="experts",
    )(x, close(w_gate), close(w_up), close(w_down))


def join_kernel(first, second, out):
    out[...] = jnp.concatenate(
        [first[...].astype(jnp.float32), second[...].astype(jnp.float32)], axis=0
    ).astype(out.dtype)


def join(first, second):
    width = first.shape[1]
    return pl.pallas_call(
        join_kernel,
        in_specs=[NEAR, NEAR],
        out_specs=NEAR,
        out_shape=jax.ShapeDtypeStruct((first.shape[0] + second.shape[0], width), first.dtype),
        compiler_params=pltpu.CompilerParams(vmem_limit_bytes=8 * MIB),
        name="join",
    )(first, second)


def pile_kernel(*refs):
    blocks, out = refs[:-1], refs[-1]
    rows = blocks[0].shape[0]
    for at, block in enumerate(blocks):
        out[pl.ds(at * rows, rows)] = block[...]


def pile(blocks):
    rows, width = blocks[0].shape
    return pl.pallas_call(
        pile_kernel,
        in_specs=[NEAR] * len(blocks),
        out_specs=NEAR,
        out_shape=jax.ShapeDtypeStruct((len(blocks) * rows, width), blocks[0].dtype),
        compiler_params=pltpu.CompilerParams(vmem_limit_bytes=(4 + len(blocks)) * MIB),
        name="pile",
    )(*blocks)


def add_kernel(first, second, *outs):
    rows = outs[0].shape[0]
    for at, out in enumerate(outs):
        part = pl.ds(at * rows, rows)
        out[...] = (
            first[part].astype(jnp.float32) + second[part].astype(jnp.float32)
        ).astype(out.dtype)


def add_split(first, second, blocks):
    rows, width = first.shape
    each = rows // blocks
    return pl.pallas_call(
        add_kernel,
        in_specs=[NEAR, NEAR],
        out_specs=[NEAR] * blocks,
        out_shape=[jax.ShapeDtypeStruct((each, width), first.dtype)] * blocks,
        compiler_params=pltpu.CompilerParams(vmem_limit_bytes=(6 + blocks) * MIB),
        name="add_split",
    )(first, second)


def total_kernel(*refs):
    blocks, own_out, back_out = refs[:-2], refs[-2], refs[-1]
    total = blocks[0][...].astype(jnp.float32)
    for block in blocks[1:]:
        total = total + block[...].astype(jnp.float32)
    own_out[...] = total[:CAP].astype(own_out.dtype)
    back_out[...] = total[CAP:].astype(back_out.dtype)


def total_of(blocks):
    width = blocks[0].shape[1]
    return pl.pallas_call(
        total_kernel,
        in_specs=[NEAR] * len(blocks),
        out_specs=[NEAR] * 2,
        out_shape=[jax.ShapeDtypeStruct((CAP, width), blocks[0].dtype)] * 2,
        compiler_params=pltpu.CompilerParams(vmem_limit_bytes=(4 + len(blocks)) * MIB),
        name="total",
    )(*blocks)


def combine_kernel(mixed, weight, own, other, out):
    total = mixed[...]
    for place, part in enumerate((own, other)):
        total = total + jnp.dot(
            weight[place][:, : part.shape[0]], part[...], preferred_element_type=jnp.float32
        )
    out[...] = total.astype(jnp.bfloat16)


def combine(mixed, weight, own, other):
    return pl.pallas_call(
        combine_kernel,
        in_specs=[NEAR] * 4,
        out_specs=NEAR,
        out_shape=jax.ShapeDtypeStruct(mixed.shape, jnp.bfloat16),
        compiler_params=pltpu.CompilerParams(vmem_limit_bytes=8 * MIB),
        name="combine",
    )(close(mixed), weight, own, other)


def shards(
    resid, queries, keys, values, segment_ids, norm_gain, routes, route_gates, w_gate, w_up, w_down
):
    count = lax.axis_size("expert")
    own = lax.axis_index("expert")
    shard_count = count // E_WIN
    odd = own % 2

    next_chip = [(i, i + 2) for i in range(count - 2)]
    crossing = [(i, i + 1) for i in range(0, count, 2)]
    crossing += [(i, i + 3) for i in range(1, count - 3, 2)]

    def swapped(block, mask):
        return lax.ppermute(block, "expert", [(i, i ^ mask) for i in range(count)])

    seg_own = segment_ids.reshape(1, -1)
    value_two = lax.ppermute(values, "expert", next_chip)
    key_block = bundle(keys, seg_own)
    key_two = lax.ppermute(key_block, "expert", next_chip)
    value_cross = lax.ppermute(values, "expert", crossing)
    key_cross = lax.ppermute(key_block, "expert", crossing)
    held = [fetch(w) for w in (w_gate, w_up, w_down)]
    key_two, held[0], held[1] = lax.optimization_barrier((key_two, held[0], held[1]))
    key_mirror = swapped(key_two, 1)
    value_two, held[2] = lax.optimization_barrier((value_two, held[2]))
    value_mirror = swapped(value_two, 1)

    beyond = 2 * WIN_DEV + 2
    delta_list = [0 * own, 0 * own + 2, 3 - 2 * odd, 1 + 2 * odd]
    my_expert = own // shard_count
    scalars = jnp.stack(
        [jnp.where(own >= delta, delta, beyond) for delta in delta_list] + [my_expert]
    ).astype(jnp.int32)

    mixed, keep, send, weight = attention(
        scalars,
        queries,
        [keys, values, key_two, value_two, key_cross, value_cross, key_mirror, value_mirror],
        seg_own, resid, norm_gain.reshape(1, -1), routes.T, route_gates.T,
    )
    partner = [(i, (i + shard_count) % count) for i in range(count)]
    masks = range(2, shard_count, 2)
    pair = join(keep, lax.ppermute(send, "expert", partner))
    local = pile([pair] + [swapped(pair, mask) for mask in masks])
    remote = swapped(local, 1)
    local_part = experts(local, *held)
    remote_part = experts(remote, *held)
    blocks = add_split(local_part, swapped(remote_part, 1), 1 + len(masks))
    own_sum, back = total_of(
        [blocks[0]] + [swapped(block, mask) for block, mask in zip(blocks[1:], masks)]
    )
    return combine(mixed, weight, own_sum, lax.ppermute(back, "expert", partner))


def solution(mesh):
    placed = (
        P(("groups", "expert"), None),
        P(("groups", "expert"), None),
        P(("groups", "expert"), None),
        P(("groups", "expert"), None),
        P(("groups", "expert")),
        P(),
        P(("groups", "expert"), None),
        P(("groups", "expert"), None),
        P(None, "expert"),
        P(None, "expert"),
        P("expert", None),
    )
    return jax.shard_map(
        shards, mesh=mesh, in_specs=placed, out_specs=P(("groups", "expert"), None), check_vma=False
    )
```

```python
import functools

import jax
import jax.numpy as jnp
from jax import lax
from jax.experimental import pallas as pl
from jax.experimental.pallas import tpu as pltpu
from jax.sharding import PartitionSpec as P

HEAD_DIM = 128
E_WIN = 2
WIN_DEV = 3
CAP = 20
EARLY = 16
SPARE = 16
HEADS_STEP = 8
MASKED = -1e30
MIB = 1024 * 1024


def far(x):
    return pltpu.with_memory_space_constraint(x, pltpu.HBM)


def close(x):
    return pltpu.with_memory_space_constraint(x, pltpu.VMEM)


NEAR = pl.BlockSpec(memory_space=pltpu.VMEM)


def bundle_kernel(keys, segs, out):
    rows = keys.shape[0]
    spare = out.shape[0] - rows
    out[:rows] = keys[...]
    out[rows:] = jnp.zeros((spare, keys.shape[1]), keys.dtype)
    out[rows:, : segs.shape[1]] = jnp.broadcast_to(
        segs[...].astype(jnp.float32), (spare, segs.shape[1])
    ).astype(keys.dtype)


def bundle(keys, segs):
    rows, width = keys.shape
    return pl.pallas_call(
        bundle_kernel,
        in_specs=[NEAR, NEAR],
        out_specs=NEAR,
        out_shape=jax.ShapeDtypeStruct((rows + SPARE, width), keys.dtype),
        cost_estimate=pl.CostEstimate(
            flops=0, bytes_accessed=4 * rows * width, transcendentals=0
        ),
        compiler_params=pltpu.CompilerParams(vmem_limit_bytes=6 * MIB),
        name="bundle",
    )(far(keys), far(segs))


def attention_kernel(
    deltas, q, k0, v0, k1, v1, k2, v2, k3, v3, seg0, seg1, seg2, seg3, resid, gain, routes, gates,
    mixed_out, early_out, rest_out, send_out, weight_out, bias,
):
    step = pl.program_id(0)
    steps = pl.num_programs(0)
    rows = q.shape[0]
    keys = (WIN_DEV + 1) * rows

    @pl.when(step == 0)
    def _():
        seg_own = seg0[...].astype(jnp.float32)
        seg_row = jnp.concatenate(
            [seg_own] + [seg[0:1, :rows].astype(jnp.float32) for seg in (seg1, seg2, seg3)],
            axis=1,
        )
        eye = lax.broadcasted_iota(jnp.int32, (rows, rows), 0) == lax.broadcasted_iota(
            jnp.int32, (rows, rows), 1
        )
        seg_col = jnp.sum(jnp.where(eye, seg_own, 0.0), axis=1, keepdims=True)
        lane = lax.broadcasted_iota(jnp.int32, (rows, keys), 1)
        sub = lax.broadcasted_iota(jnp.int32, (rows, keys), 0)
        block = lane // rows
        back = jnp.where(
            block == 0,
            deltas[0],
            jnp.where(block == 1, deltas[1], jnp.where(block == 2, deltas[2], deltas[3])),
        )
        distance = sub - (lane - block * rows) + back * rows
        allowed = (distance >= 0) & (distance <= WIN_DEV * rows) & (seg_col == seg_row)
        bias[...] = jnp.where(allowed, 0.0, MASKED)

    scale = 1.0 / HEAD_DIM**0.5
    heads = [slice(head * HEAD_DIM, (head + 1) * HEAD_DIM) for head in range(HEADS_STEP)]
    scores = jnp.stack(
        [
            lax.dot_general(
                q[:, cols],
                jnp.concatenate([k0[:, cols], k1[:, cols], k2[:, cols], k3[:, cols]], axis=0),
                (((1,), (1,)), ((), ())),
                preferred_element_type=jnp.float32,
            )
            for cols in heads
        ]
    )
    scores = scores * scale + bias[...][None]
    expo = jnp.exp(scores - jnp.max(scores, axis=2, keepdims=True))
    denom = jnp.sum(expo, axis=2, keepdims=True)
    probs = expo.astype(jnp.bfloat16)
    outs = [
        jnp.dot(
            probs[head],
            jnp.concatenate([v0[:, cols], v1[:, cols], v2[:, cols], v3[:, cols]], axis=0),
            preferred_element_type=jnp.float32,
        )
        / denom[head]
        for head, cols in enumerate(heads)
    ]
    width = HEADS_STEP * HEAD_DIM
    at = pl.ds(pl.multiple_of(step * width, width), width)
    mixed_out[:, at] = resid[...].astype(jnp.float32) + jnp.concatenate(outs, axis=1)

    @pl.when(step == steps - 1)
    def _():
        mixed = mixed_out[...]
        normed = (
            mixed * lax.rsqrt(jnp.mean(mixed * mixed, axis=1, keepdims=True) + 1e-05) * gain[...]
        ).astype(jnp.bfloat16)
        across = lax.broadcasted_iota(jnp.int32, (rows, rows), 1)
        down = lax.broadcasted_iota(jnp.int32, (rows, rows), 0)
        upper = jnp.where(down < across, 1.0, 0.0).astype(jnp.bfloat16)
        eye = jnp.where(down == across, 1.0, 0.0).astype(jnp.bfloat16)
        slot = lax.broadcasted_iota(jnp.int32, (32, rows), 0)

        def picks(expert):
            hit = routes[...] == expert
            member = jnp.max(jnp.where(hit, 1.0, 0.0), axis=0, keepdims=True)
            weight = jnp.sum(
                jnp.where(hit, gates[...].astype(jnp.float32), 0.0), axis=0, keepdims=True
            )
            rank = jnp.dot(
                jnp.broadcast_to(member, (8, rows)).astype(jnp.bfloat16),
                upper,
                preferred_element_type=jnp.float32,
            )[0:1].astype(jnp.int32)
            return member > 0.5, weight, rank

        def spread(pick, weight):
            return lax.dot_general(
                eye,
                jnp.where(pick, weight, 0.0).astype(jnp.bfloat16),
                (((1,), (1,)), ((), ())),
                preferred_element_type=jnp.float32,
            ).astype(jnp.bfloat16)

        def packed(pick):
            return jnp.dot(
                jnp.where(pick, 1.0, 0.0).astype(jnp.bfloat16),
                normed,
                preferred_element_type=jnp.float32,
            ).astype(jnp.bfloat16)

        member, weight, rank = picks(deltas[4])
        pick = (slot == rank) & member
        mine = packed(pick)
        early_out[...] = mine[:EARLY]
        rest_out[...] = mine[EARLY:CAP]
        weight_out[0] = spread(pick & (slot < EARLY), weight)
        weight_out[1] = spread((slot - CAP + EARLY == rank) & (slot >= CAP) & member, weight)
        member, weight, rank = picks(1 - deltas[4])
        pick = (slot == rank) & member
        send_out[...] = packed(pick)[:CAP]
        weight_out[2] = spread(pick, weight)


def attention(deltas, q, pairs, seg_own, resid, gain, routes, gates):
    rows, width = q.shape
    cols = HEADS_STEP * HEAD_DIM
    top = routes.shape[0]
    piece = pl.BlockSpec((rows, cols), lambda j, *_: (0, j))
    tail = pl.BlockSpec((SPARE, HEAD_DIM), lambda j, *_: (rows // SPARE, 0))

    def whole(shape):
        return pl.BlockSpec(shape, lambda j, *_: (0,) * len(shape))

    bundles = pairs[2::2]
    return pl.pallas_call(
        attention_kernel,
        grid_spec=pltpu.PrefetchScalarGridSpec(
            num_scalar_prefetch=1,
            grid=(width // cols,),
            in_specs=[piece] * (1 + len(pairs))
            + [whole((1, rows))]
            + [tail] * len(bundles)
            + [
                piece,
                whole((1, width)),
                whole((top, rows)),
                whole((top, rows)),
            ],
            out_specs=[
                whole((rows, width)),
                whole((EARLY, width)),
                whole((CAP - EARLY, width)),
                whole((CAP, width)),
                whole((3, rows, 32)),
            ],
            scratch_shapes=[pltpu.VMEM((rows, (WIN_DEV + 1) * rows), jnp.float32)],
        ),
        out_shape=[
            pltpu.VMEM((rows, width), jnp.float32),
            jax.ShapeDtypeStruct((EARLY, width), jnp.bfloat16),
            jax.ShapeDtypeStruct((CAP - EARLY, width), jnp.bfloat16),
            jax.ShapeDtypeStruct((CAP, width), jnp.bfloat16),
            jax.ShapeDtypeStruct((3, rows, 32), jnp.bfloat16),
        ],
        compiler_params=pltpu.CompilerParams(vmem_limit_bytes=14 * MIB),
        cost_estimate=pl.CostEstimate(
            flops=4 * rows * 4 * rows * width, bytes_accessed=8 * rows * width * 4,
            transcendentals=rows * 4 * rows * (width // HEAD_DIM),
        ),
        name="attention",
    )(
        deltas, far(q), far(pairs[0]), far(pairs[1]), *pairs[2:], far(seg_own), *bundles,
        far(resid), far(gain), far(routes), far(gates),
    )


def fetch_kernel(parts, source, after, held, sems):
    depth = source.shape[0] // parts
    copies = []
    for part in range(parts):
        at = pl.ds(part * depth, depth)
        copies.append(pltpu.make_async_copy(source.at[at], held.at[at], sems.at[part]))
    for copy in copies:
        copy.start()
    for copy in copies:
        copy.wait()


def fetch(weights, after):
    parts = 4
    anywhere = pl.BlockSpec(memory_space=pl.ANY)
    return pl.pallas_call(
        functools.partial(fetch_kernel, parts),
        in_specs=[anywhere, anywhere],
        out_specs=NEAR,
        out_shape=pltpu.VMEM(weights.shape, weights.dtype),
        scratch_shapes=[pltpu.SemaphoreType.DMA((parts,))],
        compiler_params=pltpu.CompilerParams(vmem_limit_bytes=2 * MIB),
        cost_estimate=pl.CostEstimate(
            flops=0, bytes_accessed=4 * weights.size, transcendentals=0
        ),
        name="fetch",
    )(far(weights), after)


def experts_kernel(local, remote, w_gate, w_up, w_down, local_out, remote_out, x, hidden):
    width, units = w_gate.shape
    tile = min(256, units)
    rows = local.shape[0]
    x[:rows] = local[...]
    x[rows:] = remote[...]

    @pl.loop(0, units // tile)
    def _(part):
        at = pl.ds(pl.multiple_of(part * tile, tile), tile)
        gate = jnp.dot(x[...], w_gate[:, at], preferred_element_type=jnp.float32)
        up = jnp.dot(x[...], w_up[:, at], preferred_element_type=jnp.float32)
        hidden[:, at] = (jax.nn.silu(gate) * up).astype(jnp.bfloat16)

    @pl.loop(0, width // 512)
    def _(part):
        at = pl.ds(pl.multiple_of(part * 512, 512), 512)
        out = jnp.dot(hidden[...], w_down[:, at], preferred_element_type=jnp.float32)
        local_out[:, at] = out[:rows].astype(jnp.bfloat16)
        remote_out[:, at] = out[rows:].astype(jnp.bfloat16)


def experts(local, remote, w_gate, w_up, w_down):
    rows, width = local.shape
    units = w_gate.shape[1]
    return pl.pallas_call(
        experts_kernel,
        in_specs=[NEAR] * 5,
        out_specs=[NEAR] * 2,
        out_shape=[jax.ShapeDtypeStruct((rows, width), jnp.bfloat16)] * 2,
        scratch_shapes=[
            pltpu.VMEM((2 * rows, width), jnp.bfloat16),
            pltpu.VMEM((2 * rows, units), jnp.bfloat16),
        ],
        compiler_params=pltpu.CompilerParams(vmem_limit_bytes=20 * MIB),
        cost_estimate=pl.CostEstimate(
            flops=12 * rows * width * units,
            bytes_accessed=8 * rows * width,
            transcendentals=2 * rows * units,
        ),
        name="experts",
    )(local, remote, close(w_gate), close(w_up), close(w_down))


def join_kernel(first, second, out):
    out[...] = jnp.concatenate(
        [first[...].astype(jnp.float32), second[...].astype(jnp.float32)], axis=0
    ).astype(out.dtype)


def join(first, second):
    width = first.shape[1]
    return pl.pallas_call(
        join_kernel,
        in_specs=[NEAR, NEAR],
        out_specs=NEAR,
        out_shape=jax.ShapeDtypeStruct((first.shape[0] + second.shape[0], width), first.dtype),
        compiler_params=pltpu.CompilerParams(vmem_limit_bytes=8 * MIB),
        name="join",
    )(first, second)


def pile_kernel(*refs):
    blocks, out = refs[:-1], refs[-1]
    rows = blocks[0].shape[0]
    for at, block in enumerate(blocks):
        out[pl.ds(at * rows, rows)] = block[...]


def pile(blocks):
    rows, width = blocks[0].shape
    return pl.pallas_call(
        pile_kernel,
        in_specs=[NEAR] * len(blocks),
        out_specs=NEAR,
        out_shape=jax.ShapeDtypeStruct((len(blocks) * rows, width), blocks[0].dtype),
        compiler_params=pltpu.CompilerParams(vmem_limit_bytes=(4 + len(blocks)) * MIB),
        name="pile",
    )(*blocks)


def add_kernel(first, second, *outs):
    rows = outs[0].shape[0]
    for at, out in enumerate(outs):
        part = pl.ds(at * rows, rows)
        out[...] = (
            first[part].astype(jnp.float32) + second[part].astype(jnp.float32)
        ).astype(out.dtype)


def add_split(first, second, blocks):
    rows, width = first.shape
    each = rows // blocks
    return pl.pallas_call(
        add_kernel,
        in_specs=[NEAR, NEAR],
        out_specs=[NEAR] * blocks,
        out_shape=[jax.ShapeDtypeStruct((each, width), first.dtype)] * blocks,
        compiler_params=pltpu.CompilerParams(vmem_limit_bytes=(6 + blocks) * MIB),
        name="add_split",
    )(first, second)


def total_kernel(*refs):
    blocks, all_out, back_out = refs[:-2], refs[-2], refs[-1]
    total = blocks[0][...].astype(jnp.float32)
    for block in blocks[1:]:
        total = total + block[...].astype(jnp.float32)
    total = total.astype(all_out.dtype)
    all_out[...] = total
    back_out[...] = total[:CAP]


def total_of(blocks):
    rows, width = blocks[0].shape
    return pl.pallas_call(
        total_kernel,
        in_specs=[NEAR] * len(blocks),
        out_specs=[NEAR] * 2,
        out_shape=[
            jax.ShapeDtypeStruct((rows, width), blocks[0].dtype),
            jax.ShapeDtypeStruct((CAP, width), blocks[0].dtype),
        ],
        compiler_params=pltpu.CompilerParams(vmem_limit_bytes=(4 + len(blocks)) * MIB),
        name="total",
    )(*blocks)


def combine_kernel(mixed, weight, late, other, *refs):
    blocks, out = refs[:-1], refs[-1]
    early = blocks[0][...].astype(jnp.float32)
    for block in blocks[1:]:
        early = early + block[...].astype(jnp.float32)
    total = mixed[...]
    for place, part in enumerate((early.astype(jnp.bfloat16), late[...], other[...])):
        total = total + jnp.dot(
            weight[place][:, : part.shape[0]], part, preferred_element_type=jnp.float32
        )
    out[...] = total.astype(jnp.bfloat16)


def combine(mixed, weight, blocks, late, other):
    return pl.pallas_call(
        combine_kernel,
        in_specs=[NEAR] * (4 + len(blocks)),
        out_specs=NEAR,
        out_shape=jax.ShapeDtypeStruct(mixed.shape, jnp.bfloat16),
        compiler_params=pltpu.CompilerParams(vmem_limit_bytes=(8 + len(blocks)) * MIB),
        name="combine",
    )(close(mixed), weight, late, other, *blocks)


def shards(
    resid, queries, keys, values, segment_ids, norm_gain, routes, route_gates, w_gate, w_up, w_down
):
    count = lax.axis_size("expert")
    own = lax.axis_index("expert")
    shard_count = count // E_WIN
    odd = own % 2

    next_chip = [(i, i + 2) for i in range(count - 2)]
    crossing = [(i, i + 1) for i in range(0, count, 2)]
    crossing += [(i, i + 3) for i in range(1, count - 3, 2)]

    def swapped(block, mask):
        return lax.ppermute(block, "expert", [(i, i ^ mask) for i in range(count)])

    seg_own = segment_ids.reshape(1, -1)
    value_two = lax.ppermute(values, "expert", next_chip)
    key_block = bundle(keys, seg_own)
    key_two = lax.ppermute(key_block, "expert", next_chip)
    value_cross = lax.ppermute(values, "expert", crossing)
    key_cross = lax.ppermute(key_block, "expert", crossing)
    beyond = 2 * WIN_DEV + 2
    delta_list = [0 * own, 0 * own + 2, 3 - 2 * odd, 1 + 2 * odd]
    my_expert = own // shard_count
    scalars = jnp.stack(
        [jnp.where(own >= delta, delta, beyond) for delta in delta_list] + [my_expert]
    ).astype(jnp.int32)
    held = [fetch(w, scalars) for w in (w_gate, w_up, w_down)]
    key_two, held[0], held[1] = lax.optimization_barrier((key_two, held[0], held[1]))
    key_mirror = swapped(key_two, 1)
    value_two, held[2] = lax.optimization_barrier((value_two, held[2]))
    value_mirror = swapped(value_two, 1)

    mixed, early, rest, send, weight = attention(
        scalars,
        queries,
        [keys, values, key_two, value_two, key_cross, value_cross, key_mirror, value_mirror],
        seg_own, resid, norm_gain.reshape(1, -1), routes.T, route_gates.T,
    )
    partner = [(i, (i + shard_count) % count) for i in range(count)]
    masks = range(2, shard_count, 2)
    got = lax.ppermute(send, "expert", partner)

    def spread(block):
        return [block] + [swapped(block, mask) for mask in masks]

    def both_cores(blocks):
        local = pile(blocks)
        return local, swapped(local, 1)

    def summed(parts):
        return add_split(parts[0], swapped(parts[1], 1), 1 + len(masks))

    def scattered(blocks):
        return [blocks[0]] + [swapped(block, mask) for block, mask in zip(blocks[1:], masks)]

    early_blocks = spread(early)
    got, early_blocks = lax.optimization_barrier((got, early_blocks))
    early_parts = experts(*both_cores(early_blocks), *held)
    late_blocks = spread(join(got, rest))
    late_blocks, early_parts = lax.optimization_barrier((late_blocks, early_parts))
    late_rows = both_cores(late_blocks)
    late_blocks = summed(experts(*late_rows, *held))
    early_blocks = summed(early_parts)
    late_blocks, early_blocks = lax.optimization_barrier((late_blocks, early_blocks))
    late, back = total_of(scattered(late_blocks))
    other = lax.ppermute(back, "expert", partner)
    return combine(mixed, weight, scattered(early_blocks), late, other)


def solution(mesh):
    placed = (
        P(("groups", "expert"), None),
        P(("groups", "expert"), None),
        P(("groups", "expert"), None),
        P(("groups", "expert"), None),
        P(("groups", "expert")),
        P(),
        P(("groups", "expert"), None),
        P(("groups", "expert"), None),
        P(None, "expert"),
        P(None, "expert"),
        P("expert", None),
    )
    return jax.shard_map(
        shards, mesh=mesh, in_specs=placed, out_specs=P(("groups", "expert"), None), check_vma=False
    )
```

```python
import functools

import jax
import jax.numpy as jnp
from jax import lax
from jax.experimental import pallas as pl
from jax.experimental.pallas import tpu as pltpu
from jax.sharding import PartitionSpec as P

HEAD_DIM = 128
E_WIN = 2
WIN_DEV = 3
CAP = 20
EARLY = 16
SPARE = 16
HEADS_STEP = 8
MASKED = -1e30
MIB = 1024 * 1024


def far(x):
    return pltpu.with_memory_space_constraint(x, pltpu.HBM)


def close(x):
    return pltpu.with_memory_space_constraint(x, pltpu.VMEM)


NEAR = pl.BlockSpec(memory_space=pltpu.VMEM)


def bundle_kernel(keys, segs, out):
    rows, width = keys.shape
    out[:, :width] = keys[...]
    out[:, width:] = jnp.zeros((rows, HEAD_DIM), keys.dtype)
    out[:SPARE, width : width + rows] = jnp.broadcast_to(
        segs[...].astype(jnp.float32), (SPARE, rows)
    ).astype(keys.dtype)


def bundle(keys, segs):
    rows, width = keys.shape
    return pl.pallas_call(
        bundle_kernel,
        in_specs=[NEAR, NEAR],
        out_specs=NEAR,
        out_shape=jax.ShapeDtypeStruct((rows, width + HEAD_DIM), keys.dtype),
        cost_estimate=pl.CostEstimate(
            flops=0, bytes_accessed=4 * rows * width, transcendentals=0
        ),
        compiler_params=pltpu.CompilerParams(vmem_limit_bytes=6 * MIB),
        name="bundle",
    )(far(keys), far(segs))


def attention_kernel(
    deltas, q, k0, v0, k1, v1, k2, v2, k3, v3, seg0, seg1, seg2, seg3, resid, gain, routes, gates,
    mixed_out, early_out, rest_out, send_out, weight_out, bias,
):
    step = pl.program_id(0)
    steps = pl.num_programs(0)
    rows = q.shape[0]
    keys = (WIN_DEV + 1) * rows

    @pl.when(step == 0)
    def _():
        seg_own = seg0[...].astype(jnp.float32)
        seg_row = jnp.concatenate(
            [seg_own] + [seg[0:1, :rows].astype(jnp.float32) for seg in (seg1, seg2, seg3)],
            axis=1,
        )
        eye = lax.broadcasted_iota(jnp.int32, (rows, rows), 0) == lax.broadcasted_iota(
            jnp.int32, (rows, rows), 1
        )
        seg_col = jnp.sum(jnp.where(eye, seg_own, 0.0), axis=1, keepdims=True)
        lane = lax.broadcasted_iota(jnp.int32, (rows, keys), 1)
        sub = lax.broadcasted_iota(jnp.int32, (rows, keys), 0)
        block = lane // rows
        back = jnp.where(
            block == 0,
            deltas[0],
            jnp.where(block == 1, deltas[1], jnp.where(block == 2, deltas[2], deltas[3])),
        )
        distance = sub - (lane - block * rows) + back * rows
        allowed = (distance >= 0) & (distance <= WIN_DEV * rows) & (seg_col == seg_row)
        bias[...] = jnp.where(allowed, 0.0, MASKED)

    scale = 1.0 / HEAD_DIM**0.5
    heads = [slice(head * HEAD_DIM, (head + 1) * HEAD_DIM) for head in range(HEADS_STEP)]
    scores = jnp.stack(
        [
            lax.dot_general(
                q[:, cols],
                jnp.concatenate([k0[:, cols], k1[:, cols], k2[:, cols], k3[:, cols]], axis=0),
                (((1,), (1,)), ((), ())),
                preferred_element_type=jnp.float32,
            )
            for cols in heads
        ]
    )
    scores = scores * scale + bias[...][None]
    expo = jnp.exp(scores - jnp.max(scores, axis=2, keepdims=True))
    denom = jnp.sum(expo, axis=2, keepdims=True)
    probs = expo.astype(jnp.bfloat16)
    outs = [
        jnp.dot(
            probs[head],
            jnp.concatenate([v0[:, cols], v1[:, cols], v2[:, cols], v3[:, cols]], axis=0),
            preferred_element_type=jnp.float32,
        )
        / denom[head]
        for head, cols in enumerate(heads)
    ]
    width = HEADS_STEP * HEAD_DIM
    at = pl.ds(pl.multiple_of(step * width, width), width)
    mixed_out[:, at] = resid[...].astype(jnp.float32) + jnp.concatenate(outs, axis=1)

    @pl.when(step == steps - 1)
    def _():
        mixed = mixed_out[...]
        normed = (
            mixed * lax.rsqrt(jnp.mean(mixed * mixed, axis=1, keepdims=True) + 1e-05) * gain[...]
        ).astype(jnp.bfloat16)
        across = lax.broadcasted_iota(jnp.int32, (rows, rows), 1)
        down = lax.broadcasted_iota(jnp.int32, (rows, rows), 0)
        upper = jnp.where(down < across, 1.0, 0.0).astype(jnp.bfloat16)
        eye = jnp.where(down == across, 1.0, 0.0).astype(jnp.bfloat16)
        slot = lax.broadcasted_iota(jnp.int32, (32, rows), 0)

        def picks(expert):
            hit = routes[...] == expert
            member = jnp.max(jnp.where(hit, 1.0, 0.0), axis=0, keepdims=True)
            weight = jnp.sum(
                jnp.where(hit, gates[...].astype(jnp.float32), 0.0), axis=0, keepdims=True
            )
            rank = jnp.dot(
                jnp.broadcast_to(member, (8, rows)).astype(jnp.bfloat16),
                upper,
                preferred_element_type=jnp.float32,
            )[0:1].astype(jnp.int32)
            return member > 0.5, weight, rank

        def spread(pick, weight):
            return lax.dot_general(
                eye,
                jnp.where(pick, weight, 0.0).astype(jnp.bfloat16),
                (((1,), (1,)), ((), ())),
                preferred_element_type=jnp.float32,
            ).astype(jnp.bfloat16)

        def packed(pick):
            return jnp.dot(
                jnp.where(pick, 1.0, 0.0).astype(jnp.bfloat16),
                normed,
                preferred_element_type=jnp.float32,
            ).astype(jnp.bfloat16)

        member, weight, rank = picks(deltas[4])
        pick = (slot == rank) & member
        mine = packed(pick)
        early_out[...] = mine[:EARLY]
        rest_out[...] = mine[EARLY:CAP]
        weight_out[0] = spread(pick & (slot < EARLY), weight)
        weight_out[1] = spread((slot - CAP + EARLY == rank) & (slot >= CAP) & member, weight)
        member, weight, rank = picks(1 - deltas[4])
        pick = (slot == rank) & member
        send_out[...] = packed(pick)[:CAP]
        weight_out[2] = spread(pick, weight)


def attention(deltas, q, pairs, seg_own, resid, gain, routes, gates):
    rows, width = q.shape
    cols = HEADS_STEP * HEAD_DIM
    top = routes.shape[0]
    piece = pl.BlockSpec((rows, cols), lambda j, *_: (0, j))
    tail = pl.BlockSpec((SPARE, HEAD_DIM), lambda j, *_: (0, width // HEAD_DIM))

    def whole(shape):
        return pl.BlockSpec(shape, lambda j, *_: (0,) * len(shape))

    bundles = pairs[2::2]
    return pl.pallas_call(
        attention_kernel,
        grid_spec=pltpu.PrefetchScalarGridSpec(
            num_scalar_prefetch=1,
            grid=(width // cols,),
            in_specs=[piece] * (1 + len(pairs))
            + [whole((1, rows))]
            + [tail] * len(bundles)
            + [
                piece,
                whole((1, width)),
                whole((top, rows)),
                whole((top, rows)),
            ],
            out_specs=[
                whole((rows, width)),
                whole((EARLY, width)),
                whole((CAP - EARLY, width)),
                whole((CAP, width)),
                whole((3, rows, 32)),
            ],
            scratch_shapes=[pltpu.VMEM((rows, (WIN_DEV + 1) * rows), jnp.float32)],
        ),
        out_shape=[
            pltpu.VMEM((rows, width), jnp.float32),
            jax.ShapeDtypeStruct((EARLY, width), jnp.bfloat16),
            jax.ShapeDtypeStruct((CAP - EARLY, width), jnp.bfloat16),
            jax.ShapeDtypeStruct((CAP, width), jnp.bfloat16),
            jax.ShapeDtypeStruct((3, rows, 32), jnp.bfloat16),
        ],
        compiler_params=pltpu.CompilerParams(vmem_limit_bytes=14 * MIB),
        cost_estimate=pl.CostEstimate(
            flops=4 * rows * 4 * rows * width, bytes_accessed=8 * rows * width * 4,
            transcendentals=rows * 4 * rows * (width // HEAD_DIM),
        ),
        name="attention",
    )(
        deltas, far(q), far(pairs[0]), far(pairs[1]), *pairs[2:], far(seg_own), *bundles,
        far(resid), far(gain), far(routes), far(gates),
    )


def fetch_kernel(parts, source, after, held, sems):
    depth = source.shape[0] // parts
    copies = []
    for part in range(parts):
        at = pl.ds(part * depth, depth)
        copies.append(pltpu.make_async_copy(source.at[at], held.at[at], sems.at[part]))
    for copy in copies:
        copy.start()
    for copy in copies:
        copy.wait()


def fetch(weights, after):
    parts = 4
    anywhere = pl.BlockSpec(memory_space=pl.ANY)
    return pl.pallas_call(
        functools.partial(fetch_kernel, parts),
        in_specs=[anywhere, anywhere],
        out_specs=NEAR,
        out_shape=pltpu.VMEM(weights.shape, weights.dtype),
        scratch_shapes=[pltpu.SemaphoreType.DMA((parts,))],
        compiler_params=pltpu.CompilerParams(vmem_limit_bytes=2 * MIB),
        cost_estimate=pl.CostEstimate(
            flops=0, bytes_accessed=4 * weights.size, transcendentals=0
        ),
        name="fetch",
    )(far(weights), after)


def experts_kernel(local, remote, w_gate, w_up, w_down, local_out, remote_out, x, hidden):
    width, units = w_gate.shape
    tile = min(512, units)
    rows = local.shape[0]
    x[:rows] = local[...]
    x[rows:] = remote[...]

    @pl.loop(0, units // tile)
    def _(part):
        at = pl.ds(pl.multiple_of(part * tile, tile), tile)
        gate = jnp.dot(x[...], w_gate[:, at], preferred_element_type=jnp.float32)
        up = jnp.dot(x[...], w_up[:, at], preferred_element_type=jnp.float32)
        hidden[:, at] = (jax.nn.silu(gate) * up).astype(jnp.bfloat16)

    @pl.loop(0, width // 1024)
    def _(part):
        at = pl.ds(pl.multiple_of(part * 1024, 1024), 1024)
        out = jnp.dot(hidden[...], w_down[:, at], preferred_element_type=jnp.float32)
        local_out[:, at] = out[:rows].astype(jnp.bfloat16)
        remote_out[:, at] = out[rows:].astype(jnp.bfloat16)


def experts(local, remote, w_gate, w_up, w_down):
    rows, width = local.shape
    units = w_gate.shape[1]
    return pl.pallas_call(
        experts_kernel,
        in_specs=[NEAR] * 5,
        out_specs=[NEAR] * 2,
        out_shape=[jax.ShapeDtypeStruct((rows, width), jnp.bfloat16)] * 2,
        scratch_shapes=[
            pltpu.VMEM((2 * rows, width), jnp.bfloat16),
            pltpu.VMEM((2 * rows, units), jnp.bfloat16),
        ],
        compiler_params=pltpu.CompilerParams(vmem_limit_bytes=20 * MIB),
        cost_estimate=pl.CostEstimate(
            flops=12 * rows * width * units,
            bytes_accessed=8 * rows * width,
            transcendentals=2 * rows * units,
        ),
        name="experts",
    )(local, remote, close(w_gate), close(w_up), close(w_down))


def join_kernel(first, second, out):
    out[...] = jnp.concatenate(
        [first[...].astype(jnp.float32), second[...].astype(jnp.float32)], axis=0
    ).astype(out.dtype)


def join(first, second):
    width = first.shape[1]
    return pl.pallas_call(
        join_kernel,
        in_specs=[NEAR, NEAR],
        out_specs=NEAR,
        out_shape=jax.ShapeDtypeStruct((first.shape[0] + second.shape[0], width), first.dtype),
        compiler_params=pltpu.CompilerParams(vmem_limit_bytes=8 * MIB),
        name="join",
    )(first, second)


def pile_kernel(*refs):
    blocks, out = refs[:-1], refs[-1]
    rows = blocks[0].shape[0]
    for at, block in enumerate(blocks):
        out[pl.ds(at * rows, rows)] = block[...]


def pile(blocks):
    rows, width = blocks[0].shape
    return pl.pallas_call(
        pile_kernel,
        in_specs=[NEAR] * len(blocks),
        out_specs=NEAR,
        out_shape=jax.ShapeDtypeStruct((len(blocks) * rows, width), blocks[0].dtype),
        compiler_params=pltpu.CompilerParams(vmem_limit_bytes=(4 + len(blocks)) * MIB),
        name="pile",
    )(*blocks)


def add_kernel(first, second, *outs):
    rows = outs[0].shape[0]
    for at, out in enumerate(outs):
        part = pl.ds(at * rows, rows)
        out[...] = (
            first[part].astype(jnp.float32) + second[part].astype(jnp.float32)
        ).astype(out.dtype)


def add_split(first, second, blocks):
    rows, width = first.shape
    each = rows // blocks
    return pl.pallas_call(
        add_kernel,
        in_specs=[NEAR, NEAR],
        out_specs=[NEAR] * blocks,
        out_shape=[jax.ShapeDtypeStruct((each, width), first.dtype)] * blocks,
        compiler_params=pltpu.CompilerParams(vmem_limit_bytes=(6 + blocks) * MIB),
        name="add_split",
    )(first, second)


def total_kernel(*refs):
    blocks, all_out, back_out = refs[:-2], refs[-2], refs[-1]
    total = blocks[0][...].astype(jnp.float32)
    for block in blocks[1:]:
        total = total + block[...].astype(jnp.float32)
    total = total.astype(all_out.dtype)
    all_out[...] = total
    back_out[...] = total[:CAP]


def total_of(blocks):
    rows, width = blocks[0].shape
    return pl.pallas_call(
        total_kernel,
        in_specs=[NEAR] * len(blocks),
        out_specs=[NEAR] * 2,
        out_shape=[
            jax.ShapeDtypeStruct((rows, width), blocks[0].dtype),
            jax.ShapeDtypeStruct((CAP, width), blocks[0].dtype),
        ],
        compiler_params=pltpu.CompilerParams(vmem_limit_bytes=(4 + len(blocks)) * MIB),
        name="total",
    )(*blocks)


def combine_kernel(mixed, weight, late, other, *refs):
    blocks, out = refs[:-1], refs[-1]
    early = blocks[0][...].astype(jnp.float32)
    for block in blocks[1:]:
        early = early + block[...].astype(jnp.float32)
    total = mixed[...]
    for place, part in enumerate((early.astype(jnp.bfloat16), late[...], other[...])):
        total = total + jnp.dot(
            weight[place][:, : part.shape[0]], part, preferred_element_type=jnp.float32
        )
    out[...] = total.astype(jnp.bfloat16)


def combine(mixed, weight, blocks, late, other):
    return pl.pallas_call(
        combine_kernel,
        in_specs=[NEAR] * (4 + len(blocks)),
        out_specs=NEAR,
        out_shape=jax.ShapeDtypeStruct(mixed.shape, jnp.bfloat16),
        compiler_params=pltpu.CompilerParams(vmem_limit_bytes=(8 + len(blocks)) * MIB),
        name="combine",
    )(close(mixed), weight, late, other, *blocks)


def shards(
    resid, queries, keys, values, segment_ids, norm_gain, routes, route_gates, w_gate, w_up, w_down
):
    count = lax.axis_size("expert")
    own = lax.axis_index("expert")
    shard_count = count // E_WIN
    odd = own % 2

    next_chip = [(i, i + 2) for i in range(count - 2)]
    crossing = [(i, i + 1) for i in range(0, count, 2)]
    crossing += [(i, i + 3) for i in range(1, count - 3, 2)]

    def swapped(block, mask):
        return lax.ppermute(block, "expert", [(i, i ^ mask) for i in range(count)])

    seg_own = segment_ids.reshape(1, -1)
    value_two = lax.ppermute(values, "expert", next_chip)
    key_block = bundle(keys, seg_own)
    key_two = lax.ppermute(key_block, "expert", next_chip)
    value_cross = lax.ppermute(values, "expert", crossing)
    key_cross = lax.ppermute(key_block, "expert", crossing)
    beyond = 2 * WIN_DEV + 2
    delta_list = [0 * own, 0 * own + 2, 3 - 2 * odd, 1 + 2 * odd]
    my_expert = own // shard_count
    scalars = jnp.stack(
        [jnp.where(own >= delta, delta, beyond) for delta in delta_list] + [my_expert]
    ).astype(jnp.int32)
    held = [fetch(w, scalars) for w in (w_gate, w_up, w_down)]
    key_two, held[0], held[1] = lax.optimization_barrier((key_two, held[0], held[1]))
    key_mirror = swapped(key_two, 1)
    value_two, held[2] = lax.optimization_barrier((value_two, held[2]))
    value_mirror = swapped(value_two, 1)

    mixed, early, rest, send, weight = attention(
        scalars,
        queries,
        [keys, values, key_two, value_two, key_cross, value_cross, key_mirror, value_mirror],
        seg_own, resid, norm_gain.reshape(1, -1), routes.T, route_gates.T,
    )
    partner = [(i, (i + shard_count) % count) for i in range(count)]
    masks = list(range(2, shard_count, 2))[::-1]
    got = lax.ppermute(send, "expert", partner)

    def spread(block):
        return [block] + [swapped(block, mask) for mask in masks]

    def both_cores(blocks):
        local = pile(blocks)
        return local, swapped(local, 1)

    def summed(parts):
        return add_split(parts[0], swapped(parts[1], 1), 1 + len(masks))

    def scattered(blocks):
        moved = [swapped(block, mask) for block, mask in zip(blocks[1:], masks)]
        return [blocks[0]] + moved[::-1]

    early_blocks = spread(early)
    got, early_blocks = lax.optimization_barrier((got, early_blocks))
    early_parts = experts(*both_cores(early_blocks), *held)
    late_blocks = spread(join(got, rest))
    late_blocks, early_parts = lax.optimization_barrier((late_blocks, early_parts))
    late_rows = both_cores(late_blocks)
    early_blocks = summed(early_parts)
    late_rows, early_blocks = lax.optimization_barrier((late_rows, early_blocks))
    early_blocks = scattered(early_blocks)
    late_parts = experts(*late_rows, *held)
    late_parts, early_blocks = lax.optimization_barrier((late_parts, early_blocks))
    late_blocks = summed(late_parts)
    late, back = total_of(scattered(late_blocks))
    other = lax.ppermute(back, "expert", partner)
    return combine(mixed, weight, early_blocks, late, other)


def solution(mesh):
    placed = (
        P(("groups", "expert"), None),
        P(("groups", "expert"), None),
        P(("groups", "expert"), None),
        P(("groups", "expert"), None),
        P(("groups", "expert")),
        P(),
        P(("groups", "expert"), None),
        P(("groups", "expert"), None),
        P(None, "expert"),
        P(None, "expert"),
        P("expert", None),
    )
    return jax.shard_map(
        shards, mesh=mesh, in_specs=placed, out_specs=P(("groups", "expert"), None), check_vma=False
    )
```

```python
import functools

import jax
import jax.numpy as jnp
from jax import lax
from jax.experimental import pallas as pl
from jax.experimental.pallas import tpu as pltpu
from jax.sharding import PartitionSpec as P

HEAD_DIM = 128
E_WIN = 2
WIN_DEV = 3
CAP = 20
EARLY = 16
SPARE = 16
HEADS_STEP = 8
MASKED = -1e30
MIB = 1024 * 1024


def far(x):
    return pltpu.with_memory_space_constraint(x, pltpu.HBM)


def close(x):
    return pltpu.with_memory_space_constraint(x, pltpu.VMEM)


NEAR = pl.BlockSpec(memory_space=pltpu.VMEM)


def bundle_kernel(keys, segs, out):
    rows, width = keys.shape
    out[:, :width] = keys[...]
    out[:, width:] = jnp.zeros((rows, HEAD_DIM), keys.dtype)
    out[:SPARE, width : width + rows] = jnp.broadcast_to(
        segs[...].astype(jnp.float32), (SPARE, rows)
    ).astype(keys.dtype)


def bundle(keys, segs):
    rows, width = keys.shape
    return pl.pallas_call(
        bundle_kernel,
        in_specs=[NEAR, NEAR],
        out_specs=NEAR,
        out_shape=jax.ShapeDtypeStruct((rows, width + HEAD_DIM), keys.dtype),
        cost_estimate=pl.CostEstimate(
            flops=0, bytes_accessed=4 * rows * width, transcendentals=0
        ),
        compiler_params=pltpu.CompilerParams(vmem_limit_bytes=6 * MIB),
        name="bundle",
    )(far(keys), far(segs))


def choose_kernel(flags, first, second, out):
    @pl.when(flags[5] == 1)
    def _():
        out[...] = first[...]

    @pl.when(flags[5] != 1)
    def _():
        out[...] = second[...]


def choose(flags, first, second):
    return pl.pallas_call(
        choose_kernel,
        in_specs=[pl.BlockSpec(memory_space=pltpu.SMEM), NEAR, NEAR],
        out_specs=NEAR,
        out_shape=jax.ShapeDtypeStruct(first.shape, first.dtype),
        compiler_params=pltpu.CompilerParams(vmem_limit_bytes=6 * MIB),
        name="choose",
    )(flags, first, second)


def attention_kernel(
    deltas, q, k0, v0, k1, v1, k2, v2, k3, v3, seg0, resid, gain, routes, gates,
    mixed_out, early_out, rest_out, send_out, weight_out,
):
    rows, model = q.shape
    keys = (WIN_DEV + 1) * rows
    width = HEADS_STEP * HEAD_DIM

    seg_own = seg0[...].astype(jnp.float32)
    seg_row = jnp.concatenate(
        [seg_own]
        + [block[:SPARE, model:][0:1, :rows].astype(jnp.float32) for block in (k1, k2, k3)],
        axis=1,
    )
    eye = lax.broadcasted_iota(jnp.int32, (rows, rows), 0) == lax.broadcasted_iota(
        jnp.int32, (rows, rows), 1
    )
    seg_col = jnp.sum(jnp.where(eye, seg_own, 0.0), axis=1, keepdims=True)
    lane = lax.broadcasted_iota(jnp.int32, (rows, keys), 1)
    sub = lax.broadcasted_iota(jnp.int32, (rows, keys), 0)
    block = lane // rows
    back = jnp.where(
        block == 0,
        deltas[0],
        jnp.where(block == 1, deltas[1], jnp.where(block == 2, deltas[2], deltas[3])),
    )
    distance = sub - (lane - block * rows) + back * rows
    allowed = (distance >= 0) & (distance <= WIN_DEV * rows) & (seg_col == seg_row)
    bias = jnp.where(allowed, 0.0, MASKED)
    scale = 1.0 / HEAD_DIM**0.5
    heads = [slice(head * HEAD_DIM, (head + 1) * HEAD_DIM) for head in range(HEADS_STEP)]

    @pl.loop(0, model // width)
    def _(step):
        at = pl.ds(pl.multiple_of(step * width, width), width)
        query = q[:, at]
        key = jnp.concatenate([k0[:, at], k1[:, at], k2[:, at], k3[:, at]], axis=0)
        value = jnp.concatenate([v0[:, at], v1[:, at], v2[:, at], v3[:, at]], axis=0)
        scores = jnp.stack(
            [
                lax.dot_general(
                    query[:, cols], key[:, cols], (((1,), (1,)), ((), ())),
                    preferred_element_type=jnp.float32,
                )
                for cols in heads
            ]
        )
        scores = scores * scale + bias[None]
        expo = jnp.exp(scores - jnp.max(scores, axis=2, keepdims=True))
        denom = jnp.sum(expo, axis=2, keepdims=True)
        probs = expo.astype(jnp.bfloat16)
        outs = [
            jnp.dot(probs[head], value[:, cols], preferred_element_type=jnp.float32)
            / denom[head]
            for head, cols in enumerate(heads)
        ]
        mixed_out[:, at] = resid[:, at].astype(jnp.float32) + jnp.concatenate(outs, axis=1)

    mixed = mixed_out[...]
    normed = (
        mixed * lax.rsqrt(jnp.mean(mixed * mixed, axis=1, keepdims=True) + 1e-05) * gain[...]
    ).astype(jnp.bfloat16)
    across = lax.broadcasted_iota(jnp.int32, (rows, rows), 1)
    down = lax.broadcasted_iota(jnp.int32, (rows, rows), 0)
    upper = jnp.where(down < across, 1.0, 0.0).astype(jnp.bfloat16)
    eye = jnp.where(down == across, 1.0, 0.0).astype(jnp.bfloat16)
    slot = lax.broadcasted_iota(jnp.int32, (32, rows), 0)

    def picks(expert):
        hit = routes[...] == expert
        member = jnp.max(jnp.where(hit, 1.0, 0.0), axis=0, keepdims=True)
        weight = jnp.sum(
            jnp.where(hit, gates[...].astype(jnp.float32), 0.0), axis=0, keepdims=True
        )
        rank = jnp.dot(
            jnp.broadcast_to(member, (8, rows)).astype(jnp.bfloat16),
            upper,
            preferred_element_type=jnp.float32,
        )[0:1].astype(jnp.int32)
        return member > 0.5, weight, rank

    def spread(pick, weight):
        return lax.dot_general(
            eye,
            jnp.where(pick, weight, 0.0).astype(jnp.bfloat16),
            (((1,), (1,)), ((), ())),
            preferred_element_type=jnp.float32,
        ).astype(jnp.bfloat16)

    def packed(pick):
        return jnp.dot(
            jnp.where(pick, 1.0, 0.0).astype(jnp.bfloat16),
            normed,
            preferred_element_type=jnp.float32,
        ).astype(jnp.bfloat16)

    member, weight, rank = picks(deltas[4])
    pick = (slot == rank) & member
    mine = packed(pick)
    early_out[...] = mine[:EARLY]
    rest_out[...] = mine[EARLY:CAP]
    weight_out[0] = spread(pick & (slot < EARLY), weight)
    weight_out[1] = spread((slot - CAP + EARLY == rank) & (slot >= CAP) & member, weight)
    member, weight, rank = picks(1 - deltas[4])
    pick = (slot == rank) & member
    send_out[...] = packed(pick)[:CAP]
    weight_out[2] = spread(pick, weight)


def attention(deltas, q, pairs, seg_own, resid, gain, routes, gates):
    rows, width = q.shape
    return pl.pallas_call(
        attention_kernel,
        in_specs=[pl.BlockSpec(memory_space=pltpu.SMEM)] + [NEAR] * (6 + len(pairs)),
        out_specs=[NEAR] * 5,
        out_shape=[
            pltpu.VMEM((rows, width), jnp.float32),
            jax.ShapeDtypeStruct((EARLY, width), jnp.bfloat16),
            jax.ShapeDtypeStruct((CAP - EARLY, width), jnp.bfloat16),
            jax.ShapeDtypeStruct((CAP, width), jnp.bfloat16),
            jax.ShapeDtypeStruct((3, rows, 32), jnp.bfloat16),
        ],
        compiler_params=pltpu.CompilerParams(vmem_limit_bytes=14 * MIB),
        cost_estimate=pl.CostEstimate(
            flops=4 * rows * 4 * rows * width, bytes_accessed=8 * rows * width * 4,
            transcendentals=rows * 4 * rows * (width // HEAD_DIM),
        ),
        name="attention",
    )(
        deltas, close(q), close(pairs[0]), close(pairs[1]), *pairs[2:], close(seg_own),
        close(resid), close(gain), close(routes), close(gates),
    )


def bring_kernel(count, *refs):
    sources, held, sems = refs[:count], refs[count + 1 : 2 * count + 1], refs[-1]
    copies = [
        pltpu.make_async_copy(source, target, sems.at[at])
        for at, (source, target) in enumerate(zip(sources, held))
    ]
    for copy in copies:
        copy.start()
    for copy in copies:
        copy.wait()


def bring(arrays, after):
    count = len(arrays)
    anywhere = pl.BlockSpec(memory_space=pl.ANY)
    return pl.pallas_call(
        functools.partial(bring_kernel, count),
        in_specs=[anywhere] * (count + 1),
        out_specs=[NEAR] * count,
        out_shape=[pltpu.VMEM(x.shape, x.dtype) for x in arrays],
        scratch_shapes=[pltpu.SemaphoreType.DMA((count,))],
        compiler_params=pltpu.CompilerParams(vmem_limit_bytes=2 * MIB),
        cost_estimate=pl.CostEstimate(
            flops=0, bytes_accessed=4 * sum(x.size for x in arrays), transcendentals=0
        ),
        name="bring",
    )(*[far(x) for x in arrays], after)


def fetch_kernel(parts, source, after, held, sems):
    depth = source.shape[0] // parts
    copies = []
    for part in range(parts):
        at = pl.ds(part * depth, depth)
        copies.append(pltpu.make_async_copy(source.at[at], held.at[at], sems.at[part]))
    for copy in copies:
        copy.start()
    for copy in copies:
        copy.wait()


def fetch(weights, after):
    parts = 4
    anywhere = pl.BlockSpec(memory_space=pl.ANY)
    return pl.pallas_call(
        functools.partial(fetch_kernel, parts),
        in_specs=[anywhere, anywhere],
        out_specs=NEAR,
        out_shape=pltpu.VMEM(weights.shape, weights.dtype),
        scratch_shapes=[pltpu.SemaphoreType.DMA((parts,))],
        compiler_params=pltpu.CompilerParams(vmem_limit_bytes=2 * MIB),
        cost_estimate=pl.CostEstimate(
            flops=0, bytes_accessed=4 * weights.size, transcendentals=0
        ),
        name="fetch",
    )(far(weights), after)


def experts_kernel(local, remote, w_gate, w_up, w_down, local_out, remote_out, x, hidden):
    width, units = w_gate.shape
    tile = min(512, units)
    rows = local.shape[0]
    x[:rows] = local[...]
    x[rows:] = remote[...]

    @pl.loop(0, units // tile)
    def _(part):
        at = pl.ds(pl.multiple_of(part * tile, tile), tile)
        gate = jnp.dot(x[...], w_gate[:, at], preferred_element_type=jnp.float32)
        up = jnp.dot(x[...], w_up[:, at], preferred_element_type=jnp.float32)
        hidden[:, at] = (jax.nn.silu(gate) * up).astype(jnp.bfloat16)

    @pl.loop(0, width // 1024)
    def _(part):
        at = pl.ds(pl.multiple_of(part * 1024, 1024), 1024)
        out = jnp.dot(hidden[...], w_down[:, at], preferred_element_type=jnp.float32)
        local_out[:, at] = out[:rows].astype(jnp.bfloat16)
        remote_out[:, at] = out[rows:].astype(jnp.bfloat16)


def experts(local, remote, w_gate, w_up, w_down):
    rows, width = local.shape
    units = w_gate.shape[1]
    return pl.pallas_call(
        experts_kernel,
        in_specs=[NEAR] * 5,
        out_specs=[NEAR] * 2,
        out_shape=[jax.ShapeDtypeStruct((rows, width), jnp.bfloat16)] * 2,
        scratch_shapes=[
            pltpu.VMEM((2 * rows, width), jnp.bfloat16),
            pltpu.VMEM((2 * rows, units), jnp.bfloat16),
        ],
        compiler_params=pltpu.CompilerParams(vmem_limit_bytes=20 * MIB),
        cost_estimate=pl.CostEstimate(
            flops=12 * rows * width * units,
            bytes_accessed=8 * rows * width,
            transcendentals=2 * rows * units,
        ),
        name="experts",
    )(local, remote, close(w_gate), close(w_up), close(w_down))


def join_kernel(first, second, out):
    out[...] = jnp.concatenate(
        [first[...].astype(jnp.float32), second[...].astype(jnp.float32)], axis=0
    ).astype(out.dtype)


def join(first, second):
    width = first.shape[1]
    return pl.pallas_call(
        join_kernel,
        in_specs=[NEAR, NEAR],
        out_specs=NEAR,
        out_shape=jax.ShapeDtypeStruct((first.shape[0] + second.shape[0], width), first.dtype),
        compiler_params=pltpu.CompilerParams(vmem_limit_bytes=8 * MIB),
        name="join",
    )(first, second)


def pile_kernel(*refs):
    blocks, out = refs[:-1], refs[-1]
    rows = blocks[0].shape[0]
    for at, block in enumerate(blocks):
        out[pl.ds(at * rows, rows)] = block[...]


def pile(blocks):
    rows, width = blocks[0].shape
    return pl.pallas_call(
        pile_kernel,
        in_specs=[NEAR] * len(blocks),
        out_specs=NEAR,
        out_shape=jax.ShapeDtypeStruct((len(blocks) * rows, width), blocks[0].dtype),
        compiler_params=pltpu.CompilerParams(vmem_limit_bytes=(4 + len(blocks)) * MIB),
        name="pile",
    )(*blocks)


def add_kernel(first, second, *outs):
    rows = outs[0].shape[0]
    for at, out in enumerate(outs):
        part = pl.ds(at * rows, rows)
        out[...] = (
            first[part].astype(jnp.float32) + second[part].astype(jnp.float32)
        ).astype(out.dtype)


def add_split(first, second, blocks):
    rows, width = first.shape
    each = rows // blocks
    return pl.pallas_call(
        add_kernel,
        in_specs=[NEAR, NEAR],
        out_specs=[NEAR] * blocks,
        out_shape=[jax.ShapeDtypeStruct((each, width), first.dtype)] * blocks,
        compiler_params=pltpu.CompilerParams(vmem_limit_bytes=(6 + blocks) * MIB),
        name="add_split",
    )(first, second)


def total_kernel(*refs):
    blocks, all_out, back_out = refs[:-2], refs[-2], refs[-1]
    total = blocks[0][...].astype(jnp.float32)
    for block in blocks[1:]:
        total = total + block[...].astype(jnp.float32)
    total = total.astype(all_out.dtype)
    all_out[...] = total
    back_out[...] = total[:CAP]


def total_of(blocks):
    rows, width = blocks[0].shape
    return pl.pallas_call(
        total_kernel,
        in_specs=[NEAR] * len(blocks),
        out_specs=[NEAR] * 2,
        out_shape=[
            jax.ShapeDtypeStruct((rows, width), blocks[0].dtype),
            jax.ShapeDtypeStruct((CAP, width), blocks[0].dtype),
        ],
        compiler_params=pltpu.CompilerParams(vmem_limit_bytes=(4 + len(blocks)) * MIB),
        name="total",
    )(*blocks)


def combine_kernel(mixed, weight, late, other, *refs):
    blocks, out = refs[:-1], refs[-1]
    early = blocks[0][...].astype(jnp.float32)
    for block in blocks[1:]:
        early = early + block[...].astype(jnp.float32)
    total = mixed[...]
    for place, part in enumerate((early.astype(jnp.bfloat16), late[...], other[...])):
        total = total + jnp.dot(
            weight[place][:, : part.shape[0]], part, preferred_element_type=jnp.float32
        )
    out[...] = total.astype(jnp.bfloat16)


def combine(mixed, weight, blocks, late, other):
    return pl.pallas_call(
        combine_kernel,
        in_specs=[NEAR] * (4 + len(blocks)),
        out_specs=NEAR,
        out_shape=jax.ShapeDtypeStruct(mixed.shape, jnp.bfloat16),
        compiler_params=pltpu.CompilerParams(vmem_limit_bytes=(8 + len(blocks)) * MIB),
        name="combine",
    )(close(mixed), weight, late, other, *blocks)


def shards(
    resid, queries, keys, values, segment_ids, norm_gain, routes, route_gates, w_gate, w_up, w_down
):
    count = lax.axis_size("expert")
    own = lax.axis_index("expert")
    shard_count = count // E_WIN
    odd = own % 2

    next_chip = [(i, i + 2) for i in range(count - 2) if i % 4 != 3]
    crossing = [(i, i + 1) for i in range(0, count, 2)]
    crossing += [(i, i + 3) for i in range(1, count - 3, 2)]
    passing = [(i, i - 1) for i in range(2, count, 4)]

    def swapped(block, mask):
        return lax.ppermute(block, "expert", [(i, i ^ mask) for i in range(count)])

    seg_own = segment_ids.reshape(1, -1)
    beyond = 2 * WIN_DEV + 2
    delta_list = [0 * own, 0 * own + 2, 3 - 2 * odd, 1 + 2 * odd]
    my_expert = own // shard_count
    relayed = (own % 4 == 1).astype(jnp.int32)
    scalars = jnp.stack(
        [jnp.where(own >= delta, delta, beyond) for delta in delta_list] + [my_expert, relayed]
    ).astype(jnp.int32)

    key_block = bundle(keys, seg_own)
    key_cross = lax.ppermute(key_block, "expert", crossing)
    value_cross = lax.ppermute(values, "expert", crossing)
    key_next = lax.ppermute(key_block, "expert", next_chip)
    value_next = lax.ppermute(values, "expert", next_chip)
    key_passed = lax.ppermute(key_cross, "expert", passing)
    value_passed = lax.ppermute(value_cross, "expert", passing)
    mine = bring(
        [
            queries, keys, values, seg_own, resid, norm_gain.reshape(1, -1), routes.T,
            route_gates.T,
        ],
        scalars,
    )
    gate_held = fetch(w_gate, scalars)
    key_two = choose(scalars, key_passed, key_next)
    key_two, gate_held, mine = lax.optimization_barrier((key_two, gate_held, mine))
    key_mirror = swapped(key_two, 1)
    value_two = choose(scalars, value_passed, value_next)
    value_mirror = swapped(value_two, 1)

    queries, keys, values, seg_own, resid, gain, routes_held, gates_held = mine
    mixed, early, rest, send, weight = attention(
        scalars,
        queries,
        [keys, values, key_two, value_two, key_cross, value_cross, key_mirror, value_mirror],
        seg_own, resid, gain, routes_held, gates_held,
    )
    up_held, down_held = fetch(w_up, weight), fetch(w_down, weight)
    partner = [(i, (i + shard_count) % count) for i in range(count)]
    masks = list(range(2, shard_count, 2))[::-1]
    got = lax.ppermute(send, "expert", partner)

    def spread(block):
        return [block] + [swapped(block, mask) for mask in masks]

    def both_cores(blocks):
        local = pile(blocks)
        return local, swapped(local, 1)

    def summed(parts):
        return add_split(parts[0], swapped(parts[1], 1), 1 + len(masks))

    def scattered(blocks):
        moved = [swapped(block, mask) for block, mask in zip(blocks[1:], masks)]
        return [blocks[0]] + moved[::-1]

    early_blocks = spread(early)
    got, early_blocks, up_held, down_held = lax.optimization_barrier(
        (got, early_blocks, up_held, down_held)
    )
    held = [gate_held, up_held, down_held]
    early_parts = experts(*both_cores(early_blocks), *held)
    late_blocks = spread(join(got, rest))
    late_blocks, early_parts = lax.optimization_barrier((late_blocks, early_parts))
    late_rows = both_cores(late_blocks)
    early_blocks = summed(early_parts)
    late_rows, early_blocks = lax.optimization_barrier((late_rows, early_blocks))
    early_blocks = scattered(early_blocks)
    late_parts = experts(*late_rows, *held)
    late_parts, early_blocks = lax.optimization_barrier((late_parts, early_blocks))
    late_blocks = summed(late_parts)
    late, back = total_of(scattered(late_blocks))
    other = lax.ppermute(back, "expert", partner)
    return combine(mixed, weight, early_blocks, late, other)


def solution(mesh):
    placed = (
        P(("groups", "expert"), None),
        P(("groups", "expert"), None),
        P(("groups", "expert"), None),
        P(("groups", "expert"), None),
        P(("groups", "expert")),
        P(),
        P(("groups", "expert"), None),
        P(("groups", "expert"), None),
        P(None, "expert"),
        P(None, "expert"),
        P("expert", None),
    )
    return jax.shard_map(
        shards, mesh=mesh, in_specs=placed, out_specs=P(("groups", "expert"), None), check_vma=False
    )
```

```python
import functools

import jax
import jax.numpy as jnp
from jax import lax
from jax.experimental import pallas as pl
from jax.experimental.pallas import tpu as pltpu
from jax.sharding import PartitionSpec as P

HEAD_DIM = 128
E_WIN = 2
WIN_DEV = 3
CAP = 20
SPARE = 16
HEADS_STEP = 8
MASKED = -1e30
MIB = 1024 * 1024


def far(x):
    return pltpu.with_memory_space_constraint(x, pltpu.HBM)


def close(x):
    return pltpu.with_memory_space_constraint(x, pltpu.VMEM)


NEAR = pl.BlockSpec(memory_space=pltpu.VMEM)


def bundle_kernel(keys, segs, out):
    rows, width = keys.shape
    out[:, :width] = keys[...]
    out[:, width:] = jnp.zeros((rows, HEAD_DIM), keys.dtype)
    out[:SPARE, width : width + rows] = jnp.broadcast_to(
        segs[...].astype(jnp.float32), (SPARE, rows)
    ).astype(keys.dtype)


def bundle(keys, segs):
    rows, width = keys.shape
    return pl.pallas_call(
        bundle_kernel,
        in_specs=[NEAR, NEAR],
        out_specs=NEAR,
        out_shape=jax.ShapeDtypeStruct((rows, width + HEAD_DIM), keys.dtype),
        cost_estimate=pl.CostEstimate(
            flops=0, bytes_accessed=4 * rows * width, transcendentals=0
        ),
        compiler_params=pltpu.CompilerParams(vmem_limit_bytes=6 * MIB),
        name="bundle",
    )(far(keys), far(segs))


def choose_kernel(flags, first, second, out):
    @pl.when(flags[5] == 1)
    def _():
        out[...] = first[...]

    @pl.when(flags[5] != 1)
    def _():
        out[...] = second[...]


def choose(flags, first, second):
    return pl.pallas_call(
        choose_kernel,
        in_specs=[pl.BlockSpec(memory_space=pltpu.SMEM), NEAR, NEAR],
        out_specs=NEAR,
        out_shape=jax.ShapeDtypeStruct(first.shape, first.dtype),
        compiler_params=pltpu.CompilerParams(vmem_limit_bytes=6 * MIB),
        name="choose",
    )(flags, close(first), close(second))


def attention_kernel(
    deltas, q, k0, v0, k1, v1, k2, v2, k3, v3, seg0, resid, gain, routes, gates,
    mixed_out, keep_out, send_out, weight_out,
):
    rows, model = q.shape
    keys = (WIN_DEV + 1) * rows
    width = HEADS_STEP * HEAD_DIM

    seg_own = seg0[...].astype(jnp.float32)
    seg_row = jnp.concatenate(
        [seg_own]
        + [block[:SPARE, model:][0:1, :rows].astype(jnp.float32) for block in (k1, k2, k3)],
        axis=1,
    )
    eye = lax.broadcasted_iota(jnp.int32, (rows, rows), 0) == lax.broadcasted_iota(
        jnp.int32, (rows, rows), 1
    )
    seg_col = jnp.sum(jnp.where(eye, seg_own, 0.0), axis=1, keepdims=True)
    lane = lax.broadcasted_iota(jnp.int32, (rows, keys), 1)
    sub = lax.broadcasted_iota(jnp.int32, (rows, keys), 0)
    block = lane // rows
    back = jnp.where(
        block == 0,
        deltas[0],
        jnp.where(block == 1, deltas[1], jnp.where(block == 2, deltas[2], deltas[3])),
    )
    distance = sub - (lane - block * rows) + back * rows
    allowed = (distance >= 0) & (distance <= WIN_DEV * rows) & (seg_col == seg_row)
    bias = jnp.where(allowed, 0.0, MASKED)
    scale = 1.0 / HEAD_DIM**0.5
    heads = [slice(head * HEAD_DIM, (head + 1) * HEAD_DIM) for head in range(HEADS_STEP)]

    @pl.loop(0, model // width)
    def _(step):
        at = pl.ds(pl.multiple_of(step * width, width), width)
        query = q[:, at]
        key = jnp.concatenate([k0[:, at], k1[:, at], k2[:, at], k3[:, at]], axis=0)
        value = jnp.concatenate([v0[:, at], v1[:, at], v2[:, at], v3[:, at]], axis=0)
        scores = jnp.stack(
            [
                lax.dot_general(
                    query[:, cols], key[:, cols], (((1,), (1,)), ((), ())),
                    preferred_element_type=jnp.float32,
                )
                for cols in heads
            ]
        )
        scores = scores * scale + bias[None]
        expo = jnp.exp(scores - jnp.max(scores, axis=2, keepdims=True))
        denom = jnp.sum(expo, axis=2, keepdims=True)
        probs = expo.astype(jnp.bfloat16)
        outs = [
            jnp.dot(probs[head], value[:, cols], preferred_element_type=jnp.float32)
            / denom[head]
            for head, cols in enumerate(heads)
        ]
        mixed_out[:, at] = resid[:, at].astype(jnp.float32) + jnp.concatenate(outs, axis=1)

    mixed = mixed_out[...]
    normed = (
        mixed * lax.rsqrt(jnp.mean(mixed * mixed, axis=1, keepdims=True) + 1e-05) * gain[...]
    ).astype(jnp.bfloat16)
    across = lax.broadcasted_iota(jnp.int32, (rows, rows), 1)
    down = lax.broadcasted_iota(jnp.int32, (rows, rows), 0)
    upper = jnp.where(down < across, 1.0, 0.0).astype(jnp.bfloat16)
    eye = jnp.where(down == across, 1.0, 0.0).astype(jnp.bfloat16)
    slot = lax.broadcasted_iota(jnp.int32, (32, rows), 0)

    def picks(expert):
        hit = routes[...] == expert
        member = jnp.max(jnp.where(hit, 1.0, 0.0), axis=0, keepdims=True)
        weight = jnp.sum(
            jnp.where(hit, gates[...].astype(jnp.float32), 0.0), axis=0, keepdims=True
        )
        rank = jnp.dot(
            jnp.broadcast_to(member, (8, rows)).astype(jnp.bfloat16),
            upper,
            preferred_element_type=jnp.float32,
        )[0:1].astype(jnp.int32)
        return member > 0.5, weight, rank

    def spread(pick, weight):
        return lax.dot_general(
            eye,
            jnp.where(pick, weight, 0.0).astype(jnp.bfloat16),
            (((1,), (1,)), ((), ())),
            preferred_element_type=jnp.float32,
        ).astype(jnp.bfloat16)

    def packed(pick):
        return jnp.dot(
            jnp.where(pick, 1.0, 0.0).astype(jnp.bfloat16),
            normed,
            preferred_element_type=jnp.float32,
        ).astype(jnp.bfloat16)

    for place, out in ((0, keep_out), (1, send_out)):
        member, weight, rank = picks(deltas[4] if place == 0 else 1 - deltas[4])
        pick = (slot == rank) & member
        out[...] = packed(pick)[:CAP]
        weight_out[place] = spread(pick, weight)


def attention(deltas, q, pairs, seg_own, resid, gain, routes, gates):
    rows, width = q.shape
    return pl.pallas_call(
        attention_kernel,
        in_specs=[pl.BlockSpec(memory_space=pltpu.SMEM)] + [NEAR] * (6 + len(pairs)),
        out_specs=[NEAR] * 4,
        out_shape=[
            pltpu.VMEM((rows, width), jnp.float32),
            jax.ShapeDtypeStruct((CAP, width), jnp.bfloat16),
            jax.ShapeDtypeStruct((CAP, width), jnp.bfloat16),
            jax.ShapeDtypeStruct((E_WIN, rows, 32), jnp.bfloat16),
        ],
        compiler_params=pltpu.CompilerParams(vmem_limit_bytes=14 * MIB),
        cost_estimate=pl.CostEstimate(
            flops=4 * rows * 4 * rows * width, bytes_accessed=8 * rows * width * 4,
            transcendentals=rows * 4 * rows * (width // HEAD_DIM),
        ),
        name="attention",
    )(
        deltas, close(q), close(pairs[0]), close(pairs[1]), *pairs[2:], close(seg_own),
        close(resid), close(gain), close(routes), close(gates),
    )


def bring_kernel(count, *refs):
    sources, held, sems = refs[:count], refs[count + 1 : 2 * count + 1], refs[-1]
    copies = [
        pltpu.make_async_copy(source, target, sems.at[at])
        for at, (source, target) in enumerate(zip(sources, held))
    ]
    for copy in copies:
        copy.start()
    for copy in copies:
        copy.wait()


def bring(arrays, after):
    count = len(arrays)
    anywhere = pl.BlockSpec(memory_space=pl.ANY)
    return pl.pallas_call(
        functools.partial(bring_kernel, count),
        in_specs=[anywhere] * (count + 1),
        out_specs=[NEAR] * count,
        out_shape=[pltpu.VMEM(x.shape, x.dtype) for x in arrays],
        scratch_shapes=[pltpu.SemaphoreType.DMA((count,))],
        compiler_params=pltpu.CompilerParams(vmem_limit_bytes=2 * MIB),
        cost_estimate=pl.CostEstimate(
            flops=0, bytes_accessed=4 * sum(x.size for x in arrays), transcendentals=0
        ),
        name="bring",
    )(*[far(x) for x in arrays], after)


def fetch_kernel(parts, source, after, held, sems):
    depth = source.shape[0] // parts
    copies = []
    for part in range(parts):
        at = pl.ds(part * depth, depth)
        copies.append(pltpu.make_async_copy(source.at[at], held.at[at], sems.at[part]))
    for copy in copies:
        copy.start()
    for copy in copies:
        copy.wait()


def fetch(weights, after):
    parts = 4
    anywhere = pl.BlockSpec(memory_space=pl.ANY)
    return pl.pallas_call(
        functools.partial(fetch_kernel, parts),
        in_specs=[anywhere, anywhere],
        out_specs=NEAR,
        out_shape=pltpu.VMEM(weights.shape, weights.dtype),
        scratch_shapes=[pltpu.SemaphoreType.DMA((parts,))],
        compiler_params=pltpu.CompilerParams(vmem_limit_bytes=2 * MIB),
        cost_estimate=pl.CostEstimate(
            flops=0, bytes_accessed=4 * weights.size, transcendentals=0
        ),
        name="fetch",
    )(far(weights), after)


def experts_kernel(local, remote, w_gate, w_up, w_down, local_out, remote_out, x, hidden):
    width, units = w_gate.shape
    tile = min(512, units)
    rows = local.shape[0]
    x[:rows] = local[...]
    x[rows:] = remote[...]

    @pl.loop(0, units // tile)
    def _(part):
        at = pl.ds(pl.multiple_of(part * tile, tile), tile)
        gate = jnp.dot(x[...], w_gate[:, at], preferred_element_type=jnp.float32)
        up = jnp.dot(x[...], w_up[:, at], preferred_element_type=jnp.float32)
        hidden[:, at] = (jax.nn.silu(gate) * up).astype(jnp.bfloat16)

    @pl.loop(0, width // 1024)
    def _(part):
        at = pl.ds(pl.multiple_of(part * 1024, 1024), 1024)
        out = jnp.dot(hidden[...], w_down[:, at], preferred_element_type=jnp.float32)
        local_out[:, at] = out[:rows].astype(jnp.bfloat16)
        remote_out[:, at] = out[rows:].astype(jnp.bfloat16)


def experts(local, remote, w_gate, w_up, w_down):
    rows, width = local.shape
    units = w_gate.shape[1]
    return pl.pallas_call(
        experts_kernel,
        in_specs=[NEAR] * 5,
        out_specs=[NEAR] * 2,
        out_shape=[jax.ShapeDtypeStruct((rows, width), jnp.bfloat16)] * 2,
        scratch_shapes=[
            pltpu.VMEM((2 * rows, width), jnp.bfloat16),
            pltpu.VMEM((2 * rows, units), jnp.bfloat16),
        ],
        compiler_params=pltpu.CompilerParams(vmem_limit_bytes=20 * MIB),
        cost_estimate=pl.CostEstimate(
            flops=12 * rows * width * units,
            bytes_accessed=8 * rows * width,
            transcendentals=2 * rows * units,
        ),
        name="experts",
    )(local, remote, close(w_gate), close(w_up), close(w_down))


def pile_kernel(*refs):
    blocks, out = refs[:-1], refs[-1]
    out[...] = jnp.concatenate(
        [block[...].astype(jnp.float32) for block in blocks], axis=0
    ).astype(out.dtype)


def pile(blocks):
    rows, width = blocks[0].shape
    return pl.pallas_call(
        pile_kernel,
        in_specs=[NEAR] * len(blocks),
        out_specs=NEAR,
        out_shape=jax.ShapeDtypeStruct((len(blocks) * rows, width), blocks[0].dtype),
        compiler_params=pltpu.CompilerParams(vmem_limit_bytes=(4 + len(blocks)) * MIB),
        name="pile",
    )(*blocks)


def add_kernel(first, second, *outs):
    rows = outs[0].shape[0]
    total = first[...].astype(jnp.float32) + second[...].astype(jnp.float32)
    for at, out in enumerate(outs):
        out[...] = total[at * rows : (at + 1) * rows].astype(out.dtype)


def add_split(first, second, blocks):
    rows, width = first.shape
    each = rows // blocks
    return pl.pallas_call(
        add_kernel,
        in_specs=[NEAR, NEAR],
        out_specs=[NEAR] * blocks,
        out_shape=[jax.ShapeDtypeStruct((each, width), first.dtype)] * blocks,
        compiler_params=pltpu.CompilerParams(vmem_limit_bytes=(6 + blocks) * MIB),
        name="add_split",
    )(first, second)


def total(blocks):
    result = blocks[0][...].astype(jnp.float32)
    for block in blocks[1:]:
        result = result + block[...].astype(jnp.float32)
    return result.astype(jnp.bfloat16)


def total_kernel(*refs):
    refs[-1][...] = total(refs[:-1])


def total_of(blocks):
    return pl.pallas_call(
        total_kernel,
        in_specs=[NEAR] * len(blocks),
        out_specs=NEAR,
        out_shape=jax.ShapeDtypeStruct(blocks[0].shape, blocks[0].dtype),
        compiler_params=pltpu.CompilerParams(vmem_limit_bytes=(4 + len(blocks)) * MIB),
        name="total",
    )(*blocks)


def combine_kernel(place, base, weight, *refs):
    blocks, out = refs[:-1], refs[-1]
    part = jnp.dot(
        weight[place][:, :CAP], total(blocks), preferred_element_type=jnp.float32
    )
    out[...] = (base[...] + part).astype(out.dtype)


def combine(place, base, weight, blocks, result):
    return pl.pallas_call(
        functools.partial(combine_kernel, place),
        in_specs=[NEAR] * (2 + len(blocks)),
        out_specs=NEAR,
        out_shape=result,
        compiler_params=pltpu.CompilerParams(vmem_limit_bytes=(8 + len(blocks)) * MIB),
        name="combine",
    )(close(base), weight, *blocks)


def shards(
    resid, queries, keys, values, segment_ids, norm_gain, routes, route_gates, w_gate, w_up, w_down
):
    count = lax.axis_size("expert")
    own = lax.axis_index("expert")
    shard_count = count // E_WIN
    odd = own % 2

    next_chip = [(i, i + 2) for i in range(count - 2) if i % 4 != 3]
    crossing = [(i, i + 1) for i in range(0, count, 2)]
    crossing += [(i, i + 3) for i in range(1, count - 3, 2)]
    passing = [(i, i - 1) for i in range(2, count, 4)]

    def swapped(block, mask):
        return lax.ppermute(block, "expert", [(i, i ^ mask) for i in range(count)])

    seg_own = segment_ids.reshape(1, -1)
    beyond = 2 * WIN_DEV + 2
    delta_list = [0 * own, 0 * own + 2, 3 - 2 * odd, 1 + 2 * odd]
    my_expert = own // shard_count
    relayed = (own % 4 == 1).astype(jnp.int32)
    scalars = jnp.stack(
        [jnp.where(own >= delta, delta, beyond) for delta in delta_list] + [my_expert, relayed]
    ).astype(jnp.int32)

    key_block = bundle(keys, seg_own)
    key_cross = lax.ppermute(key_block, "expert", crossing)
    value_cross = lax.ppermute(values, "expert", crossing)
    key_next = lax.ppermute(key_block, "expert", next_chip)
    value_next = lax.ppermute(values, "expert", next_chip)
    key_passed = lax.ppermute(key_cross, "expert", passing)
    value_passed = lax.ppermute(value_cross, "expert", passing)
    mine = bring(
        [
            queries, keys, values, seg_own, resid, norm_gain.reshape(1, -1), routes.T,
            route_gates.T,
        ],
        scalars,
    )
    gate_held = fetch(w_gate, scalars)
    key_two = choose(scalars, key_passed, key_next)
    key_two, gate_held, mine = lax.optimization_barrier((key_two, gate_held, mine))
    key_mirror = swapped(key_two, 1)
    value_two = choose(scalars, value_passed, value_next)
    value_mirror = swapped(value_two, 1)

    queries, keys, values, seg_own, resid, gain, routes_held, gates_held = mine
    mixed, keep, send, weight = attention(
        scalars,
        queries,
        [keys, values, key_two, value_two, key_cross, value_cross, key_mirror, value_mirror],
        seg_own, resid, gain, routes_held, gates_held,
    )
    up_held, down_held = fetch(w_up, weight), fetch(w_down, weight)
    partner = [(i, (i + shard_count) % count) for i in range(count)]
    masks = list(range(2, shard_count, 2))[::-1]
    got = lax.ppermute(send, "expert", partner)

    def spread(block):
        return [block] + [swapped(block, mask) for mask in masks]

    def both_cores(blocks):
        local = pile(blocks)
        return local, swapped(local, 1)

    def summed(parts):
        return add_split(parts[0], swapped(parts[1], 1), 1 + len(masks))

    def scattered(blocks):
        moved = [swapped(block, mask) for block, mask in zip(blocks[1:], masks)]
        return [blocks[0]] + moved[::-1]

    early_blocks = spread(keep)
    early_blocks, got, up_held, down_held = lax.optimization_barrier(
        (early_blocks, got, up_held, down_held)
    )
    held = [gate_held, up_held, down_held]
    early_parts = experts(*both_cores(early_blocks), *held)
    late_blocks = spread(got)
    late_blocks, early_parts = lax.optimization_barrier((late_blocks, early_parts))
    late_blocks = summed(experts(*both_cores(late_blocks), *held))
    early_blocks = summed(early_parts)
    late_blocks, early_blocks = lax.optimization_barrier((late_blocks, early_blocks))
    late_blocks = scattered(late_blocks)
    late_blocks[:-1], early_blocks = lax.optimization_barrier((late_blocks[:-1], early_blocks))
    early_blocks = scattered(early_blocks)
    back = total_of(late_blocks)
    other = lax.ppermute(back, "expert", partner)
    base = combine(0, mixed, weight, early_blocks, pltpu.VMEM(mixed.shape, jnp.float32))
    return combine(
        1, base, weight, [other], jax.ShapeDtypeStruct(mixed.shape, jnp.bfloat16)
    )


def solution(mesh):
    placed = (
        P(("groups", "expert"), None),
        P(("groups", "expert"), None),
        P(("groups", "expert"), None),
        P(("groups", "expert"), None),
        P(("groups", "expert")),
        P(),
        P(("groups", "expert"), None),
        P(("groups", "expert"), None),
        P(None, "expert"),
        P(None, "expert"),
        P("expert", None),
    )
    return jax.shard_map(
        shards, mesh=mesh, in_specs=placed, out_specs=P(("groups", "expert"), None), check_vma=False
    )
```

```python
import functools

import jax
import jax.numpy as jnp
from jax import lax
from jax.experimental import pallas as pl
from jax.experimental.pallas import tpu as pltpu
from jax.sharding import PartitionSpec as P

HEAD_DIM = 128
E_WIN = 2
WIN_DEV = 3
CAP = 20
SPARE = 16
HEADS_STEP = 8
MASKED = -1e30
MIB = 1024 * 1024


def far(x):
    return pltpu.with_memory_space_constraint(x, pltpu.HBM)


def close(x):
    return pltpu.with_memory_space_constraint(x, pltpu.VMEM)


NEAR = pl.BlockSpec(memory_space=pltpu.VMEM)


def bundle_kernel(keys, segs, out):
    rows, width = keys.shape
    out[:, :width] = keys[...]
    out[:, width:] = jnp.zeros((rows, HEAD_DIM), keys.dtype)
    out[:SPARE, width : width + rows] = jnp.broadcast_to(
        segs[...].astype(jnp.float32), (SPARE, rows)
    ).astype(keys.dtype)


def bundle(keys, segs):
    rows, width = keys.shape
    return pl.pallas_call(
        bundle_kernel,
        in_specs=[NEAR, NEAR],
        out_specs=NEAR,
        out_shape=jax.ShapeDtypeStruct((rows, width + HEAD_DIM), keys.dtype),
        cost_estimate=pl.CostEstimate(
            flops=0, bytes_accessed=4 * rows * width, transcendentals=0
        ),
        compiler_params=pltpu.CompilerParams(vmem_limit_bytes=6 * MIB),
        name="bundle",
    )(far(keys), far(segs))


def choose_kernel(flags, first, second, out):
    @pl.when(flags[5] == 1)
    def _():
        out[...] = first[...]

    @pl.when(flags[5] != 1)
    def _():
        out[...] = second[...]


def choose(flags, first, second):
    return pl.pallas_call(
        choose_kernel,
        in_specs=[pl.BlockSpec(memory_space=pltpu.SMEM), NEAR, NEAR],
        out_specs=NEAR,
        out_shape=jax.ShapeDtypeStruct(first.shape, first.dtype),
        compiler_params=pltpu.CompilerParams(vmem_limit_bytes=6 * MIB),
        name="choose",
    )(flags, close(first), close(second))


def attention_kernel(
    deltas, q, k0, v0, k1, v1, k2, v2, k3, v3, seg0, resid, gain, routes, gates,
    mixed_out, keep_out, send_out, weight_out,
):
    rows, model = q.shape
    keys = (WIN_DEV + 1) * rows
    width = HEADS_STEP * HEAD_DIM

    seg_own = seg0[...].astype(jnp.float32)
    seg_row = jnp.concatenate(
        [seg_own]
        + [block[:SPARE, model:][0:1, :rows].astype(jnp.float32) for block in (k1, k2, k3)],
        axis=1,
    )
    eye = lax.broadcasted_iota(jnp.int32, (rows, rows), 0) == lax.broadcasted_iota(
        jnp.int32, (rows, rows), 1
    )
    seg_col = jnp.sum(jnp.where(eye, seg_own, 0.0), axis=1, keepdims=True)
    lane = lax.broadcasted_iota(jnp.int32, (rows, keys), 1)
    sub = lax.broadcasted_iota(jnp.int32, (rows, keys), 0)
    block = lane // rows
    back = jnp.where(
        block == 0,
        deltas[0],
        jnp.where(block == 1, deltas[1], jnp.where(block == 2, deltas[2], deltas[3])),
    )
    distance = sub - (lane - block * rows) + back * rows
    allowed = (distance >= 0) & (distance <= WIN_DEV * rows) & (seg_col == seg_row)
    bias = jnp.where(allowed, 0.0, MASKED)
    scale = 1.0 / HEAD_DIM**0.5
    heads = [slice(head * HEAD_DIM, (head + 1) * HEAD_DIM) for head in range(HEADS_STEP)]

    @pl.loop(0, model // width)
    def _(step):
        at = pl.ds(pl.multiple_of(step * width, width), width)
        query = q[:, at]
        key = jnp.concatenate([k0[:, at], k1[:, at], k2[:, at], k3[:, at]], axis=0)
        value = jnp.concatenate([v0[:, at], v1[:, at], v2[:, at], v3[:, at]], axis=0)
        scores = jnp.stack(
            [
                lax.dot_general(
                    query[:, cols], key[:, cols], (((1,), (1,)), ((), ())),
                    preferred_element_type=jnp.float32,
                )
                for cols in heads
            ]
        )
        scores = scores * scale + bias[None]
        expo = jnp.exp(scores - jnp.max(scores, axis=2, keepdims=True))
        denom = jnp.sum(expo, axis=2, keepdims=True)
        probs = expo.astype(jnp.bfloat16)
        outs = [
            jnp.dot(probs[head], value[:, cols], preferred_element_type=jnp.float32)
            / denom[head]
            for head, cols in enumerate(heads)
        ]
        mixed_out[:, at] = resid[:, at].astype(jnp.float32) + jnp.concatenate(outs, axis=1)

    mixed = mixed_out[...]
    normed = (
        mixed * lax.rsqrt(jnp.mean(mixed * mixed, axis=1, keepdims=True) + 1e-05) * gain[...]
    ).astype(jnp.bfloat16)
    across = lax.broadcasted_iota(jnp.int32, (rows, rows), 1)
    down = lax.broadcasted_iota(jnp.int32, (rows, rows), 0)
    upper = jnp.where(down < across, 1.0, 0.0).astype(jnp.bfloat16)
    eye = jnp.where(down == across, 1.0, 0.0).astype(jnp.bfloat16)
    slot = lax.broadcasted_iota(jnp.int32, (32, rows), 0)

    def picks(expert):
        hit = routes[...] == expert
        member = jnp.max(jnp.where(hit, 1.0, 0.0), axis=0, keepdims=True)
        weight = jnp.sum(
            jnp.where(hit, gates[...].astype(jnp.float32), 0.0), axis=0, keepdims=True
        )
        rank = jnp.dot(
            jnp.broadcast_to(member, (8, rows)).astype(jnp.bfloat16),
            upper,
            preferred_element_type=jnp.float32,
        )[0:1].astype(jnp.int32)
        return member > 0.5, weight, rank

    def spread(pick, weight):
        return lax.dot_general(
            eye,
            jnp.where(pick, weight, 0.0).astype(jnp.bfloat16),
            (((1,), (1,)), ((), ())),
            preferred_element_type=jnp.float32,
        ).astype(jnp.bfloat16)

    def packed(pick):
        return jnp.dot(
            jnp.where(pick, 1.0, 0.0).astype(jnp.bfloat16),
            normed,
            preferred_element_type=jnp.float32,
        ).astype(jnp.bfloat16)

    for place, out in ((0, keep_out), (1, send_out)):
        member, weight, rank = picks(deltas[4] if place == 0 else 1 - deltas[4])
        pick = (slot == rank) & member
        out[...] = packed(pick)[:CAP]
        weight_out[place] = spread(pick, weight)


def attention(deltas, q, pairs, seg_own, resid, gain, routes, gates):
    rows, width = q.shape
    return pl.pallas_call(
        attention_kernel,
        in_specs=[pl.BlockSpec(memory_space=pltpu.SMEM)] + [NEAR] * (6 + len(pairs)),
        out_specs=[NEAR] * 4,
        out_shape=[
            pltpu.VMEM((rows, width), jnp.float32),
            jax.ShapeDtypeStruct((CAP, width), jnp.bfloat16),
            jax.ShapeDtypeStruct((CAP, width), jnp.bfloat16),
            jax.ShapeDtypeStruct((E_WIN, rows, 32), jnp.bfloat16),
        ],
        compiler_params=pltpu.CompilerParams(vmem_limit_bytes=14 * MIB),
        cost_estimate=pl.CostEstimate(
            flops=4 * rows * 4 * rows * width, bytes_accessed=8 * rows * width * 4,
            transcendentals=rows * 4 * rows * (width // HEAD_DIM),
        ),
        name="attention",
    )(
        deltas, close(q), close(pairs[0]), close(pairs[1]), *pairs[2:], close(seg_own),
        close(resid), close(gain), close(routes), close(gates),
    )


def bring_kernel(count, *refs):
    sources, held, sems = refs[:count], refs[count + 1 : 2 * count + 1], refs[-1]
    copies = [
        pltpu.make_async_copy(source, target, sems.at[at])
        for at, (source, target) in enumerate(zip(sources, held))
    ]
    for copy in copies:
        copy.start()
    for copy in copies:
        copy.wait()


def bring(arrays, after):
    count = len(arrays)
    anywhere = pl.BlockSpec(memory_space=pl.ANY)
    return pl.pallas_call(
        functools.partial(bring_kernel, count),
        in_specs=[anywhere] * (count + 1),
        out_specs=[NEAR] * count,
        out_shape=[pltpu.VMEM(x.shape, x.dtype) for x in arrays],
        scratch_shapes=[pltpu.SemaphoreType.DMA((count,))],
        compiler_params=pltpu.CompilerParams(vmem_limit_bytes=2 * MIB),
        cost_estimate=pl.CostEstimate(
            flops=0, bytes_accessed=4 * sum(x.size for x in arrays), transcendentals=0
        ),
        name="bring",
    )(*[far(x) for x in arrays], after)


def fetch_kernel(parts, source, after, held, sems):
    depth = source.shape[0] // parts
    copies = []
    for part in range(parts):
        at = pl.ds(part * depth, depth)
        copies.append(pltpu.make_async_copy(source.at[at], held.at[at], sems.at[part]))
    for copy in copies:
        copy.start()
    for copy in copies:
        copy.wait()


def fetch(weights, after):
    parts = 4
    anywhere = pl.BlockSpec(memory_space=pl.ANY)
    return pl.pallas_call(
        functools.partial(fetch_kernel, parts),
        in_specs=[anywhere, anywhere],
        out_specs=NEAR,
        out_shape=pltpu.VMEM(weights.shape, weights.dtype),
        scratch_shapes=[pltpu.SemaphoreType.DMA((parts,))],
        compiler_params=pltpu.CompilerParams(vmem_limit_bytes=2 * MIB),
        cost_estimate=pl.CostEstimate(
            flops=0, bytes_accessed=4 * weights.size, transcendentals=0
        ),
        name="fetch",
    )(far(weights), after)


def experts_kernel(local, remote, w_gate, w_up, w_down, local_out, remote_out, x, hidden):
    width, units = w_gate.shape
    tile = min(512, units)
    rows = local.shape[0]
    x[:rows] = local[...]
    x[rows:] = remote[...]

    @pl.loop(0, units // tile)
    def _(part):
        at = pl.ds(pl.multiple_of(part * tile, tile), tile)
        gate = jnp.dot(x[...], w_gate[:, at], preferred_element_type=jnp.float32)
        up = jnp.dot(x[...], w_up[:, at], preferred_element_type=jnp.float32)
        hidden[:, at] = (jax.nn.silu(gate) * up).astype(jnp.bfloat16)

    @pl.loop(0, width // 1024)
    def _(part):
        at = pl.ds(pl.multiple_of(part * 1024, 1024), 1024)
        out = jnp.dot(hidden[...], w_down[:, at], preferred_element_type=jnp.float32)
        local_out[:, at] = out[:rows].astype(jnp.bfloat16)
        remote_out[:, at] = out[rows:].astype(jnp.bfloat16)


def experts(local, remote, w_gate, w_up, w_down):
    rows, width = local.shape
    units = w_gate.shape[1]
    return pl.pallas_call(
        experts_kernel,
        in_specs=[NEAR] * 5,
        out_specs=[NEAR] * 2,
        out_shape=[jax.ShapeDtypeStruct((rows, width), jnp.bfloat16)] * 2,
        scratch_shapes=[
            pltpu.VMEM((2 * rows, width), jnp.bfloat16),
            pltpu.VMEM((2 * rows, units), jnp.bfloat16),
        ],
        compiler_params=pltpu.CompilerParams(vmem_limit_bytes=20 * MIB),
        cost_estimate=pl.CostEstimate(
            flops=12 * rows * width * units,
            bytes_accessed=8 * rows * width,
            transcendentals=2 * rows * units,
        ),
        name="experts",
    )(local, remote, close(w_gate), close(w_up), close(w_down))


def pile_kernel(*refs):
    blocks, out = refs[:-1], refs[-1]
    out[...] = jnp.concatenate(
        [block[...].astype(jnp.float32) for block in blocks], axis=0
    ).astype(out.dtype)


def pile(blocks):
    rows, width = blocks[0].shape
    return pl.pallas_call(
        pile_kernel,
        in_specs=[NEAR] * len(blocks),
        out_specs=NEAR,
        out_shape=jax.ShapeDtypeStruct((len(blocks) * rows, width), blocks[0].dtype),
        compiler_params=pltpu.CompilerParams(vmem_limit_bytes=(4 + len(blocks)) * MIB),
        name="pile",
    )(*blocks)


def add_kernel(first, second, *outs):
    rows = outs[0].shape[0]
    total = first[...].astype(jnp.float32) + second[...].astype(jnp.float32)
    for at, out in enumerate(outs):
        out[...] = total[at * rows : (at + 1) * rows].astype(out.dtype)


def add_split(first, second, blocks):
    rows, width = first.shape
    each = rows // blocks
    return pl.pallas_call(
        add_kernel,
        in_specs=[NEAR, NEAR],
        out_specs=[NEAR] * blocks,
        out_shape=[jax.ShapeDtypeStruct((each, width), first.dtype)] * blocks,
        compiler_params=pltpu.CompilerParams(vmem_limit_bytes=(6 + blocks) * MIB),
        name="add_split",
    )(first, second)


def total(blocks):
    result = blocks[0][...].astype(jnp.float32)
    for block in blocks[1:]:
        result = result + block[...].astype(jnp.float32)
    return result.astype(jnp.bfloat16)


def total_kernel(*refs):
    refs[-1][...] = total(refs[:-1])


def total_of(blocks):
    return pl.pallas_call(
        total_kernel,
        in_specs=[NEAR] * len(blocks),
        out_specs=NEAR,
        out_shape=jax.ShapeDtypeStruct(blocks[0].shape, blocks[0].dtype),
        compiler_params=pltpu.CompilerParams(vmem_limit_bytes=(4 + len(blocks)) * MIB),
        name="total",
    )(*blocks)


def combine_kernel(place, base, weight, *refs):
    blocks, out = refs[:-1], refs[-1]
    part = jnp.dot(
        weight[place][:, :CAP], total(blocks), preferred_element_type=jnp.float32
    )
    out[...] = (base[...] + part).astype(out.dtype)


def combine(place, base, weight, blocks, result):
    return pl.pallas_call(
        functools.partial(combine_kernel, place),
        in_specs=[NEAR] * (2 + len(blocks)),
        out_specs=NEAR,
        out_shape=result,
        compiler_params=pltpu.CompilerParams(vmem_limit_bytes=(8 + len(blocks)) * MIB),
        name="combine",
    )(close(base), weight, *blocks)


def shards(
    resid, queries, keys, values, segment_ids, norm_gain, routes, route_gates, w_gate, w_up, w_down
):
    count = lax.axis_size("expert")
    own = lax.axis_index("expert")
    shard_count = count // E_WIN
    odd = own % 2

    next_chip = [(i, i + 2) for i in range(count - 2) if i % 4 < 2]
    crossing = [(i, i + 1) for i in range(0, count, 2)]
    crossing += [(i, i + 3) for i in range(1, count - 3, 2)]
    passing = [(i, i - 1) for i in range(2, count, 4)]
    passing += [(i, i + 1) for i in range(3, count - 1, 4)]

    def swapped(block, mask):
        return lax.ppermute(block, "expert", [(i, i ^ mask) for i in range(count)])

    seg_own = segment_ids.reshape(1, -1)
    beyond = 2 * WIN_DEV + 2
    delta_list = [0 * own, 0 * own + 2, 3 - 2 * odd, 1 + 2 * odd]
    my_expert = own // shard_count
    relayed = (own % 4 < 2).astype(jnp.int32)
    scalars = jnp.stack(
        [jnp.where(own >= delta, delta, beyond) for delta in delta_list] + [my_expert, relayed]
    ).astype(jnp.int32)

    key_block = bundle(keys, seg_own)
    key_next = lax.ppermute(key_block, "expert", next_chip)
    key_cross = lax.ppermute(key_block, "expert", crossing)
    value_cross = lax.ppermute(values, "expert", crossing)
    value_next = lax.ppermute(values, "expert", next_chip)
    key_passed = lax.ppermute(key_cross, "expert", passing)
    value_passed = lax.ppermute(value_cross, "expert", passing)
    mine = bring(
        [
            queries, keys, values, seg_own, resid, norm_gain.reshape(1, -1), routes.T,
            route_gates.T,
        ],
        scalars,
    )
    gate_held = fetch(w_gate, scalars)
    key_two = choose(scalars, key_passed, key_next)
    key_two, gate_held, mine = lax.optimization_barrier((key_two, gate_held, mine))
    key_mirror = swapped(key_two, 1)
    value_two = choose(scalars, value_passed, value_next)
    value_mirror = swapped(value_two, 1)

    queries, keys, values, seg_own, resid, gain, routes_held, gates_held = mine
    mixed, keep, send, weight = attention(
        scalars,
        queries,
        [keys, values, key_two, value_two, key_cross, value_cross, key_mirror, value_mirror],
        seg_own, resid, gain, routes_held, gates_held,
    )
    up_held, down_held = fetch(w_up, weight), fetch(w_down, weight)
    partner = [(i, (i + shard_count) % count) for i in range(count)]
    masks = list(range(2, shard_count, 2))[::-1]
    got = lax.ppermute(send, "expert", partner)

    def spread(block):
        return [block] + [swapped(block, mask) for mask in masks]

    def both_cores(blocks):
        local = pile(blocks)
        return local, swapped(local, 1)

    def summed(parts):
        return add_split(parts[0], swapped(parts[1], 1), 1 + len(masks))

    def scattered(blocks):
        moved = [swapped(block, mask) for block, mask in zip(blocks[1:], masks)]
        return [blocks[0]] + moved[::-1]

    early_blocks = spread(keep)
    early_blocks, got, up_held, down_held = lax.optimization_barrier(
        (early_blocks, got, up_held, down_held)
    )
    held = [gate_held, up_held, down_held]
    early_parts = experts(*both_cores(early_blocks), *held)
    late_blocks = spread(got)
    late_blocks, early_parts = lax.optimization_barrier((late_blocks, early_parts))
    late_blocks = summed(experts(*both_cores(late_blocks), *held))
    early_blocks = summed(early_parts)
    late_blocks, early_blocks = lax.optimization_barrier((late_blocks, early_blocks))
    late_blocks = scattered(late_blocks)
    late_blocks[:-1], early_blocks = lax.optimization_barrier((late_blocks[:-1], early_blocks))
    early_blocks = scattered(early_blocks)
    back = total_of(late_blocks)
    other = lax.ppermute(back, "expert", partner)
    base = combine(0, mixed, weight, early_blocks, pltpu.VMEM(mixed.shape, jnp.float32))
    return combine(
        1, base, weight, [other], jax.ShapeDtypeStruct(mixed.shape, jnp.bfloat16)
    )


def solution(mesh):
    placed = (
        P(("groups", "expert"), None),
        P(("groups", "expert"), None),
        P(("groups", "expert"), None),
        P(("groups", "expert"), None),
        P(("groups", "expert")),
        P(),
        P(("groups", "expert"), None),
        P(("groups", "expert"), None),
        P(None, "expert"),
        P(None, "expert"),
        P("expert", None),
    )
    return jax.shard_map(
        shards, mesh=mesh, in_specs=placed, out_specs=P(("groups", "expert"), None), check_vma=False
    )
```

```python
import functools

import jax
import jax.numpy as jnp
from jax import lax
from jax.experimental import pallas as pl
from jax.experimental.pallas import tpu as pltpu
from jax.sharding import PartitionSpec as P

HEAD_DIM = 128
E_WIN = 2
WIN_DEV = 3
BLOCKS = 5
CAP = 20
SPARE = 16
HEADS_STEP = 8
MASKED = -1e30
MIB = 1024 * 1024


def far(x):
    return pltpu.with_memory_space_constraint(x, pltpu.HBM)


def close(x):
    return pltpu.with_memory_space_constraint(x, pltpu.VMEM)


NEAR = pl.BlockSpec(memory_space=pltpu.VMEM)


def bundle_kernel(keys, segs, out):
    rows, width = keys.shape
    out[:, :width] = keys[...]
    out[:, width:] = jnp.zeros((rows, HEAD_DIM), keys.dtype)
    out[:SPARE, width : width + rows] = jnp.broadcast_to(
        segs[...].astype(jnp.float32), (SPARE, rows)
    ).astype(keys.dtype)


def bundle(keys, segs):
    rows, width = keys.shape
    return pl.pallas_call(
        bundle_kernel,
        in_specs=[NEAR, NEAR],
        out_specs=NEAR,
        out_shape=jax.ShapeDtypeStruct((rows, width + HEAD_DIM), keys.dtype),
        cost_estimate=pl.CostEstimate(
            flops=0, bytes_accessed=4 * rows * width, transcendentals=0
        ),
        compiler_params=pltpu.CompilerParams(vmem_limit_bytes=6 * MIB),
        name="bundle",
    )(far(keys), far(segs))


def choose_kernel(flags, first, second, third, out):
    for value, block in enumerate((first, second, third)):

        @pl.when(flags[6] == value)
        def _():
            out[...] = block[...]


def choose(flags, blocks):
    return pl.pallas_call(
        choose_kernel,
        in_specs=[pl.BlockSpec(memory_space=pltpu.SMEM)] + [NEAR] * 3,
        out_specs=NEAR,
        out_shape=jax.ShapeDtypeStruct(blocks[0].shape, blocks[0].dtype),
        compiler_params=pltpu.CompilerParams(vmem_limit_bytes=6 * MIB),
        name="choose",
    )(flags, *[close(block) for block in blocks])


def attention_kernel(
    deltas, q, k0, v0, k1, v1, k2, v2, k3, v3, k4, v4, seg0, resid, gain, routes, gates,
    mixed_out, keep_out, send_out, weight_out,
):
    rows, model = q.shape
    keys = BLOCKS * rows
    width = HEADS_STEP * HEAD_DIM

    seg_own = seg0[...].astype(jnp.float32)
    seg_row = jnp.concatenate(
        [seg_own]
        + [block[:SPARE, model:][0:1, :rows].astype(jnp.float32) for block in (k1, k2, k3, k4)],
        axis=1,
    )
    eye = lax.broadcasted_iota(jnp.int32, (rows, rows), 0) == lax.broadcasted_iota(
        jnp.int32, (rows, rows), 1
    )
    seg_col = jnp.sum(jnp.where(eye, seg_own, 0.0), axis=1, keepdims=True)
    lane = lax.broadcasted_iota(jnp.int32, (rows, keys), 1)
    sub = lax.broadcasted_iota(jnp.int32, (rows, keys), 0)
    block = lane // rows
    back = jnp.zeros_like(block)
    for at in range(1, BLOCKS):
        back = jnp.where(block == at, deltas[at], back)
    distance = sub - (lane - block * rows) + back * rows
    allowed = (distance >= 0) & (distance <= WIN_DEV * rows) & (seg_col == seg_row)
    bias = jnp.where(allowed, 0.0, MASKED)
    scale = 1.0 / HEAD_DIM**0.5
    heads = [slice(head * HEAD_DIM, (head + 1) * HEAD_DIM) for head in range(HEADS_STEP)]

    @pl.loop(0, model // width)
    def _(step):
        at = pl.ds(pl.multiple_of(step * width, width), width)
        query = q[:, at]
        key = jnp.concatenate([k0[:, at], k1[:, at], k2[:, at], k3[:, at], k4[:, at]], axis=0)
        value = jnp.concatenate([v0[:, at], v1[:, at], v2[:, at], v3[:, at], v4[:, at]], axis=0)
        scores = jnp.stack(
            [
                lax.dot_general(
                    query[:, cols], key[:, cols], (((1,), (1,)), ((), ())),
                    preferred_element_type=jnp.float32,
                )
                for cols in heads
            ]
        )
        scores = scores * scale + bias[None]
        expo = jnp.exp(scores - jnp.max(scores, axis=2, keepdims=True))
        denom = jnp.sum(expo, axis=2, keepdims=True)
        probs = expo.astype(jnp.bfloat16)
        outs = [
            jnp.dot(probs[head], value[:, cols], preferred_element_type=jnp.float32)
            / denom[head]
            for head, cols in enumerate(heads)
        ]
        mixed_out[:, at] = resid[:, at].astype(jnp.float32) + jnp.concatenate(outs, axis=1)

    mixed = mixed_out[...]
    normed = (
        mixed * lax.rsqrt(jnp.mean(mixed * mixed, axis=1, keepdims=True) + 1e-05) * gain[...]
    ).astype(jnp.bfloat16)
    across = lax.broadcasted_iota(jnp.int32, (rows, rows), 1)
    down = lax.broadcasted_iota(jnp.int32, (rows, rows), 0)
    upper = jnp.where(down < across, 1.0, 0.0).astype(jnp.bfloat16)
    eye = jnp.where(down == across, 1.0, 0.0).astype(jnp.bfloat16)
    slot = lax.broadcasted_iota(jnp.int32, (32, rows), 0)

    def picks(expert):
        hit = routes[...] == expert
        member = jnp.max(jnp.where(hit, 1.0, 0.0), axis=0, keepdims=True)
        weight = jnp.sum(
            jnp.where(hit, gates[...].astype(jnp.float32), 0.0), axis=0, keepdims=True
        )
        rank = jnp.dot(
            jnp.broadcast_to(member, (8, rows)).astype(jnp.bfloat16),
            upper,
            preferred_element_type=jnp.float32,
        )[0:1].astype(jnp.int32)
        return member > 0.5, weight, rank

    def spread(pick, weight):
        return lax.dot_general(
            eye,
            jnp.where(pick, weight, 0.0).astype(jnp.bfloat16),
            (((1,), (1,)), ((), ())),
            preferred_element_type=jnp.float32,
        ).astype(jnp.bfloat16)

    def packed(pick):
        return jnp.dot(
            jnp.where(pick, 1.0, 0.0).astype(jnp.bfloat16),
            normed,
            preferred_element_type=jnp.float32,
        ).astype(jnp.bfloat16)

    for place, out in ((0, keep_out), (1, send_out)):
        member, weight, rank = picks(deltas[5] if place == 0 else 1 - deltas[5])
        pick = (slot == rank) & member
        out[...] = packed(pick)[:CAP]
        weight_out[place] = spread(pick, weight)


def attention(deltas, q, pairs, seg_own, resid, gain, routes, gates):
    rows, width = q.shape
    return pl.pallas_call(
        attention_kernel,
        in_specs=[pl.BlockSpec(memory_space=pltpu.SMEM)] + [NEAR] * (6 + len(pairs)),
        out_specs=[NEAR] * 4,
        out_shape=[
            pltpu.VMEM((rows, width), jnp.float32),
            jax.ShapeDtypeStruct((CAP, width), jnp.bfloat16),
            jax.ShapeDtypeStruct((CAP, width), jnp.bfloat16),
            jax.ShapeDtypeStruct((E_WIN, rows, 32), jnp.bfloat16),
        ],
        compiler_params=pltpu.CompilerParams(vmem_limit_bytes=14 * MIB),
        cost_estimate=pl.CostEstimate(
            flops=4 * rows * BLOCKS * rows * width, bytes_accessed=8 * rows * width * 4,
            transcendentals=rows * BLOCKS * rows * (width // HEAD_DIM),
        ),
        name="attention",
    )(
        deltas, close(q), close(pairs[0]), close(pairs[1]), *pairs[2:], close(seg_own),
        close(resid), close(gain), close(routes), close(gates),
    )


def bring_kernel(count, *refs):
    sources, held, sems = refs[:count], refs[count + 1 : 2 * count + 1], refs[-1]
    copies = [
        pltpu.make_async_copy(source, target, sems.at[at])
        for at, (source, target) in enumerate(zip(sources, held))
    ]
    for copy in copies:
        copy.start()
    for copy in copies:
        copy.wait()


def bring(arrays, after):
    count = len(arrays)
    anywhere = pl.BlockSpec(memory_space=pl.ANY)
    return pl.pallas_call(
        functools.partial(bring_kernel, count),
        in_specs=[anywhere] * (count + 1),
        out_specs=[NEAR] * count,
        out_shape=[pltpu.VMEM(x.shape, x.dtype) for x in arrays],
        scratch_shapes=[pltpu.SemaphoreType.DMA((count,))],
        compiler_params=pltpu.CompilerParams(vmem_limit_bytes=2 * MIB),
        cost_estimate=pl.CostEstimate(
            flops=0, bytes_accessed=4 * sum(x.size for x in arrays), transcendentals=0
        ),
        name="bring",
    )(*[far(x) for x in arrays], after)


def fetch_kernel(parts, source, after, held, sems):
    depth = source.shape[0] // parts
    copies = []
    for part in range(parts):
        at = pl.ds(part * depth, depth)
        copies.append(pltpu.make_async_copy(source.at[at], held.at[at], sems.at[part]))
    for copy in copies:
        copy.start()
    for copy in copies:
        copy.wait()


def fetch(weights, after):
    parts = 4
    anywhere = pl.BlockSpec(memory_space=pl.ANY)
    return pl.pallas_call(
        functools.partial(fetch_kernel, parts),
        in_specs=[anywhere, anywhere],
        out_specs=NEAR,
        out_shape=pltpu.VMEM(weights.shape, weights.dtype),
        scratch_shapes=[pltpu.SemaphoreType.DMA((parts,))],
        compiler_params=pltpu.CompilerParams(vmem_limit_bytes=2 * MIB),
        cost_estimate=pl.CostEstimate(
            flops=0, bytes_accessed=4 * weights.size, transcendentals=0
        ),
        name="fetch",
    )(far(weights), after)


def experts_kernel(local, remote, w_gate, w_up, w_down, local_out, remote_out, x, hidden):
    width, units = w_gate.shape
    tile = min(512, units)
    rows = local.shape[0]
    x[:rows] = local[...]
    x[rows:] = remote[...]

    @pl.loop(0, units // tile)
    def _(part):
        at = pl.ds(pl.multiple_of(part * tile, tile), tile)
        gate = jnp.dot(x[...], w_gate[:, at], preferred_element_type=jnp.float32)
        up = jnp.dot(x[...], w_up[:, at], preferred_element_type=jnp.float32)
        hidden[:, at] = (jax.nn.silu(gate) * up).astype(jnp.bfloat16)

    @pl.loop(0, width // 1024)
    def _(part):
        at = pl.ds(pl.multiple_of(part * 1024, 1024), 1024)
        out = jnp.dot(hidden[...], w_down[:, at], preferred_element_type=jnp.float32)
        local_out[:, at] = out[:rows].astype(jnp.bfloat16)
        remote_out[:, at] = out[rows:].astype(jnp.bfloat16)


def experts(local, remote, w_gate, w_up, w_down):
    rows, width = local.shape
    units = w_gate.shape[1]
    return pl.pallas_call(
        experts_kernel,
        in_specs=[NEAR] * 5,
        out_specs=[NEAR] * 2,
        out_shape=[jax.ShapeDtypeStruct((rows, width), jnp.bfloat16)] * 2,
        scratch_shapes=[
            pltpu.VMEM((2 * rows, width), jnp.bfloat16),
            pltpu.VMEM((2 * rows, units), jnp.bfloat16),
        ],
        compiler_params=pltpu.CompilerParams(vmem_limit_bytes=20 * MIB),
        cost_estimate=pl.CostEstimate(
            flops=12 * rows * width * units,
            bytes_accessed=8 * rows * width,
            transcendentals=2 * rows * units,
        ),
        name="experts",
    )(local, remote, close(w_gate), close(w_up), close(w_down))


def pile_kernel(*refs):
    blocks, out = refs[:-1], refs[-1]
    out[...] = jnp.concatenate(
        [block[...].astype(jnp.float32) for block in blocks], axis=0
    ).astype(out.dtype)


def pile(blocks):
    rows, width = blocks[0].shape
    return pl.pallas_call(
        pile_kernel,
        in_specs=[NEAR] * len(blocks),
        out_specs=NEAR,
        out_shape=jax.ShapeDtypeStruct((len(blocks) * rows, width), blocks[0].dtype),
        compiler_params=pltpu.CompilerParams(vmem_limit_bytes=(4 + len(blocks)) * MIB),
        name="pile",
    )(*blocks)


def add_kernel(first, second, *outs):
    rows = outs[0].shape[0]
    total = first[...].astype(jnp.float32) + second[...].astype(jnp.float32)
    for at, out in enumerate(outs):
        out[...] = total[at * rows : (at + 1) * rows].astype(out.dtype)


def add_split(first, second, blocks):
    rows, width = first.shape
    each = rows // blocks
    return pl.pallas_call(
        add_kernel,
        in_specs=[NEAR, NEAR],
        out_specs=[NEAR] * blocks,
        out_shape=[jax.ShapeDtypeStruct((each, width), first.dtype)] * blocks,
        compiler_params=pltpu.CompilerParams(vmem_limit_bytes=(6 + blocks) * MIB),
        name="add_split",
    )(first, second)


def total(blocks):
    result = blocks[0][...].astype(jnp.float32)
    for block in blocks[1:]:
        result = result + block[...].astype(jnp.float32)
    return result.astype(jnp.bfloat16)


def total_kernel(*refs):
    refs[-1][...] = total(refs[:-1])


def total_of(blocks):
    return pl.pallas_call(
        total_kernel,
        in_specs=[NEAR] * len(blocks),
        out_specs=NEAR,
        out_shape=jax.ShapeDtypeStruct(blocks[0].shape, blocks[0].dtype),
        compiler_params=pltpu.CompilerParams(vmem_limit_bytes=(4 + len(blocks)) * MIB),
        name="total",
    )(*blocks)


def combine_kernel(place, base, weight, *refs):
    blocks, out = refs[:-1], refs[-1]
    part = jnp.dot(
        weight[place][:, :CAP], total(blocks), preferred_element_type=jnp.float32
    )
    out[...] = (base[...] + part).astype(out.dtype)


def combine(place, base, weight, blocks, result):
    return pl.pallas_call(
        functools.partial(combine_kernel, place),
        in_specs=[NEAR] * (2 + len(blocks)),
        out_specs=NEAR,
        out_shape=result,
        compiler_params=pltpu.CompilerParams(vmem_limit_bytes=(8 + len(blocks)) * MIB),
        name="combine",
    )(close(base), weight, *blocks)


def shards(
    resid, queries, keys, values, segment_ids, norm_gain, routes, route_gates, w_gate, w_up, w_down
):
    count = lax.axis_size("expert")
    own = lax.axis_index("expert")
    shard_count = count // E_WIN

    place = own % 4

    def moved(block, steps):
        pairs = [(i, i + steps[i % 4]) for i in range(count) if i % 4 in steps]
        return lax.ppermute(block, "expert", [pair for pair in pairs if pair[1] < count])

    across = {0: 3, 1: 3, 2: -1, 3: 3}
    passed = {1: 4, 2: -2}
    beside = {0: 1, 1: 1, 2: 1}

    def swapped(block, mask):
        return lax.ppermute(block, "expert", [(i, i ^ mask) for i in range(count)])

    seg_own = segment_ids.reshape(1, -1)
    beyond = 2 * WIN_DEV + 2
    delta_list = [
        0 * own,
        jnp.where(place == 1, beyond, 3),
        jnp.where(place == 0, 1, jnp.where(place == 1, 3, beyond)),
        jnp.where(place == 0, beyond, 1),
        0 * own + 2,
    ]
    my_expert = own // shard_count
    source = jnp.where(place < 2, 0, jnp.where(place == 2, 1, 2))
    scalars = jnp.stack(
        [jnp.where(own >= delta, delta, beyond) for delta in delta_list] + [my_expert, source]
    ).astype(jnp.int32)

    key_block = bundle(keys, seg_own)
    key_one, value_one = moved(key_block, across), moved(values, across)
    key_three, value_three = moved(key_block, beside), moved(values, beside)
    key_two, value_two = moved(key_one, passed), moved(value_one, passed)
    mine = bring(
        [
            queries, keys, values, seg_own, resid, norm_gain.reshape(1, -1), routes.T,
            route_gates.T,
        ],
        scalars,
    )
    gate_held = fetch(w_gate, scalars)
    key_four = choose(scalars, [key_two, key_three, key_one])
    key_four, gate_held, mine = lax.optimization_barrier((key_four, gate_held, mine))
    key_four = swapped(key_four, 1)
    value_four = swapped(choose(scalars, [value_two, value_three, value_one]), 1)

    queries, keys, values, seg_own, resid, gain, routes_held, gates_held = mine
    mixed, keep, send, weight = attention(
        scalars,
        queries,
        [
            keys, values, key_one, value_one, key_two, value_two, key_three, value_three,
            key_four, value_four,
        ],
        seg_own, resid, gain, routes_held, gates_held,
    )
    up_held, down_held = fetch(w_up, weight), fetch(w_down, weight)
    partner = [(i, (i + shard_count) % count) for i in range(count)]
    masks = list(range(2, shard_count, 2))[::-1]
    got = lax.ppermute(send, "expert", partner)

    def spread(block):
        return [block] + [swapped(block, mask) for mask in masks]

    def both_cores(blocks):
        local = pile(blocks)
        return local, swapped(local, 1)

    def summed(parts):
        return add_split(parts[0], swapped(parts[1], 1), 1 + len(masks))

    def scattered(blocks):
        moved = [swapped(block, mask) for block, mask in zip(blocks[1:], masks)]
        return [blocks[0]] + moved[::-1]

    early_blocks = spread(keep)
    early_blocks, got, up_held, down_held = lax.optimization_barrier(
        (early_blocks, got, up_held, down_held)
    )
    held = [gate_held, up_held, down_held]
    early_parts = experts(*both_cores(early_blocks), *held)
    late_blocks = spread(got)
    late_blocks, early_parts = lax.optimization_barrier((late_blocks, early_parts))
    late_blocks = summed(experts(*both_cores(late_blocks), *held))
    early_blocks = summed(early_parts)
    late_blocks, early_blocks = lax.optimization_barrier((late_blocks, early_blocks))
    late_blocks = scattered(late_blocks)
    late_blocks[:-1], early_blocks = lax.optimization_barrier((late_blocks[:-1], early_blocks))
    early_blocks = scattered(early_blocks)
    back = total_of(late_blocks)
    other = lax.ppermute(back, "expert", partner)
    base = combine(0, mixed, weight, early_blocks, pltpu.VMEM(mixed.shape, jnp.float32))
    return combine(
        1, base, weight, [other], jax.ShapeDtypeStruct(mixed.shape, jnp.bfloat16)
    )


def solution(mesh):
    placed = (
        P(("groups", "expert"), None),
        P(("groups", "expert"), None),
        P(("groups", "expert"), None),
        P(("groups", "expert"), None),
        P(("groups", "expert")),
        P(),
        P(("groups", "expert"), None),
        P(("groups", "expert"), None),
        P(None, "expert"),
        P(None, "expert"),
        P("expert", None),
    )
    return jax.shard_map(
        shards, mesh=mesh, in_specs=placed, out_specs=P(("groups", "expert"), None), check_vma=False
    )
```

```python
import functools

import jax
import jax.numpy as jnp
from jax import lax
from jax.experimental import pallas as pl
from jax.experimental.pallas import tpu as pltpu
from jax.sharding import PartitionSpec as P

HEAD_DIM = 128
E_WIN = 2
WIN_DEV = 3
BLOCKS = 5
CAP = 20
SPARE = 16
HEADS_STEP = 8
MASKED = -1e30
MIB = 1024 * 1024


def far(x):
    return pltpu.with_memory_space_constraint(x, pltpu.HBM)


def close(x):
    return pltpu.with_memory_space_constraint(x, pltpu.VMEM)


NEAR = pl.BlockSpec(memory_space=pltpu.VMEM)


def bundle_kernel(keys, segs, out):
    rows, width = keys.shape
    out[:, :width] = keys[...]
    out[:, width:] = jnp.zeros((rows, HEAD_DIM), keys.dtype)
    out[:SPARE, width : width + rows] = jnp.broadcast_to(
        segs[...].astype(jnp.float32), (SPARE, rows)
    ).astype(keys.dtype)


def bundle(keys, segs):
    rows, width = keys.shape
    return pl.pallas_call(
        bundle_kernel,
        in_specs=[NEAR, NEAR],
        out_specs=NEAR,
        out_shape=pltpu.VMEM((rows, width + HEAD_DIM), keys.dtype),
        cost_estimate=pl.CostEstimate(
            flops=0, bytes_accessed=4 * rows * width, transcendentals=0
        ),
        compiler_params=pltpu.CompilerParams(vmem_limit_bytes=6 * MIB),
        name="bundle",
    )(far(keys), far(segs))


def choose_kernel(flags, first, second, third, out):
    for value, block in enumerate((first, second, third)):

        @pl.when(flags[6] == value)
        def _():
            out[...] = block[...]


def choose(flags, blocks):
    return pl.pallas_call(
        choose_kernel,
        in_specs=[pl.BlockSpec(memory_space=pltpu.SMEM)] + [NEAR] * 3,
        out_specs=NEAR,
        out_shape=jax.ShapeDtypeStruct(blocks[0].shape, blocks[0].dtype),
        compiler_params=pltpu.CompilerParams(vmem_limit_bytes=6 * MIB),
        name="choose",
    )(flags, *[close(block) for block in blocks])


def attention_kernel(
    deltas, q, k0, v0, k1, v1, k2, v2, k3, v3, k4, v4, seg0, resid, gain, routes, gates,
    mixed_out, keep_out, send_out, weight_out,
):
    rows, model = q.shape
    keys = BLOCKS * rows
    width = HEADS_STEP * HEAD_DIM

    seg_own = seg0[...].astype(jnp.float32)
    seg_row = jnp.concatenate(
        [seg_own]
        + [block[:SPARE, model:][0:1, :rows].astype(jnp.float32) for block in (k1, k2, k3, k4)],
        axis=1,
    )
    eye = lax.broadcasted_iota(jnp.int32, (rows, rows), 0) == lax.broadcasted_iota(
        jnp.int32, (rows, rows), 1
    )
    seg_col = jnp.sum(jnp.where(eye, seg_own, 0.0), axis=1, keepdims=True)
    lane = lax.broadcasted_iota(jnp.int32, (rows, keys), 1)
    sub = lax.broadcasted_iota(jnp.int32, (rows, keys), 0)
    block = lane // rows
    back = jnp.zeros_like(block)
    for at in range(1, BLOCKS):
        back = jnp.where(block == at, deltas[at], back)
    distance = sub - (lane - block * rows) + back * rows
    allowed = (distance >= 0) & (distance <= WIN_DEV * rows) & (seg_col == seg_row)
    bias = jnp.where(allowed, 0.0, MASKED)
    scale = 1.0 / HEAD_DIM**0.5
    heads = [slice(head * HEAD_DIM, (head + 1) * HEAD_DIM) for head in range(HEADS_STEP)]

    @pl.loop(0, model // width)
    def _(step):
        at = pl.ds(pl.multiple_of(step * width, width), width)
        query = q[:, at]
        key = jnp.concatenate([k0[:, at], k1[:, at], k2[:, at], k3[:, at], k4[:, at]], axis=0)
        value = jnp.concatenate([v0[:, at], v1[:, at], v2[:, at], v3[:, at], v4[:, at]], axis=0)
        scores = jnp.stack(
            [
                lax.dot_general(
                    query[:, cols], key[:, cols], (((1,), (1,)), ((), ())),
                    preferred_element_type=jnp.float32,
                )
                for cols in heads
            ]
        )
        scores = scores * scale + bias[None]
        expo = jnp.exp(scores - jnp.max(scores, axis=2, keepdims=True))
        denom = jnp.sum(expo, axis=2, keepdims=True)
        probs = expo.astype(jnp.bfloat16)
        outs = [
            jnp.dot(probs[head], value[:, cols], preferred_element_type=jnp.float32)
            / denom[head]
            for head, cols in enumerate(heads)
        ]
        mixed_out[:, at] = resid[:, at].astype(jnp.float32) + jnp.concatenate(outs, axis=1)

    mixed = mixed_out[...]
    normed = (
        mixed * lax.rsqrt(jnp.mean(mixed * mixed, axis=1, keepdims=True) + 1e-05) * gain[...]
    ).astype(jnp.bfloat16)
    across = lax.broadcasted_iota(jnp.int32, (rows, rows), 1)
    down = lax.broadcasted_iota(jnp.int32, (rows, rows), 0)
    upper = jnp.where(down < across, 1.0, 0.0).astype(jnp.bfloat16)
    eye = jnp.where(down == across, 1.0, 0.0).astype(jnp.bfloat16)
    slot = lax.broadcasted_iota(jnp.int32, (32, rows), 0)

    def picks(expert):
        hit = routes[...] == expert
        member = jnp.max(jnp.where(hit, 1.0, 0.0), axis=0, keepdims=True)
        weight = jnp.sum(
            jnp.where(hit, gates[...].astype(jnp.float32), 0.0), axis=0, keepdims=True
        )
        rank = jnp.dot(
            jnp.broadcast_to(member, (8, rows)).astype(jnp.bfloat16),
            upper,
            preferred_element_type=jnp.float32,
        )[0:1].astype(jnp.int32)
        return member > 0.5, weight, rank

    def spread(pick, weight):
        return lax.dot_general(
            eye,
            jnp.where(pick, weight, 0.0).astype(jnp.bfloat16),
            (((1,), (1,)), ((), ())),
            preferred_element_type=jnp.float32,
        ).astype(jnp.bfloat16)

    def packed(pick):
        return jnp.dot(
            jnp.where(pick, 1.0, 0.0).astype(jnp.bfloat16),
            normed,
            preferred_element_type=jnp.float32,
        ).astype(jnp.bfloat16)

    for place, out in ((0, keep_out), (1, send_out)):
        member, weight, rank = picks(deltas[5] if place == 0 else 1 - deltas[5])
        pick = (slot == rank) & member
        out[...] = packed(pick)[:CAP]
        weight_out[place] = spread(pick, weight)


def attention(deltas, q, pairs, seg_own, resid, gain, routes, gates):
    rows, width = q.shape
    return pl.pallas_call(
        attention_kernel,
        in_specs=[pl.BlockSpec(memory_space=pltpu.SMEM)] + [NEAR] * (6 + len(pairs)),
        out_specs=[NEAR] * 4,
        out_shape=[
            pltpu.VMEM((rows, width), jnp.float32),
            jax.ShapeDtypeStruct((CAP, width), jnp.bfloat16),
            jax.ShapeDtypeStruct((CAP, width), jnp.bfloat16),
            jax.ShapeDtypeStruct((E_WIN, rows, 32), jnp.bfloat16),
        ],
        compiler_params=pltpu.CompilerParams(vmem_limit_bytes=14 * MIB),
        cost_estimate=pl.CostEstimate(
            flops=4 * rows * BLOCKS * rows * width, bytes_accessed=8 * rows * width * 4,
            transcendentals=rows * BLOCKS * rows * (width // HEAD_DIM),
        ),
        name="attention",
    )(
        deltas, close(q), close(pairs[0]), close(pairs[1]), *pairs[2:], close(seg_own),
        close(resid), close(gain), close(routes), close(gates),
    )


def bring_kernel(count, *refs):
    sources, held, sems = refs[:count], refs[count + 1 : 2 * count + 1], refs[-1]
    copies = [
        pltpu.make_async_copy(source, target, sems.at[at])
        for at, (source, target) in enumerate(zip(sources, held))
    ]
    for copy in copies:
        copy.start()
    for copy in copies:
        copy.wait()


def bring(arrays, after):
    count = len(arrays)
    anywhere = pl.BlockSpec(memory_space=pl.ANY)
    return pl.pallas_call(
        functools.partial(bring_kernel, count),
        in_specs=[anywhere] * (count + 1),
        out_specs=[NEAR] * count,
        out_shape=[pltpu.VMEM(x.shape, x.dtype) for x in arrays],
        scratch_shapes=[pltpu.SemaphoreType.DMA((count,))],
        compiler_params=pltpu.CompilerParams(vmem_limit_bytes=2 * MIB),
        cost_estimate=pl.CostEstimate(
            flops=0, bytes_accessed=4 * sum(x.size for x in arrays), transcendentals=0
        ),
        name="bring",
    )(*[far(x) for x in arrays], after)


def fetch_kernel(parts, source, after, held, sems):
    depth = source.shape[0] // parts
    copies = []
    for part in range(parts):
        at = pl.ds(part * depth, depth)
        copies.append(pltpu.make_async_copy(source.at[at], held.at[at], sems.at[part]))
    for copy in copies:
        copy.start()
    for copy in copies:
        copy.wait()


def fetch(weights, after):
    parts = 4
    anywhere = pl.BlockSpec(memory_space=pl.ANY)
    return pl.pallas_call(
        functools.partial(fetch_kernel, parts),
        in_specs=[anywhere, anywhere],
        out_specs=NEAR,
        out_shape=pltpu.VMEM(weights.shape, weights.dtype),
        scratch_shapes=[pltpu.SemaphoreType.DMA((parts,))],
        compiler_params=pltpu.CompilerParams(vmem_limit_bytes=2 * MIB),
        cost_estimate=pl.CostEstimate(
            flops=0, bytes_accessed=4 * weights.size, transcendentals=0
        ),
        name="fetch",
    )(far(weights), after)


def experts_kernel(local, remote, w_gate, w_up, w_down, local_out, remote_out, x, hidden):
    width, units = w_gate.shape
    tile = min(512, units)
    rows = local.shape[0]
    x[:rows] = local[...]
    x[rows:] = remote[...]

    @pl.loop(0, units // tile)
    def _(part):
        at = pl.ds(pl.multiple_of(part * tile, tile), tile)
        gate = jnp.dot(x[...], w_gate[:, at], preferred_element_type=jnp.float32)
        up = jnp.dot(x[...], w_up[:, at], preferred_element_type=jnp.float32)
        hidden[:, at] = (jax.nn.silu(gate) * up).astype(jnp.bfloat16)

    @pl.loop(0, width // 1024)
    def _(part):
        at = pl.ds(pl.multiple_of(part * 1024, 1024), 1024)
        out = jnp.dot(hidden[...], w_down[:, at], preferred_element_type=jnp.float32)
        local_out[:, at] = out[:rows].astype(jnp.bfloat16)
        remote_out[:, at] = out[rows:].astype(jnp.bfloat16)


def experts(local, remote, w_gate, w_up, w_down):
    rows, width = local.shape
    units = w_gate.shape[1]
    return pl.pallas_call(
        experts_kernel,
        in_specs=[NEAR] * 5,
        out_specs=[NEAR] * 2,
        out_shape=[jax.ShapeDtypeStruct((rows, width), jnp.bfloat16)] * 2,
        scratch_shapes=[
            pltpu.VMEM((2 * rows, width), jnp.bfloat16),
            pltpu.VMEM((2 * rows, units), jnp.bfloat16),
        ],
        compiler_params=pltpu.CompilerParams(vmem_limit_bytes=20 * MIB),
        cost_estimate=pl.CostEstimate(
            flops=12 * rows * width * units,
            bytes_accessed=8 * rows * width,
            transcendentals=2 * rows * units,
        ),
        name="experts",
    )(local, remote, close(w_gate), close(w_up), close(w_down))


def pile_kernel(*refs):
    blocks, out = refs[:-1], refs[-1]
    out[...] = jnp.concatenate(
        [block[...].astype(jnp.float32) for block in blocks], axis=0
    ).astype(out.dtype)


def pile(blocks):
    rows, width = blocks[0].shape
    return pl.pallas_call(
        pile_kernel,
        in_specs=[NEAR] * len(blocks),
        out_specs=NEAR,
        out_shape=jax.ShapeDtypeStruct((len(blocks) * rows, width), blocks[0].dtype),
        compiler_params=pltpu.CompilerParams(vmem_limit_bytes=(4 + len(blocks)) * MIB),
        name="pile",
    )(*blocks)


def add_kernel(first, second, *outs):
    rows = outs[0].shape[0]
    total = first[...].astype(jnp.float32) + second[...].astype(jnp.float32)
    for at, out in enumerate(outs):
        out[...] = total[at * rows : (at + 1) * rows].astype(out.dtype)


def add_split(first, second, blocks):
    rows, width = first.shape
    each = rows // blocks
    return pl.pallas_call(
        add_kernel,
        in_specs=[NEAR, NEAR],
        out_specs=[NEAR] * blocks,
        out_shape=[jax.ShapeDtypeStruct((each, width), first.dtype)] * blocks,
        compiler_params=pltpu.CompilerParams(vmem_limit_bytes=(6 + blocks) * MIB),
        name="add_split",
    )(first, second)


def total(blocks):
    result = blocks[0][...].astype(jnp.float32)
    for block in blocks[1:]:
        result = result + block[...].astype(jnp.float32)
    return result.astype(jnp.bfloat16)


def total_kernel(*refs):
    refs[-1][...] = total(refs[:-1])


def total_of(blocks):
    return pl.pallas_call(
        total_kernel,
        in_specs=[NEAR] * len(blocks),
        out_specs=NEAR,
        out_shape=jax.ShapeDtypeStruct(blocks[0].shape, blocks[0].dtype),
        compiler_params=pltpu.CompilerParams(vmem_limit_bytes=(4 + len(blocks)) * MIB),
        name="total",
    )(*blocks)


def combine_kernel(place, base, weight, *refs):
    blocks, out = refs[:-1], refs[-1]
    part = jnp.dot(
        weight[place][:, :CAP], total(blocks), preferred_element_type=jnp.float32
    )
    out[...] = (base[...] + part).astype(out.dtype)


def combine(place, base, weight, blocks, result):
    return pl.pallas_call(
        functools.partial(combine_kernel, place),
        in_specs=[NEAR] * (2 + len(blocks)),
        out_specs=NEAR,
        out_shape=result,
        compiler_params=pltpu.CompilerParams(vmem_limit_bytes=(8 + len(blocks)) * MIB),
        name="combine",
    )(close(base), weight, *blocks)


def shards(
    resid, queries, keys, values, segment_ids, norm_gain, routes, route_gates, w_gate, w_up, w_down
):
    count = lax.axis_size("expert")
    own = lax.axis_index("expert")
    shard_count = count // E_WIN

    place = own % 4

    def moved(block, steps):
        pairs = [(i, i + steps[i % 4]) for i in range(count) if i % 4 in steps]
        return lax.ppermute(block, "expert", [pair for pair in pairs if pair[1] < count])

    across = {0: 3, 1: 3, 2: -1, 3: 3}
    passed = {1: 4, 2: -2}
    beside = {0: 1, 1: 1, 2: 1}

    def swapped(block, mask):
        return lax.ppermute(block, "expert", [(i, i ^ mask) for i in range(count)])

    seg_own = segment_ids.reshape(1, -1)
    beyond = 2 * WIN_DEV + 2
    delta_list = [
        0 * own,
        jnp.where(place == 1, beyond, 3),
        jnp.where(place == 0, 1, jnp.where(place == 1, 3, beyond)),
        jnp.where(place == 0, beyond, 1),
        0 * own + 2,
    ]
    my_expert = own // shard_count
    source = jnp.where(place < 2, 0, jnp.where(place == 2, 1, 2))
    scalars = jnp.stack(
        [jnp.where(own >= delta, delta, beyond) for delta in delta_list] + [my_expert, source]
    ).astype(jnp.int32)

    key_block = bundle(keys, seg_own)
    key_one, value_one = moved(key_block, across), moved(values, across)
    key_three, value_three = moved(key_block, beside), moved(values, beside)
    mine = bring(
        [
            queries, keys, values, seg_own, resid, norm_gain.reshape(1, -1), routes.T,
            route_gates.T,
        ],
        scalars,
    )
    gate_held = fetch(w_gate, scalars)
    key_two = moved(key_one, passed)
    value_one, gate_held, mine = lax.optimization_barrier((value_one, gate_held, mine))
    value_two = moved(value_one, passed)
    key_four = swapped(choose(scalars, [key_two, key_three, key_one]), 1)
    value_four = swapped(choose(scalars, [value_two, value_three, value_one]), 1)

    queries, keys, values, seg_own, resid, gain, routes_held, gates_held = mine
    mixed, keep, send, weight = attention(
        scalars,
        queries,
        [
            keys, values, key_one, value_one, key_two, value_two, key_three, value_three,
            key_four, value_four,
        ],
        seg_own, resid, gain, routes_held, gates_held,
    )
    up_held, down_held = fetch(w_up, weight), fetch(w_down, weight)
    partner = [(i, (i + shard_count) % count) for i in range(count)]
    masks = list(range(2, shard_count, 2))[::-1]
    got = lax.ppermute(send, "expert", partner)

    def spread(block):
        return [block] + [swapped(block, mask) for mask in masks]

    def both_cores(blocks):
        local = pile(blocks)
        return local, swapped(local, 1)

    def summed(parts):
        return add_split(parts[0], swapped(parts[1], 1), 1 + len(masks))

    def scattered(blocks):
        moved = [swapped(block, mask) for block, mask in zip(blocks[1:], masks)]
        return [blocks[0]] + moved[::-1]

    early_blocks = spread(keep)
    early_blocks, got, up_held, down_held = lax.optimization_barrier(
        (early_blocks, got, up_held, down_held)
    )
    held = [gate_held, up_held, down_held]
    early_parts = experts(*both_cores(early_blocks), *held)
    late_blocks = spread(got)
    late_blocks, early_parts = lax.optimization_barrier((late_blocks, early_parts))
    late_blocks = summed(experts(*both_cores(late_blocks), *held))
    early_blocks = summed(early_parts)
    late_blocks, early_blocks = lax.optimization_barrier((late_blocks, early_blocks))
    late_blocks = scattered(late_blocks)
    late_blocks[:-1], early_blocks = lax.optimization_barrier((late_blocks[:-1], early_blocks))
    early_blocks = scattered(early_blocks)
    back = total_of(late_blocks)
    other = lax.ppermute(back, "expert", partner)
    base = combine(0, mixed, weight, early_blocks, pltpu.VMEM(mixed.shape, jnp.float32))
    return combine(
        1, base, weight, [other], jax.ShapeDtypeStruct(mixed.shape, jnp.bfloat16)
    )


def solution(mesh):
    placed = (
        P(("groups", "expert"), None),
        P(("groups", "expert"), None),
        P(("groups", "expert"), None),
        P(("groups", "expert"), None),
        P(("groups", "expert")),
        P(),
        P(("groups", "expert"), None),
        P(("groups", "expert"), None),
        P(None, "expert"),
        P(None, "expert"),
        P("expert", None),
    )
    return jax.shard_map(
        shards, mesh=mesh, in_specs=placed, out_specs=P(("groups", "expert"), None), check_vma=False
    )
```

```python
import functools

import jax
import jax.numpy as jnp
from jax import lax
from jax.experimental import pallas as pl
from jax.experimental.pallas import tpu as pltpu
from jax.sharding import PartitionSpec as P

HEAD_DIM = 128
E_WIN = 2
WIN_DEV = 3
BLOCKS = 5
CAP = 20
SPARE = 16
HEADS_STEP = 8
MASKED = -1e30
MIB = 1024 * 1024


def far(x):
    return pltpu.with_memory_space_constraint(x, pltpu.HBM)


def close(x):
    return pltpu.with_memory_space_constraint(x, pltpu.VMEM)


NEAR = pl.BlockSpec(memory_space=pltpu.VMEM)


def bundle_kernel(keys, segs, out):
    rows, width = keys.shape
    out[:, :width] = keys[...]
    out[:, width:] = jnp.zeros((rows, HEAD_DIM), keys.dtype)
    out[:SPARE, width : width + rows] = jnp.broadcast_to(
        segs[...].astype(jnp.float32), (SPARE, rows)
    ).astype(keys.dtype)


def bundle(keys, segs):
    rows, width = keys.shape
    return pl.pallas_call(
        bundle_kernel,
        in_specs=[NEAR, NEAR],
        out_specs=NEAR,
        out_shape=pltpu.VMEM((rows, width + HEAD_DIM), keys.dtype),
        cost_estimate=pl.CostEstimate(
            flops=0, bytes_accessed=4 * rows * width, transcendentals=0
        ),
        compiler_params=pltpu.CompilerParams(vmem_limit_bytes=6 * MIB),
        name="bundle",
    )(far(keys), far(segs))


def choose_kernel(flags, first, second, third, out):
    for value, block in enumerate((first, second, third)):

        @pl.when(flags[6] == value)
        def _():
            out[...] = block[...]


def choose(flags, blocks):
    return pl.pallas_call(
        choose_kernel,
        in_specs=[pl.BlockSpec(memory_space=pltpu.SMEM)] + [NEAR] * 3,
        out_specs=NEAR,
        out_shape=jax.ShapeDtypeStruct(blocks[0].shape, blocks[0].dtype),
        compiler_params=pltpu.CompilerParams(vmem_limit_bytes=6 * MIB),
        name="choose",
    )(flags, *[close(block) for block in blocks])


def attention_kernel(
    deltas, q, k0, v0, k1, v1, k2, v2, k3, v3, k4, v4, seg0, resid, gain, routes, gates,
    mixed_out, keep_out, send_out, weight_out,
):
    rows, model = q.shape
    keys = BLOCKS * rows
    width = HEADS_STEP * HEAD_DIM

    seg_own = seg0[...].astype(jnp.float32)
    seg_row = jnp.concatenate(
        [seg_own]
        + [block[:SPARE, model:][0:1, :rows].astype(jnp.float32) for block in (k1, k2, k3, k4)],
        axis=1,
    )
    eye = lax.broadcasted_iota(jnp.int32, (rows, rows), 0) == lax.broadcasted_iota(
        jnp.int32, (rows, rows), 1
    )
    seg_col = jnp.sum(jnp.where(eye, seg_own, 0.0), axis=1, keepdims=True)
    lane = lax.broadcasted_iota(jnp.int32, (rows, keys), 1)
    sub = lax.broadcasted_iota(jnp.int32, (rows, keys), 0)
    block = lane // rows
    back = jnp.zeros_like(block)
    for at in range(1, BLOCKS):
        back = jnp.where(block == at, deltas[at], back)
    distance = sub - (lane - block * rows) + back * rows
    allowed = (distance >= 0) & (distance <= WIN_DEV * rows) & (seg_col == seg_row)
    bias = jnp.where(allowed, 0.0, MASKED)
    scale = 1.0 / HEAD_DIM**0.5
    heads = [slice(head * HEAD_DIM, (head + 1) * HEAD_DIM) for head in range(HEADS_STEP)]

    @pl.loop(0, model // width)
    def _(step):
        at = pl.ds(pl.multiple_of(step * width, width), width)
        query = q[:, at]
        key = jnp.concatenate([k0[:, at], k1[:, at], k2[:, at], k3[:, at], k4[:, at]], axis=0)
        value = jnp.concatenate([v0[:, at], v1[:, at], v2[:, at], v3[:, at], v4[:, at]], axis=0)
        scores = jnp.stack(
            [
                lax.dot_general(
                    query[:, cols], key[:, cols], (((1,), (1,)), ((), ())),
                    preferred_element_type=jnp.float32,
                )
                for cols in heads
            ]
        )
        scores = scores * scale + bias[None]
        expo = jnp.exp(scores - jnp.max(scores, axis=2, keepdims=True))
        denom = jnp.sum(expo, axis=2, keepdims=True)
        probs = expo.astype(jnp.bfloat16)
        outs = [
            jnp.dot(probs[head], value[:, cols], preferred_element_type=jnp.float32)
            / denom[head]
            for head, cols in enumerate(heads)
        ]
        mixed_out[:, at] = resid[:, at].astype(jnp.float32) + jnp.concatenate(outs, axis=1)

    mixed = mixed_out[...]
    normed = (
        mixed * lax.rsqrt(jnp.mean(mixed * mixed, axis=1, keepdims=True) + 1e-05) * gain[...]
    ).astype(jnp.bfloat16)
    across = lax.broadcasted_iota(jnp.int32, (rows, rows), 1)
    down = lax.broadcasted_iota(jnp.int32, (rows, rows), 0)
    upper = jnp.where(down < across, 1.0, 0.0).astype(jnp.bfloat16)
    eye = jnp.where(down == across, 1.0, 0.0).astype(jnp.bfloat16)
    slot = lax.broadcasted_iota(jnp.int32, (32, rows), 0)

    def picks(expert):
        hit = routes[...] == expert
        member = jnp.max(jnp.where(hit, 1.0, 0.0), axis=0, keepdims=True)
        weight = jnp.sum(
            jnp.where(hit, gates[...].astype(jnp.float32), 0.0), axis=0, keepdims=True
        )
        rank = jnp.dot(
            jnp.broadcast_to(member, (8, rows)).astype(jnp.bfloat16),
            upper,
            preferred_element_type=jnp.float32,
        )[0:1].astype(jnp.int32)
        return member > 0.5, weight, rank

    def spread(pick, weight):
        return lax.dot_general(
            eye,
            jnp.where(pick, weight, 0.0).astype(jnp.bfloat16),
            (((1,), (1,)), ((), ())),
            preferred_element_type=jnp.float32,
        ).astype(jnp.bfloat16)

    def packed(pick):
        return jnp.dot(
            jnp.where(pick, 1.0, 0.0).astype(jnp.bfloat16),
            normed,
            preferred_element_type=jnp.float32,
        ).astype(jnp.bfloat16)

    for place, out in ((0, keep_out), (1, send_out)):
        member, weight, rank = picks(deltas[5] if place == 0 else 1 - deltas[5])
        pick = (slot == rank) & member
        out[...] = packed(pick)[:CAP]
        weight_out[place] = spread(pick, weight)


def attention(deltas, q, pairs, seg_own, resid, gain, routes, gates):
    rows, width = q.shape
    return pl.pallas_call(
        attention_kernel,
        in_specs=[pl.BlockSpec(memory_space=pltpu.SMEM)] + [NEAR] * (6 + len(pairs)),
        out_specs=[NEAR] * 4,
        out_shape=[
            pltpu.VMEM((rows, width), jnp.float32),
            jax.ShapeDtypeStruct((CAP, width), jnp.bfloat16),
            jax.ShapeDtypeStruct((CAP, width), jnp.bfloat16),
            jax.ShapeDtypeStruct((E_WIN, rows, 32), jnp.bfloat16),
        ],
        compiler_params=pltpu.CompilerParams(vmem_limit_bytes=14 * MIB),
        cost_estimate=pl.CostEstimate(
            flops=4 * rows * BLOCKS * rows * width, bytes_accessed=8 * rows * width * 4,
            transcendentals=rows * BLOCKS * rows * (width // HEAD_DIM),
        ),
        name="attention",
    )(
        deltas, close(q), close(pairs[0]), close(pairs[1]), *pairs[2:], close(seg_own),
        close(resid), close(gain), close(routes), close(gates),
    )


def bring_kernel(count, *refs):
    sources, held, sems = refs[:count], refs[count + 1 : 2 * count + 1], refs[-1]
    copies = [
        pltpu.make_async_copy(source, target, sems.at[at])
        for at, (source, target) in enumerate(zip(sources, held))
    ]
    for copy in copies:
        copy.start()
    for copy in copies:
        copy.wait()


def bring(arrays, after):
    count = len(arrays)
    anywhere = pl.BlockSpec(memory_space=pl.ANY)
    return pl.pallas_call(
        functools.partial(bring_kernel, count),
        in_specs=[anywhere] * (count + 1),
        out_specs=[NEAR] * count,
        out_shape=[pltpu.VMEM(x.shape, x.dtype) for x in arrays],
        scratch_shapes=[pltpu.SemaphoreType.DMA((count,))],
        compiler_params=pltpu.CompilerParams(vmem_limit_bytes=2 * MIB),
        cost_estimate=pl.CostEstimate(
            flops=0, bytes_accessed=4 * sum(x.size for x in arrays), transcendentals=0
        ),
        name="bring",
    )(*[far(x) for x in arrays], after)


def fetch_kernel(parts, source, after, held, sems):
    depth = source.shape[0] // parts
    copies = []
    for part in range(parts):
        at = pl.ds(part * depth, depth)
        copies.append(pltpu.make_async_copy(source.at[at], held.at[at], sems.at[part]))
    for copy in copies:
        copy.start()
    for copy in copies:
        copy.wait()


def fetch(weights, after):
    parts = 4
    anywhere = pl.BlockSpec(memory_space=pl.ANY)
    return pl.pallas_call(
        functools.partial(fetch_kernel, parts),
        in_specs=[anywhere, anywhere],
        out_specs=NEAR,
        out_shape=pltpu.VMEM(weights.shape, weights.dtype),
        scratch_shapes=[pltpu.SemaphoreType.DMA((parts,))],
        compiler_params=pltpu.CompilerParams(vmem_limit_bytes=2 * MIB),
        cost_estimate=pl.CostEstimate(
            flops=0, bytes_accessed=4 * weights.size, transcendentals=0
        ),
        name="fetch",
    )(far(weights), after)


def experts_kernel(local, remote, w_gate, w_up, w_down, local_out, remote_out, x, hidden):
    width, units = w_gate.shape
    tile = min(512, units)
    rows = local.shape[0]
    x[:rows] = local[...]
    x[rows:] = remote[...]

    @pl.loop(0, units // tile)
    def _(part):
        at = pl.ds(pl.multiple_of(part * tile, tile), tile)
        gate = jnp.dot(x[...], w_gate[:, at], preferred_element_type=jnp.float32)
        up = jnp.dot(x[...], w_up[:, at], preferred_element_type=jnp.float32)
        hidden[:, at] = (jax.nn.silu(gate) * up).astype(jnp.bfloat16)

    @pl.loop(0, width // 1024)
    def _(part):
        at = pl.ds(pl.multiple_of(part * 1024, 1024), 1024)
        out = jnp.dot(hidden[...], w_down[:, at], preferred_element_type=jnp.float32)
        local_out[:, at] = out[:rows].astype(jnp.bfloat16)
        remote_out[:, at] = out[rows:].astype(jnp.bfloat16)


def experts(local, remote, w_gate, w_up, w_down):
    rows, width = local.shape
    units = w_gate.shape[1]
    return pl.pallas_call(
        experts_kernel,
        in_specs=[NEAR] * 5,
        out_specs=[NEAR] * 2,
        out_shape=[jax.ShapeDtypeStruct((rows, width), jnp.bfloat16)] * 2,
        scratch_shapes=[
            pltpu.VMEM((2 * rows, width), jnp.bfloat16),
            pltpu.VMEM((2 * rows, units), jnp.bfloat16),
        ],
        compiler_params=pltpu.CompilerParams(vmem_limit_bytes=20 * MIB),
        cost_estimate=pl.CostEstimate(
            flops=12 * rows * width * units,
            bytes_accessed=8 * rows * width,
            transcendentals=2 * rows * units,
        ),
        name="experts",
    )(local, remote, close(w_gate), close(w_up), close(w_down))


def pile_kernel(*refs):
    blocks, out = refs[:-1], refs[-1]
    out[...] = jnp.concatenate(
        [block[...].astype(jnp.float32) for block in blocks], axis=0
    ).astype(out.dtype)


def pile(blocks):
    rows, width = blocks[0].shape
    return pl.pallas_call(
        pile_kernel,
        in_specs=[NEAR] * len(blocks),
        out_specs=NEAR,
        out_shape=jax.ShapeDtypeStruct((len(blocks) * rows, width), blocks[0].dtype),
        compiler_params=pltpu.CompilerParams(vmem_limit_bytes=(4 + len(blocks)) * MIB),
        name="pile",
    )(*blocks)


def add_kernel(first, second, *outs):
    rows = outs[0].shape[0]
    total = first[...].astype(jnp.float32) + second[...].astype(jnp.float32)
    for at, out in enumerate(outs):
        out[...] = total[at * rows : (at + 1) * rows].astype(out.dtype)


def add_split(first, second, blocks):
    rows, width = first.shape
    each = rows // blocks
    return pl.pallas_call(
        add_kernel,
        in_specs=[NEAR, NEAR],
        out_specs=[NEAR] * blocks,
        out_shape=[jax.ShapeDtypeStruct((each, width), first.dtype)] * blocks,
        compiler_params=pltpu.CompilerParams(vmem_limit_bytes=(6 + blocks) * MIB),
        name="add_split",
    )(first, second)


def total(blocks):
    result = blocks[0][...].astype(jnp.float32)
    for block in blocks[1:]:
        result = result + block[...].astype(jnp.float32)
    return result.astype(jnp.bfloat16)


def total_kernel(*refs):
    refs[-1][...] = total(refs[:-1])


def total_of(blocks):
    return pl.pallas_call(
        total_kernel,
        in_specs=[NEAR] * len(blocks),
        out_specs=NEAR,
        out_shape=jax.ShapeDtypeStruct(blocks[0].shape, blocks[0].dtype),
        compiler_params=pltpu.CompilerParams(vmem_limit_bytes=(4 + len(blocks)) * MIB),
        name="total",
    )(*blocks)


def combine_kernel(place, base, weight, *refs):
    blocks, out = refs[:-1], refs[-1]
    part = jnp.dot(
        weight[place][:, :CAP], total(blocks), preferred_element_type=jnp.float32
    )
    out[...] = (base[...] + part).astype(out.dtype)


def combine(place, base, weight, blocks, result):
    return pl.pallas_call(
        functools.partial(combine_kernel, place),
        in_specs=[NEAR] * (2 + len(blocks)),
        out_specs=NEAR,
        out_shape=result,
        compiler_params=pltpu.CompilerParams(vmem_limit_bytes=(8 + len(blocks)) * MIB),
        name="combine",
    )(close(base), weight, *blocks)


def shards(
    resid, queries, keys, values, segment_ids, norm_gain, routes, route_gates, w_gate, w_up, w_down
):
    count = lax.axis_size("expert")
    own = lax.axis_index("expert")
    shard_count = count // E_WIN

    place = own % 4

    def moved(block, steps):
        pairs = [(i, i + steps[i % 4]) for i in range(count) if i % 4 in steps]
        return lax.ppermute(block, "expert", [pair for pair in pairs if pair[1] < count])

    across = {0: 3, 1: 3, 2: -1, 3: 3}
    passed = {1: 4, 2: -2}
    beside = {0: 1, 1: 1, 2: 1}

    def swapped(block, mask):
        return lax.ppermute(block, "expert", [(i, i ^ mask) for i in range(count)])

    seg_own = segment_ids.reshape(1, -1)
    beyond = 2 * WIN_DEV + 2
    delta_list = [
        0 * own,
        jnp.where(place == 1, beyond, 3),
        jnp.where(place == 0, 1, jnp.where(place == 1, 3, beyond)),
        jnp.where(place == 0, beyond, 1),
        0 * own + 2,
    ]
    my_expert = own // shard_count
    source = jnp.where(place < 2, 0, jnp.where(place == 2, 1, 2))
    scalars = jnp.stack(
        [jnp.where(own >= delta, delta, beyond) for delta in delta_list] + [my_expert, source]
    ).astype(jnp.int32)

    key_block = bundle(keys, seg_own)
    key_one, value_one = moved(key_block, across), moved(values, across)
    key_three, value_three = moved(key_block, beside), moved(values, beside)
    mine = bring(
        [
            queries, keys, values, seg_own, resid, norm_gain.reshape(1, -1), routes.T,
            route_gates.T,
        ],
        scalars,
    )
    gate_held = fetch(w_gate, scalars)
    key_two = moved(key_one, passed)
    value_one, gate_held, mine = lax.optimization_barrier((value_one, gate_held, mine))
    value_two = moved(value_one, passed)
    key_four = swapped(choose(scalars, [key_two, key_three, key_one]), 1)
    value_four = swapped(choose(scalars, [value_two, value_three, value_one]), 1)

    queries, keys, values, seg_own, resid, gain, routes_held, gates_held = mine
    mixed, keep, send, weight = attention(
        scalars,
        queries,
        [
            keys, values, key_one, value_one, key_two, value_two, key_three, value_three,
            key_four, value_four,
        ],
        seg_own, resid, gain, routes_held, gates_held,
    )
    up_held, down_held = fetch(w_up, weight), fetch(w_down, weight)
    partner = [(i, (i + shard_count) % count) for i in range(count)]
    masks = list(range(2, shard_count, 2))[::-1]
    got = lax.ppermute(send, "expert", partner)

    def spread(block):
        return [block] + [swapped(block, mask) for mask in masks]

    def both_cores(blocks):
        local = pile(blocks)
        return local, swapped(local, 1)

    def summed(parts):
        return add_split(parts[0], swapped(parts[1], 1), 1 + len(masks))

    def scattered(blocks):
        moved = [swapped(block, mask) for block, mask in zip(blocks[1:], masks)]
        return [blocks[0]] + moved[::-1]

    early_blocks = spread(keep)
    early_blocks, got, up_held, down_held = lax.optimization_barrier(
        (early_blocks, got, up_held, down_held)
    )
    held = [gate_held, up_held, down_held]
    early_parts = experts(*both_cores(early_blocks), *held)
    late_blocks = spread(got)
    late_blocks, _ = lax.optimization_barrier((late_blocks, early_parts))
    late_local = pile(late_blocks)
    early_blocks = scattered(summed(early_parts))
    late_parts = experts(late_local, swapped(late_local, 1), *held)
    late_parts, early_blocks = lax.optimization_barrier((late_parts, early_blocks))
    back = total_of(scattered(summed(late_parts)))
    other = lax.ppermute(back, "expert", partner)
    base = combine(0, mixed, weight, early_blocks, pltpu.VMEM(mixed.shape, jnp.float32))
    return combine(
        1, base, weight, [other], jax.ShapeDtypeStruct(mixed.shape, jnp.bfloat16)
    )


def solution(mesh):
    placed = (
        P(("groups", "expert"), None),
        P(("groups", "expert"), None),
        P(("groups", "expert"), None),
        P(("groups", "expert"), None),
        P(("groups", "expert")),
        P(),
        P(("groups", "expert"), None),
        P(("groups", "expert"), None),
        P(None, "expert"),
        P(None, "expert"),
        P("expert", None),
    )
    return jax.shard_map(
        shards, mesh=mesh, in_specs=placed, out_specs=P(("groups", "expert"), None), check_vma=False
    )
```

```python
import functools

import jax
import jax.numpy as jnp
from jax import lax
from jax.experimental import pallas as pl
from jax.experimental.pallas import tpu as pltpu
from jax.sharding import PartitionSpec as P

HEAD_DIM = 128
E_WIN = 2
WIN_DEV = 3
BLOCKS = 5
CAP = 20
SPARE = 16
HEADS_STEP = 16
MASKED = -1e30
MIB = 1024 * 1024


def far(x):
    return pltpu.with_memory_space_constraint(x, pltpu.HBM)


def close(x):
    return pltpu.with_memory_space_constraint(x, pltpu.VMEM)


NEAR = pl.BlockSpec(memory_space=pltpu.VMEM)


def bundle_kernel(keys, segs, out):
    rows, width = keys.shape
    out[:, :width] = keys[...]
    out[:, width:] = jnp.zeros((rows, HEAD_DIM), keys.dtype)
    out[:SPARE, width : width + rows] = jnp.broadcast_to(
        segs[...].astype(jnp.float32), (SPARE, rows)
    ).astype(keys.dtype)


def bundle(keys, segs):
    rows, width = keys.shape
    return pl.pallas_call(
        bundle_kernel,
        in_specs=[NEAR, NEAR],
        out_specs=NEAR,
        out_shape=pltpu.VMEM((rows, width + HEAD_DIM), keys.dtype),
        cost_estimate=pl.CostEstimate(
            flops=0, bytes_accessed=4 * rows * width, transcendentals=0
        ),
        compiler_params=pltpu.CompilerParams(vmem_limit_bytes=6 * MIB),
        name="bundle",
    )(far(keys), far(segs))


def choose_kernel(flags, first, second, third, out):
    for value, block in enumerate((first, second, third)):

        @pl.when(flags[6] == value)
        def _():
            out[...] = block[...]


def choose(flags, blocks):
    return pl.pallas_call(
        choose_kernel,
        in_specs=[pl.BlockSpec(memory_space=pltpu.SMEM)] + [NEAR] * 3,
        out_specs=NEAR,
        out_shape=jax.ShapeDtypeStruct(blocks[0].shape, blocks[0].dtype),
        compiler_params=pltpu.CompilerParams(vmem_limit_bytes=6 * MIB),
        name="choose",
    )(flags, *[close(block) for block in blocks])


def attention_kernel(
    deltas, q, k0, v0, k1, v1, k2, v2, k3, v3, k4, v4, seg0, resid, gain, routes, gates,
    mixed_out, keep_out, send_out, weight_out,
):
    rows, model = q.shape
    keys = BLOCKS * rows
    width = HEADS_STEP * HEAD_DIM

    seg_own = seg0[...].astype(jnp.float32)
    seg_row = jnp.concatenate(
        [seg_own]
        + [block[:SPARE, model:][0:1, :rows].astype(jnp.float32) for block in (k1, k2, k3, k4)],
        axis=1,
    )
    eye = lax.broadcasted_iota(jnp.int32, (rows, rows), 0) == lax.broadcasted_iota(
        jnp.int32, (rows, rows), 1
    )
    seg_col = jnp.sum(jnp.where(eye, seg_own, 0.0), axis=1, keepdims=True)
    lane = lax.broadcasted_iota(jnp.int32, (rows, keys), 1)
    sub = lax.broadcasted_iota(jnp.int32, (rows, keys), 0)
    block = lane // rows
    back = jnp.zeros_like(block)
    for at in range(1, BLOCKS):
        back = jnp.where(block == at, deltas[at], back)
    distance = sub - (lane - block * rows) + back * rows
    allowed = (distance >= 0) & (distance <= WIN_DEV * rows) & (seg_col == seg_row)
    bias = jnp.where(allowed, 0.0, MASKED)
    scale = 1.0 / HEAD_DIM**0.5
    heads = [slice(head * HEAD_DIM, (head + 1) * HEAD_DIM) for head in range(HEADS_STEP)]

    @pl.loop(0, model // width)
    def _(step):
        at = pl.ds(pl.multiple_of(step * width, width), width)
        query = q[:, at]
        key = jnp.concatenate([k0[:, at], k1[:, at], k2[:, at], k3[:, at], k4[:, at]], axis=0)
        value = jnp.concatenate([v0[:, at], v1[:, at], v2[:, at], v3[:, at], v4[:, at]], axis=0)
        scores = jnp.stack(
            [
                lax.dot_general(
                    query[:, cols], key[:, cols], (((1,), (1,)), ((), ())),
                    preferred_element_type=jnp.float32,
                )
                for cols in heads
            ]
        )
        scores = scores * scale + bias[None]
        expo = jnp.exp(scores - jnp.max(scores, axis=2, keepdims=True))
        denom = jnp.sum(expo, axis=2, keepdims=True)
        probs = expo.astype(jnp.bfloat16)
        outs = [
            jnp.dot(probs[head], value[:, cols], preferred_element_type=jnp.float32)
            / denom[head]
            for head, cols in enumerate(heads)
        ]
        mixed_out[:, at] = resid[:, at].astype(jnp.float32) + jnp.concatenate(outs, axis=1)

    mixed = mixed_out[...]
    normed = (
        mixed * lax.rsqrt(jnp.mean(mixed * mixed, axis=1, keepdims=True) + 1e-05) * gain[...]
    ).astype(jnp.bfloat16)
    across = lax.broadcasted_iota(jnp.int32, (rows, rows), 1)
    down = lax.broadcasted_iota(jnp.int32, (rows, rows), 0)
    upper = jnp.where(down < across, 1.0, 0.0).astype(jnp.bfloat16)
    eye = jnp.where(down == across, 1.0, 0.0).astype(jnp.bfloat16)
    slot = lax.broadcasted_iota(jnp.int32, (32, rows), 0)

    def picks(expert):
        hit = routes[...] == expert
        member = jnp.max(jnp.where(hit, 1.0, 0.0), axis=0, keepdims=True)
        weight = jnp.sum(
            jnp.where(hit, gates[...].astype(jnp.float32), 0.0), axis=0, keepdims=True
        )
        rank = jnp.dot(
            jnp.broadcast_to(member, (8, rows)).astype(jnp.bfloat16),
            upper,
            preferred_element_type=jnp.float32,
        )[0:1].astype(jnp.int32)
        return member > 0.5, weight, rank

    def spread(pick, weight):
        return lax.dot_general(
            eye,
            jnp.where(pick, weight, 0.0).astype(jnp.bfloat16),
            (((1,), (1,)), ((), ())),
            preferred_element_type=jnp.float32,
        ).astype(jnp.bfloat16)

    def packed(pick):
        return jnp.dot(
            jnp.where(pick, 1.0, 0.0).astype(jnp.bfloat16),
            normed,
            preferred_element_type=jnp.float32,
        ).astype(jnp.bfloat16)

    for place, out in ((0, keep_out), (1, send_out)):
        member, weight, rank = picks(deltas[5] if place == 0 else 1 - deltas[5])
        pick = (slot == rank) & member
        out[...] = packed(pick)[:CAP]
        weight_out[place] = spread(pick, weight)


def attention(deltas, q, pairs, seg_own, resid, gain, routes, gates):
    rows, width = q.shape
    return pl.pallas_call(
        attention_kernel,
        in_specs=[pl.BlockSpec(memory_space=pltpu.SMEM)] + [NEAR] * (6 + len(pairs)),
        out_specs=[NEAR] * 4,
        out_shape=[
            pltpu.VMEM((rows, width), jnp.float32),
            jax.ShapeDtypeStruct((CAP, width), jnp.bfloat16),
            jax.ShapeDtypeStruct((CAP, width), jnp.bfloat16),
            jax.ShapeDtypeStruct((E_WIN, rows, 32), jnp.bfloat16),
        ],
        compiler_params=pltpu.CompilerParams(vmem_limit_bytes=18 * MIB),
        cost_estimate=pl.CostEstimate(
            flops=4 * rows * BLOCKS * rows * width, bytes_accessed=8 * rows * width * 4,
            transcendentals=rows * BLOCKS * rows * (width // HEAD_DIM),
        ),
        name="attention",
    )(
        deltas, close(q), close(pairs[0]), close(pairs[1]), *pairs[2:], close(seg_own),
        close(resid), close(gain), close(routes), close(gates),
    )


def bring_kernel(count, *refs):
    sources, held, sems = refs[:count], refs[count + 1 : 2 * count + 1], refs[-1]
    copies = [
        pltpu.make_async_copy(source, target, sems.at[at])
        for at, (source, target) in enumerate(zip(sources, held))
    ]
    for copy in copies:
        copy.start()
    for copy in copies:
        copy.wait()


def bring(arrays, after):
    count = len(arrays)
    anywhere = pl.BlockSpec(memory_space=pl.ANY)
    return pl.pallas_call(
        functools.partial(bring_kernel, count),
        in_specs=[anywhere] * (count + 1),
        out_specs=[NEAR] * count,
        out_shape=[pltpu.VMEM(x.shape, x.dtype) for x in arrays],
        scratch_shapes=[pltpu.SemaphoreType.DMA((count,))],
        compiler_params=pltpu.CompilerParams(vmem_limit_bytes=2 * MIB),
        cost_estimate=pl.CostEstimate(
            flops=0, bytes_accessed=4 * sum(x.size for x in arrays), transcendentals=0
        ),
        name="bring",
    )(*[far(x) for x in arrays], after)


def fetch_kernel(parts, source, after, held, sems):
    depth = source.shape[0] // parts
    copies = []
    for part in range(parts):
        at = pl.ds(part * depth, depth)
        copies.append(pltpu.make_async_copy(source.at[at], held.at[at], sems.at[part]))
    for copy in copies:
        copy.start()
    for copy in copies:
        copy.wait()


def fetch(weights, after):
    parts = 4
    anywhere = pl.BlockSpec(memory_space=pl.ANY)
    return pl.pallas_call(
        functools.partial(fetch_kernel, parts),
        in_specs=[anywhere, anywhere],
        out_specs=NEAR,
        out_shape=pltpu.VMEM(weights.shape, weights.dtype),
        scratch_shapes=[pltpu.SemaphoreType.DMA((parts,))],
        compiler_params=pltpu.CompilerParams(vmem_limit_bytes=2 * MIB),
        cost_estimate=pl.CostEstimate(
            flops=0, bytes_accessed=4 * weights.size, transcendentals=0
        ),
        name="fetch",
    )(far(weights), after)


def experts_kernel(local, remote, w_gate, w_up, w_down, local_out, remote_out, x, hidden):
    width, units = w_gate.shape
    tile = min(1024, units)
    rows = local.shape[0]
    x[:rows] = local[...]
    x[rows:] = remote[...]

    @pl.loop(0, units // tile)
    def _(part):
        at = pl.ds(pl.multiple_of(part * tile, tile), tile)
        gate = jnp.dot(x[...], w_gate[:, at], preferred_element_type=jnp.float32)
        up = jnp.dot(x[...], w_up[:, at], preferred_element_type=jnp.float32)
        hidden[:, at] = (jax.nn.silu(gate) * up).astype(jnp.bfloat16)

    @pl.loop(0, width // 2048)
    def _(part):
        at = pl.ds(pl.multiple_of(part * 2048, 2048), 2048)
        out = jnp.dot(hidden[...], w_down[:, at], preferred_element_type=jnp.float32)
        local_out[:, at] = out[:rows].astype(jnp.bfloat16)
        remote_out[:, at] = out[rows:].astype(jnp.bfloat16)


def experts(local, remote, w_gate, w_up, w_down):
    rows, width = local.shape
    units = w_gate.shape[1]
    return pl.pallas_call(
        experts_kernel,
        in_specs=[NEAR] * 5,
        out_specs=[NEAR] * 2,
        out_shape=[jax.ShapeDtypeStruct((rows, width), jnp.bfloat16)] * 2,
        scratch_shapes=[
            pltpu.VMEM((2 * rows, width), jnp.bfloat16),
            pltpu.VMEM((2 * rows, units), jnp.bfloat16),
        ],
        compiler_params=pltpu.CompilerParams(vmem_limit_bytes=20 * MIB),
        cost_estimate=pl.CostEstimate(
            flops=12 * rows * width * units,
            bytes_accessed=8 * rows * width,
            transcendentals=2 * rows * units,
        ),
        name="experts",
    )(local, remote, close(w_gate), close(w_up), close(w_down))


def pile_kernel(*refs):
    blocks, out = refs[:-1], refs[-1]
    out[...] = jnp.concatenate(
        [block[...].astype(jnp.float32) for block in blocks], axis=0
    ).astype(out.dtype)


def pile(blocks):
    rows, width = blocks[0].shape
    return pl.pallas_call(
        pile_kernel,
        in_specs=[NEAR] * len(blocks),
        out_specs=NEAR,
        out_shape=jax.ShapeDtypeStruct((len(blocks) * rows, width), blocks[0].dtype),
        compiler_params=pltpu.CompilerParams(vmem_limit_bytes=(4 + len(blocks)) * MIB),
        name="pile",
    )(*blocks)


def add_kernel(first, second, *outs):
    rows = outs[0].shape[0]
    total = first[...].astype(jnp.float32) + second[...].astype(jnp.float32)
    for at, out in enumerate(outs):
        out[...] = total[at * rows : (at + 1) * rows].astype(out.dtype)


def add_split(first, second, blocks):
    rows, width = first.shape
    each = rows // blocks
    return pl.pallas_call(
        add_kernel,
        in_specs=[NEAR, NEAR],
        out_specs=[NEAR] * blocks,
        out_shape=[jax.ShapeDtypeStruct((each, width), first.dtype)] * blocks,
        compiler_params=pltpu.CompilerParams(vmem_limit_bytes=(6 + blocks) * MIB),
        name="add_split",
    )(first, second)


def total(blocks):
    result = blocks[0][...].astype(jnp.float32)
    for block in blocks[1:]:
        result = result + block[...].astype(jnp.float32)
    return result.astype(jnp.bfloat16)


def total_kernel(*refs):
    refs[-1][...] = total(refs[:-1])


def total_of(blocks):
    return pl.pallas_call(
        total_kernel,
        in_specs=[NEAR] * len(blocks),
        out_specs=NEAR,
        out_shape=jax.ShapeDtypeStruct(blocks[0].shape, blocks[0].dtype),
        compiler_params=pltpu.CompilerParams(vmem_limit_bytes=(4 + len(blocks)) * MIB),
        name="total",
    )(*blocks)


def combine_kernel(place, base, weight, *refs):
    blocks, out = refs[:-1], refs[-1]
    part = jnp.dot(
        weight[place][:, :CAP], total(blocks), preferred_element_type=jnp.float32
    )
    out[...] = (base[...] + part).astype(out.dtype)


def combine(place, base, weight, blocks, result):
    return pl.pallas_call(
        functools.partial(combine_kernel, place),
        in_specs=[NEAR] * (2 + len(blocks)),
        out_specs=NEAR,
        out_shape=result,
        compiler_params=pltpu.CompilerParams(vmem_limit_bytes=(8 + len(blocks)) * MIB),
        name="combine",
    )(close(base), weight, *blocks)


def shards(
    resid, queries, keys, values, segment_ids, norm_gain, routes, route_gates, w_gate, w_up, w_down
):
    count = lax.axis_size("expert")
    own = lax.axis_index("expert")
    shard_count = count // E_WIN

    place = own % 4

    def moved(block, steps):
        pairs = [(i, i + steps[i % 4]) for i in range(count) if i % 4 in steps]
        return lax.ppermute(block, "expert", [pair for pair in pairs if pair[1] < count])

    across = {0: 3, 1: 3, 2: -1, 3: 3}
    passed = {1: 4, 2: -2}
    beside = {0: 1, 1: 1, 2: 1}

    def swapped(block, mask):
        return lax.ppermute(block, "expert", [(i, i ^ mask) for i in range(count)])

    seg_own = segment_ids.reshape(1, -1)
    beyond = 2 * WIN_DEV + 2
    delta_list = [
        0 * own,
        jnp.where(place == 1, beyond, 3),
        jnp.where(place == 0, 1, jnp.where(place == 1, 3, beyond)),
        jnp.where(place == 0, beyond, 1),
        0 * own + 2,
    ]
    my_expert = own // shard_count
    source = jnp.where(place < 2, 0, jnp.where(place == 2, 1, 2))
    scalars = jnp.stack(
        [jnp.where(own >= delta, delta, beyond) for delta in delta_list] + [my_expert, source]
    ).astype(jnp.int32)

    key_block = bundle(keys, seg_own)
    key_one, value_one = moved(key_block, across), moved(values, across)
    key_three, value_three = moved(key_block, beside), moved(values, beside)
    mine = bring(
        [
            queries, keys, values, seg_own, resid, norm_gain.reshape(1, -1), routes.T,
            route_gates.T,
        ],
        scalars,
    )
    gate_held = fetch(w_gate, scalars)
    key_two = moved(key_one, passed)
    value_one, gate_held, mine = lax.optimization_barrier((value_one, gate_held, mine))
    value_two = moved(value_one, passed)
    key_four = swapped(choose(scalars, [key_two, key_three, key_one]), 1)
    value_four = swapped(choose(scalars, [value_two, value_three, value_one]), 1)

    queries, keys, values, seg_own, resid, gain, routes_held, gates_held = mine
    mixed, keep, send, weight = attention(
        scalars,
        queries,
        [
            keys, values, key_one, value_one, key_two, value_two, key_three, value_three,
            key_four, value_four,
        ],
        seg_own, resid, gain, routes_held, gates_held,
    )
    up_held, down_held = fetch(w_up, weight), fetch(w_down, weight)
    partner = [(i, (i + shard_count) % count) for i in range(count)]
    masks = list(range(2, shard_count, 2))[::-1]
    got = lax.ppermute(send, "expert", partner)

    def spread(block):
        return [block] + [swapped(block, mask) for mask in masks]

    def both_cores(blocks):
        local = pile(blocks)
        return local, swapped(local, 1)

    def summed(parts):
        return add_split(parts[0], swapped(parts[1], 1), 1 + len(masks))

    def scattered(blocks):
        moved = [swapped(block, mask) for block, mask in zip(blocks[1:], masks)]
        return [blocks[0]] + moved[::-1]

    early_blocks = spread(keep)
    early_blocks, got, up_held, down_held = lax.optimization_barrier(
        (early_blocks, got, up_held, down_held)
    )
    held = [gate_held, up_held, down_held]
    early_parts = experts(*both_cores(early_blocks), *held)
    late_blocks = spread(got)
    late_blocks, early_parts = lax.optimization_barrier((late_blocks, early_parts))
    late_blocks = summed(experts(*both_cores(late_blocks), *held))
    early_blocks = summed(early_parts)
    late_blocks, early_blocks = lax.optimization_barrier((late_blocks, early_blocks))
    late_blocks = scattered(late_blocks)
    late_blocks[:-1], early_blocks = lax.optimization_barrier((late_blocks[:-1], early_blocks))
    early_blocks = scattered(early_blocks)
    back = total_of(late_blocks)
    other = lax.ppermute(back, "expert", partner)
    base = combine(0, mixed, weight, early_blocks, pltpu.VMEM(mixed.shape, jnp.float32))
    return combine(
        1, base, weight, [other], jax.ShapeDtypeStruct(mixed.shape, jnp.bfloat16)
    )


def solution(mesh):
    placed = (
        P(("groups", "expert"), None),
        P(("groups", "expert"), None),
        P(("groups", "expert"), None),
        P(("groups", "expert"), None),
        P(("groups", "expert")),
        P(),
        P(("groups", "expert"), None),
        P(("groups", "expert"), None),
        P(None, "expert"),
        P(None, "expert"),
        P("expert", None),
    )
    return jax.shard_map(
        shards, mesh=mesh, in_specs=placed, out_specs=P(("groups", "expert"), None), check_vma=False
    )
```

```python
import functools

import jax
import jax.numpy as jnp
from jax import lax
from jax.experimental import pallas as pl
from jax.experimental.pallas import tpu as pltpu
from jax.sharding import PartitionSpec as P

HEAD_DIM = 128
E_WIN = 2
WIN_DEV = 3
BLOCKS = 5
CAP = 20
SPARE = 16
HEADS_STEP = 32
MASKED = -1e30
MIB = 1024 * 1024


def far(x):
    return pltpu.with_memory_space_constraint(x, pltpu.HBM)


def close(x):
    return pltpu.with_memory_space_constraint(x, pltpu.VMEM)


NEAR = pl.BlockSpec(memory_space=pltpu.VMEM)


def bundle_kernel(keys, segs, out):
    rows, width = keys.shape
    out[:, :width] = keys[...]
    out[:, width:] = jnp.zeros((rows, HEAD_DIM), keys.dtype)
    out[:SPARE, width : width + rows] = jnp.broadcast_to(
        segs[...].astype(jnp.float32), (SPARE, rows)
    ).astype(keys.dtype)


def bundle(keys, segs):
    rows, width = keys.shape
    return pl.pallas_call(
        bundle_kernel,
        in_specs=[NEAR, NEAR],
        out_specs=NEAR,
        out_shape=pltpu.VMEM((rows, width + HEAD_DIM), keys.dtype),
        cost_estimate=pl.CostEstimate(
            flops=0, bytes_accessed=4 * rows * width, transcendentals=0
        ),
        compiler_params=pltpu.CompilerParams(vmem_limit_bytes=6 * MIB),
        name="bundle",
    )(far(keys), far(segs))


def choose_kernel(flags, first, second, third, out):
    for value, block in enumerate((first, second, third)):

        @pl.when(flags[6] == value)
        def _():
            out[...] = block[...]


def choose(flags, blocks):
    return pl.pallas_call(
        choose_kernel,
        in_specs=[pl.BlockSpec(memory_space=pltpu.SMEM)] + [NEAR] * 3,
        out_specs=NEAR,
        out_shape=jax.ShapeDtypeStruct(blocks[0].shape, blocks[0].dtype),
        compiler_params=pltpu.CompilerParams(vmem_limit_bytes=6 * MIB),
        name="choose",
    )(flags, *[close(block) for block in blocks])


def attention_kernel(
    deltas, q, k0, v0, k1, v1, k2, v2, k3, v3, k4, v4, seg0, resid, gain, routes, gates,
    mixed_out, keep_out, send_out, weight_out,
):
    rows, model = q.shape
    keys = BLOCKS * rows
    width = HEADS_STEP * HEAD_DIM

    seg_own = seg0[...].astype(jnp.float32)
    seg_row = jnp.concatenate(
        [seg_own]
        + [block[:SPARE, model:][0:1, :rows].astype(jnp.float32) for block in (k1, k2, k3, k4)],
        axis=1,
    )
    eye = lax.broadcasted_iota(jnp.int32, (rows, rows), 0) == lax.broadcasted_iota(
        jnp.int32, (rows, rows), 1
    )
    seg_col = jnp.sum(jnp.where(eye, seg_own, 0.0), axis=1, keepdims=True)
    lane = lax.broadcasted_iota(jnp.int32, (rows, keys), 1)
    sub = lax.broadcasted_iota(jnp.int32, (rows, keys), 0)
    block = lane // rows
    back = jnp.zeros_like(block)
    for at in range(1, BLOCKS):
        back = jnp.where(block == at, deltas[at], back)
    distance = sub - (lane - block * rows) + back * rows
    allowed = (distance >= 0) & (distance <= WIN_DEV * rows) & (seg_col == seg_row)
    bias = jnp.where(allowed, 0.0, MASKED)
    scale = 1.0 / HEAD_DIM**0.5
    heads = [slice(head * HEAD_DIM, (head + 1) * HEAD_DIM) for head in range(HEADS_STEP)]

    @pl.loop(0, model // width)
    def _(step):
        at = pl.ds(pl.multiple_of(step * width, width), width)
        query = q[:, at]
        key = jnp.concatenate([k0[:, at], k1[:, at], k2[:, at], k3[:, at], k4[:, at]], axis=0)
        value = jnp.concatenate([v0[:, at], v1[:, at], v2[:, at], v3[:, at], v4[:, at]], axis=0)
        scores = jnp.stack(
            [
                lax.dot_general(
                    query[:, cols], key[:, cols], (((1,), (1,)), ((), ())),
                    preferred_element_type=jnp.float32,
                )
                for cols in heads
            ]
        )
        scores = scores * scale + bias[None]
        expo = jnp.exp(scores - jnp.max(scores, axis=2, keepdims=True))
        denom = jnp.sum(expo, axis=2, keepdims=True)
        probs = expo.astype(jnp.bfloat16)
        outs = [
            jnp.dot(probs[head], value[:, cols], preferred_element_type=jnp.float32)
            / denom[head]
            for head, cols in enumerate(heads)
        ]
        mixed_out[:, at] = resid[:, at].astype(jnp.float32) + jnp.concatenate(outs, axis=1)

    mixed = mixed_out[...]
    normed = (
        mixed * lax.rsqrt(jnp.mean(mixed * mixed, axis=1, keepdims=True) + 1e-05) * gain[...]
    ).astype(jnp.bfloat16)
    across = lax.broadcasted_iota(jnp.int32, (rows, rows), 1)
    down = lax.broadcasted_iota(jnp.int32, (rows, rows), 0)
    upper = jnp.where(down < across, 1.0, 0.0).astype(jnp.bfloat16)
    eye = jnp.where(down == across, 1.0, 0.0).astype(jnp.bfloat16)
    slot = lax.broadcasted_iota(jnp.int32, (32, rows), 0)

    def picks(expert):
        hit = routes[...] == expert
        member = jnp.max(jnp.where(hit, 1.0, 0.0), axis=0, keepdims=True)
        weight = jnp.sum(
            jnp.where(hit, gates[...].astype(jnp.float32), 0.0), axis=0, keepdims=True
        )
        rank = jnp.dot(
            jnp.broadcast_to(member, (8, rows)).astype(jnp.bfloat16),
            upper,
            preferred_element_type=jnp.float32,
        )[0:1].astype(jnp.int32)
        return member > 0.5, weight, rank

    def spread(pick, weight):
        return lax.dot_general(
            eye,
            jnp.where(pick, weight, 0.0).astype(jnp.bfloat16),
            (((1,), (1,)), ((), ())),
            preferred_element_type=jnp.float32,
        ).astype(jnp.bfloat16)

    def packed(pick):
        return jnp.dot(
            jnp.where(pick, 1.0, 0.0).astype(jnp.bfloat16),
            normed,
            preferred_element_type=jnp.float32,
        ).astype(jnp.bfloat16)

    for place, out in ((0, keep_out), (1, send_out)):
        member, weight, rank = picks(deltas[5] if place == 0 else 1 - deltas[5])
        pick = (slot == rank) & member
        out[...] = packed(pick)[:CAP]
        weight_out[place] = spread(pick, weight)


def attention(deltas, q, pairs, seg_own, resid, gain, routes, gates):
    rows, width = q.shape
    return pl.pallas_call(
        attention_kernel,
        in_specs=[pl.BlockSpec(memory_space=pltpu.SMEM)] + [NEAR] * (6 + len(pairs)),
        out_specs=[NEAR] * 4,
        out_shape=[
            pltpu.VMEM((rows, width), jnp.float32),
            jax.ShapeDtypeStruct((CAP, width), jnp.bfloat16),
            jax.ShapeDtypeStruct((CAP, width), jnp.bfloat16),
            jax.ShapeDtypeStruct((E_WIN, rows, 32), jnp.bfloat16),
        ],
        compiler_params=pltpu.CompilerParams(vmem_limit_bytes=18 * MIB),
        cost_estimate=pl.CostEstimate(
            flops=4 * rows * BLOCKS * rows * width, bytes_accessed=8 * rows * width * 4,
            transcendentals=rows * BLOCKS * rows * (width // HEAD_DIM),
        ),
        name="attention",
    )(
        deltas, close(q), close(pairs[0]), close(pairs[1]), *pairs[2:], close(seg_own),
        close(resid), close(gain), close(routes), close(gates),
    )


def bring_kernel(count, *refs):
    sources, held, sems = refs[:count], refs[count + 1 : 2 * count + 1], refs[-1]
    copies = [
        pltpu.make_async_copy(source, target, sems.at[at])
        for at, (source, target) in enumerate(zip(sources, held))
    ]
    for copy in copies:
        copy.start()
    for copy in copies:
        copy.wait()


def bring(arrays, after):
    count = len(arrays)
    anywhere = pl.BlockSpec(memory_space=pl.ANY)
    return pl.pallas_call(
        functools.partial(bring_kernel, count),
        in_specs=[anywhere] * (count + 1),
        out_specs=[NEAR] * count,
        out_shape=[pltpu.VMEM(x.shape, x.dtype) for x in arrays],
        scratch_shapes=[pltpu.SemaphoreType.DMA((count,))],
        compiler_params=pltpu.CompilerParams(vmem_limit_bytes=2 * MIB),
        cost_estimate=pl.CostEstimate(
            flops=0, bytes_accessed=4 * sum(x.size for x in arrays), transcendentals=0
        ),
        name="bring",
    )(*[far(x) for x in arrays], after)


def fetch_kernel(parts, source, after, held, sems):
    depth = source.shape[0] // parts
    copies = []
    for part in range(parts):
        at = pl.ds(part * depth, depth)
        copies.append(pltpu.make_async_copy(source.at[at], held.at[at], sems.at[part]))
    for copy in copies:
        copy.start()
    for copy in copies:
        copy.wait()


def fetch(weights, after):
    parts = 4
    anywhere = pl.BlockSpec(memory_space=pl.ANY)
    return pl.pallas_call(
        functools.partial(fetch_kernel, parts),
        in_specs=[anywhere, anywhere],
        out_specs=NEAR,
        out_shape=pltpu.VMEM(weights.shape, weights.dtype),
        scratch_shapes=[pltpu.SemaphoreType.DMA((parts,))],
        compiler_params=pltpu.CompilerParams(vmem_limit_bytes=2 * MIB),
        cost_estimate=pl.CostEstimate(
            flops=0, bytes_accessed=4 * weights.size, transcendentals=0
        ),
        name="fetch",
    )(far(weights), after)


def experts_kernel(local, remote, w_gate, w_up, w_down, local_out, remote_out, x, hidden):
    width, units = w_gate.shape
    tile = min(1024, units)
    rows = local.shape[0]
    x[:rows] = local[...]
    x[rows:] = remote[...]

    @pl.loop(0, units // tile)
    def _(part):
        at = pl.ds(pl.multiple_of(part * tile, tile), tile)
        gate = jnp.dot(x[...], w_gate[:, at], preferred_element_type=jnp.float32)
        up = jnp.dot(x[...], w_up[:, at], preferred_element_type=jnp.float32)
        hidden[:, at] = (jax.nn.silu(gate) * up).astype(jnp.bfloat16)

    out = jnp.dot(hidden[...], w_down[...], preferred_element_type=jnp.float32)
    local_out[...] = out[:rows].astype(jnp.bfloat16)
    remote_out[...] = out[rows:].astype(jnp.bfloat16)


def experts(local, remote, w_gate, w_up, w_down):
    rows, width = local.shape
    units = w_gate.shape[1]
    return pl.pallas_call(
        experts_kernel,
        in_specs=[NEAR] * 5,
        out_specs=[NEAR] * 2,
        out_shape=[jax.ShapeDtypeStruct((rows, width), jnp.bfloat16)] * 2,
        scratch_shapes=[
            pltpu.VMEM((2 * rows, width), jnp.bfloat16),
            pltpu.VMEM((2 * rows, units), jnp.bfloat16),
        ],
        compiler_params=pltpu.CompilerParams(vmem_limit_bytes=20 * MIB),
        cost_estimate=pl.CostEstimate(
            flops=12 * rows * width * units,
            bytes_accessed=8 * rows * width,
            transcendentals=2 * rows * units,
        ),
        name="experts",
    )(local, remote, close(w_gate), close(w_up), close(w_down))


def pile_kernel(*refs):
    blocks, out = refs[:-1], refs[-1]
    out[...] = jnp.concatenate(
        [block[...].astype(jnp.float32) for block in blocks], axis=0
    ).astype(out.dtype)


def pile(blocks):
    rows, width = blocks[0].shape
    return pl.pallas_call(
        pile_kernel,
        in_specs=[NEAR] * len(blocks),
        out_specs=NEAR,
        out_shape=jax.ShapeDtypeStruct((len(blocks) * rows, width), blocks[0].dtype),
        compiler_params=pltpu.CompilerParams(vmem_limit_bytes=(4 + len(blocks)) * MIB),
        name="pile",
    )(*blocks)


def add_kernel(first, second, *outs):
    rows = outs[0].shape[0]
    total = first[...].astype(jnp.float32) + second[...].astype(jnp.float32)
    for at, out in enumerate(outs):
        out[...] = total[at * rows : (at + 1) * rows].astype(out.dtype)


def add_split(first, second, blocks):
    rows, width = first.shape
    each = rows // blocks
    return pl.pallas_call(
        add_kernel,
        in_specs=[NEAR, NEAR],
        out_specs=[NEAR] * blocks,
        out_shape=[jax.ShapeDtypeStruct((each, width), first.dtype)] * blocks,
        compiler_params=pltpu.CompilerParams(vmem_limit_bytes=(6 + blocks) * MIB),
        name="add_split",
    )(first, second)


def total(blocks):
    result = blocks[0][...].astype(jnp.float32)
    for block in blocks[1:]:
        result = result + block[...].astype(jnp.float32)
    return result.astype(jnp.bfloat16)


def total_kernel(*refs):
    refs[-1][...] = total(refs[:-1])


def total_of(blocks):
    return pl.pallas_call(
        total_kernel,
        in_specs=[NEAR] * len(blocks),
        out_specs=NEAR,
        out_shape=jax.ShapeDtypeStruct(blocks[0].shape, blocks[0].dtype),
        compiler_params=pltpu.CompilerParams(vmem_limit_bytes=(4 + len(blocks)) * MIB),
        name="total",
    )(*blocks)


def combine_kernel(place, base, weight, *refs):
    blocks, out = refs[:-1], refs[-1]
    part = jnp.dot(
        weight[place][:, :CAP], total(blocks), preferred_element_type=jnp.float32
    )
    out[...] = (base[...] + part).astype(out.dtype)


def combine(place, base, weight, blocks, result):
    return pl.pallas_call(
        functools.partial(combine_kernel, place),
        in_specs=[NEAR] * (2 + len(blocks)),
        out_specs=NEAR,
        out_shape=result,
        compiler_params=pltpu.CompilerParams(vmem_limit_bytes=(8 + len(blocks)) * MIB),
        name="combine",
    )(close(base), weight, *blocks)


def finish_kernel(parts, base, weight, other, out, held, sems):
    width = base.shape[1] // parts
    copies = []
    for part in range(parts):
        at = pl.ds(part * width, width)
        held[:, at] = (
            base[:, at]
            + jnp.dot(weight[1][:, :CAP], other[:, at], preferred_element_type=jnp.float32)
        ).astype(held.dtype)
        copies.append(pltpu.make_async_copy(held.at[:, at], out.at[:, at], sems.at[part]))
        copies[-1].start()
    for copy in copies:
        copy.wait()


def finish(base, weight, other):
    parts = 4
    return pl.pallas_call(
        functools.partial(finish_kernel, parts),
        in_specs=[NEAR] * 3,
        out_specs=pl.BlockSpec(memory_space=pl.ANY),
        out_shape=jax.ShapeDtypeStruct(base.shape, jnp.bfloat16),
        scratch_shapes=[
            pltpu.VMEM(base.shape, jnp.bfloat16),
            pltpu.SemaphoreType.DMA((parts,)),
        ],
        compiler_params=pltpu.CompilerParams(vmem_limit_bytes=8 * MIB),
        name="finish",
    )(close(base), weight, other)


def shards(
    resid, queries, keys, values, segment_ids, norm_gain, routes, route_gates, w_gate, w_up, w_down
):
    count = lax.axis_size("expert")
    own = lax.axis_index("expert")
    shard_count = count // E_WIN

    place = own % 4

    def moved(block, steps):
        pairs = [(i, i + steps[i % 4]) for i in range(count) if i % 4 in steps]
        return lax.ppermute(block, "expert", [pair for pair in pairs if pair[1] < count])

    across = {0: 3, 1: 3, 2: -1, 3: 3}
    passed = {1: 4, 2: -2}
    beside = {0: 1, 1: 1, 2: 1}

    def swapped(block, mask):
        return lax.ppermute(block, "expert", [(i, i ^ mask) for i in range(count)])

    seg_own = segment_ids.reshape(1, -1)
    beyond = 2 * WIN_DEV + 2
    delta_list = [
        0 * own,
        jnp.where(place == 1, beyond, 3),
        jnp.where(place == 0, 1, jnp.where(place == 1, 3, beyond)),
        jnp.where(place == 0, beyond, 1),
        0 * own + 2,
    ]
    my_expert = own // shard_count
    source = jnp.where(place < 2, 0, jnp.where(place == 2, 1, 2))
    scalars = jnp.stack(
        [jnp.where(own >= delta, delta, beyond) for delta in delta_list] + [my_expert, source]
    ).astype(jnp.int32)

    key_block = bundle(keys, seg_own)
    key_one, value_one = moved(key_block, across), moved(values, across)
    key_three, value_three = moved(key_block, beside), moved(values, beside)
    mine = bring(
        [
            queries, keys, values, seg_own, resid, norm_gain.reshape(1, -1), routes.T,
            route_gates.T,
        ],
        scalars,
    )
    gate_held = fetch(w_gate, scalars)
    key_two = moved(key_one, passed)
    value_one, gate_held, mine = lax.optimization_barrier((value_one, gate_held, mine))
    value_two = moved(value_one, passed)
    key_four = swapped(choose(scalars, [key_two, key_three, key_one]), 1)
    value_four = swapped(choose(scalars, [value_two, value_three, value_one]), 1)

    queries, keys, values, seg_own, resid, gain, routes_held, gates_held = mine
    mixed, keep, send, weight = attention(
        scalars,
        queries,
        [
            keys, values, key_one, value_one, key_two, value_two, key_three, value_three,
            key_four, value_four,
        ],
        seg_own, resid, gain, routes_held, gates_held,
    )
    up_held, down_held = fetch(w_up, weight), fetch(w_down, weight)
    partner = [(i, (i + shard_count) % count) for i in range(count)]
    masks = list(range(2, shard_count, 2))[::-1]
    got = lax.ppermute(send, "expert", partner)

    def spread(block):
        return [block] + [swapped(block, mask) for mask in masks]

    def both_cores(blocks):
        local = pile(blocks)
        return local, swapped(local, 1)

    def summed(parts):
        return add_split(parts[0], swapped(parts[1], 1), 1 + len(masks))

    def scattered(blocks):
        moved = [swapped(block, mask) for block, mask in zip(blocks[1:], masks)]
        return [blocks[0]] + moved[::-1]

    early_blocks = spread(keep)
    early_blocks, got, up_held, down_held = lax.optimization_barrier(
        (early_blocks, got, up_held, down_held)
    )
    held = [gate_held, up_held, down_held]
    early_parts = experts(*both_cores(early_blocks), *held)
    late_blocks = spread(got)
    late_blocks, early_parts = lax.optimization_barrier((late_blocks, early_parts))
    late_blocks = summed(experts(*both_cores(late_blocks), *held))
    early_blocks = summed(early_parts)
    late_blocks, early_blocks = lax.optimization_barrier((late_blocks, early_blocks))
    late_blocks = scattered(late_blocks)
    late_blocks[:-1], early_blocks = lax.optimization_barrier((late_blocks[:-1], early_blocks))
    early_blocks = scattered(early_blocks)
    back = total_of(late_blocks)
    other = lax.ppermute(back, "expert", partner)
    base = combine(0, mixed, weight, early_blocks, pltpu.VMEM(mixed.shape, jnp.float32))
    return finish(base, weight, other)


def solution(mesh):
    placed = (
        P(("groups", "expert"), None),
        P(("groups", "expert"), None),
        P(("groups", "expert"), None),
        P(("groups", "expert"), None),
        P(("groups", "expert")),
        P(),
        P(("groups", "expert"), None),
        P(("groups", "expert"), None),
        P(None, "expert"),
        P(None, "expert"),
        P("expert", None),
    )
    return jax.shard_map(
        shards, mesh=mesh, in_specs=placed, out_specs=P(("groups", "expert"), None), check_vma=False
    )
```

```python
import functools

import jax
import jax.numpy as jnp
from jax import lax
from jax.experimental import pallas as pl
from jax.experimental.pallas import tpu as pltpu
from jax.sharding import PartitionSpec as P

HEAD_DIM = 128
E_WIN = 2
WIN_DEV = 3
BLOCKS = 5
CAP = 20
SPARE = 16
HEADS_STEP = 32
MASKED = -1e30
MIB = 1024 * 1024


def far(x):
    return pltpu.with_memory_space_constraint(x, pltpu.HBM)


def close(x):
    return pltpu.with_memory_space_constraint(x, pltpu.VMEM)


NEAR = pl.BlockSpec(memory_space=pltpu.VMEM)


def bundle_kernel(keys, segs, out):
    rows, width = keys.shape
    out[:, :width] = keys[...]
    out[:, width:] = jnp.zeros((rows, HEAD_DIM), keys.dtype)
    out[:SPARE, width : width + rows] = jnp.broadcast_to(
        segs[...].astype(jnp.float32), (SPARE, rows)
    ).astype(keys.dtype)


def bundle(keys, segs):
    rows, width = keys.shape
    return pl.pallas_call(
        bundle_kernel,
        in_specs=[NEAR, NEAR],
        out_specs=NEAR,
        out_shape=pltpu.VMEM((rows, width + HEAD_DIM), keys.dtype),
        cost_estimate=pl.CostEstimate(
            flops=0, bytes_accessed=4 * rows * width, transcendentals=0
        ),
        compiler_params=pltpu.CompilerParams(vmem_limit_bytes=6 * MIB),
        name="bundle",
    )(far(keys), far(segs))


def choose_kernel(flags, first, second, third, out):
    for value, block in enumerate((first, second, third)):

        @pl.when(flags[6] == value)
        def _():
            out[...] = block[...]


def choose(flags, blocks):
    return pl.pallas_call(
        choose_kernel,
        in_specs=[pl.BlockSpec(memory_space=pltpu.SMEM)] + [NEAR] * 3,
        out_specs=NEAR,
        out_shape=jax.ShapeDtypeStruct(blocks[0].shape, blocks[0].dtype),
        compiler_params=pltpu.CompilerParams(vmem_limit_bytes=6 * MIB),
        name="choose",
    )(flags, *[close(block) for block in blocks])


def attention_kernel(
    deltas, q, k0, v0, k1, v1, k2, v2, k3, v3, k4, v4, seg0, resid, gain, routes, gates,
    mixed_out, keep_out, send_out, weight_out,
):
    rows, model = q.shape
    keys = BLOCKS * rows
    width = HEADS_STEP * HEAD_DIM

    seg_own = seg0[...].astype(jnp.float32)
    seg_row = jnp.concatenate(
        [seg_own]
        + [block[:SPARE, model:][0:1, :rows].astype(jnp.float32) for block in (k1, k2, k3, k4)],
        axis=1,
    )
    eye = lax.broadcasted_iota(jnp.int32, (rows, rows), 0) == lax.broadcasted_iota(
        jnp.int32, (rows, rows), 1
    )
    seg_col = jnp.sum(jnp.where(eye, seg_own, 0.0), axis=1, keepdims=True)
    lane = lax.broadcasted_iota(jnp.int32, (rows, keys), 1)
    sub = lax.broadcasted_iota(jnp.int32, (rows, keys), 0)
    block = lane // rows
    back = jnp.zeros_like(block)
    for at in range(1, BLOCKS):
        back = jnp.where(block == at, deltas[at], back)
    distance = sub - (lane - block * rows) + back * rows
    allowed = (distance >= 0) & (distance <= WIN_DEV * rows) & (seg_col == seg_row)
    bias = jnp.where(allowed, 0.0, MASKED)
    scale = 1.0 / HEAD_DIM**0.5
    heads = [slice(head * HEAD_DIM, (head + 1) * HEAD_DIM) for head in range(HEADS_STEP)]

    @pl.loop(0, model // width)
    def _(step):
        at = pl.ds(pl.multiple_of(step * width, width), width)
        query = q[:, at]
        key = jnp.concatenate([k0[:, at], k1[:, at], k2[:, at], k3[:, at], k4[:, at]], axis=0)
        value = jnp.concatenate([v0[:, at], v1[:, at], v2[:, at], v3[:, at], v4[:, at]], axis=0)
        scores = jnp.stack(
            [
                lax.dot_general(
                    query[:, cols], key[:, cols], (((1,), (1,)), ((), ())),
                    preferred_element_type=jnp.float32,
                )
                for cols in heads
            ]
        )
        scores = scores * scale + bias[None]
        expo = jnp.exp(scores - jnp.max(scores, axis=2, keepdims=True))
        denom = jnp.sum(expo, axis=2, keepdims=True)
        probs = expo.astype(jnp.bfloat16)
        outs = [
            jnp.dot(probs[head], value[:, cols], preferred_element_type=jnp.float32)
            / denom[head]
            for head, cols in enumerate(heads)
        ]
        mixed_out[:, at] = resid[:, at].astype(jnp.float32) + jnp.concatenate(outs, axis=1)

    mixed = mixed_out[...]
    normed = (
        mixed * lax.rsqrt(jnp.mean(mixed * mixed, axis=1, keepdims=True) + 1e-05) * gain[...]
    ).astype(jnp.bfloat16)
    across = lax.broadcasted_iota(jnp.int32, (rows, rows), 1)
    down = lax.broadcasted_iota(jnp.int32, (rows, rows), 0)
    upper = jnp.where(down < across, 1.0, 0.0).astype(jnp.bfloat16)
    eye = jnp.where(down == across, 1.0, 0.0).astype(jnp.bfloat16)
    slot = lax.broadcasted_iota(jnp.int32, (32, rows), 0)

    def picks(expert):
        hit = routes[...] == expert
        member = jnp.max(jnp.where(hit, 1.0, 0.0), axis=0, keepdims=True)
        weight = jnp.sum(
            jnp.where(hit, gates[...].astype(jnp.float32), 0.0), axis=0, keepdims=True
        )
        rank = jnp.dot(
            jnp.broadcast_to(member, (8, rows)).astype(jnp.bfloat16),
            upper,
            preferred_element_type=jnp.float32,
        )[0:1].astype(jnp.int32)
        return member > 0.5, weight, rank

    def spread(pick, weight):
        return lax.dot_general(
            eye,
            jnp.where(pick, weight, 0.0).astype(jnp.bfloat16),
            (((1,), (1,)), ((), ())),
            preferred_element_type=jnp.float32,
        ).astype(jnp.bfloat16)

    def packed(pick):
        return jnp.dot(
            jnp.where(pick, 1.0, 0.0).astype(jnp.bfloat16),
            normed,
            preferred_element_type=jnp.float32,
        ).astype(jnp.bfloat16)

    for place, out in ((0, keep_out), (1, send_out)):
        member, weight, rank = picks(deltas[5] if place == 0 else 1 - deltas[5])
        pick = (slot == rank) & member
        out[...] = packed(pick)[:CAP]
        weight_out[place] = spread(pick, weight)


def attention(deltas, q, pairs, seg_own, resid, gain, routes, gates):
    rows, width = q.shape
    return pl.pallas_call(
        attention_kernel,
        in_specs=[pl.BlockSpec(memory_space=pltpu.SMEM)] + [NEAR] * (6 + len(pairs)),
        out_specs=[NEAR] * 4,
        out_shape=[
            pltpu.VMEM((rows, width), jnp.float32),
            jax.ShapeDtypeStruct((CAP, width), jnp.bfloat16),
            jax.ShapeDtypeStruct((CAP, width), jnp.bfloat16),
            jax.ShapeDtypeStruct((E_WIN, rows, 32), jnp.bfloat16),
        ],
        compiler_params=pltpu.CompilerParams(vmem_limit_bytes=18 * MIB),
        cost_estimate=pl.CostEstimate(
            flops=4 * rows * BLOCKS * rows * width, bytes_accessed=8 * rows * width * 4,
            transcendentals=rows * BLOCKS * rows * (width // HEAD_DIM),
        ),
        name="attention",
    )(
        deltas, close(q), close(pairs[0]), close(pairs[1]), *pairs[2:], close(seg_own),
        close(resid), close(gain), close(routes), close(gates),
    )


def bring_kernel(count, *refs):
    sources, held, sems = refs[:count], refs[count + 1 : 2 * count + 1], refs[-1]
    copies = [
        pltpu.make_async_copy(source, target, sems.at[at])
        for at, (source, target) in enumerate(zip(sources, held))
    ]
    for copy in copies:
        copy.start()
    for copy in copies:
        copy.wait()


def bring(arrays, after):
    count = len(arrays)
    anywhere = pl.BlockSpec(memory_space=pl.ANY)
    return pl.pallas_call(
        functools.partial(bring_kernel, count),
        in_specs=[anywhere] * (count + 1),
        out_specs=[NEAR] * count,
        out_shape=[pltpu.VMEM(x.shape, x.dtype) for x in arrays],
        scratch_shapes=[pltpu.SemaphoreType.DMA((count,))],
        compiler_params=pltpu.CompilerParams(vmem_limit_bytes=2 * MIB),
        cost_estimate=pl.CostEstimate(
            flops=0, bytes_accessed=4 * sum(x.size for x in arrays), transcendentals=0
        ),
        name="bring",
    )(*[far(x) for x in arrays], after)


def fetch_kernel(parts, source, after, held, sems):
    depth = source.shape[0] // parts
    copies = []
    for part in range(parts):
        at = pl.ds(part * depth, depth)
        copies.append(pltpu.make_async_copy(source.at[at], held.at[at], sems.at[part]))
    for copy in copies:
        copy.start()
    for copy in copies:
        copy.wait()


def fetch(weights, after):
    parts = 4
    anywhere = pl.BlockSpec(memory_space=pl.ANY)
    return pl.pallas_call(
        functools.partial(fetch_kernel, parts),
        in_specs=[anywhere, anywhere],
        out_specs=NEAR,
        out_shape=pltpu.VMEM(weights.shape, weights.dtype),
        scratch_shapes=[pltpu.SemaphoreType.DMA((parts,))],
        compiler_params=pltpu.CompilerParams(vmem_limit_bytes=2 * MIB),
        cost_estimate=pl.CostEstimate(
            flops=0, bytes_accessed=4 * weights.size, transcendentals=0
        ),
        name="fetch",
    )(far(weights), after)


def experts_kernel(local, remote, w_gate, w_up, w_down, local_out, remote_out, x, hidden):
    width, units = w_gate.shape
    tile = min(1024, units)
    rows = local.shape[0]
    x[:rows] = local[...]
    x[rows:] = remote[...]

    @pl.loop(0, units // tile)
    def _(part):
        at = pl.ds(pl.multiple_of(part * tile, tile), tile)
        gate = jnp.dot(x[...], w_gate[:, at], preferred_element_type=jnp.float32)
        up = jnp.dot(x[...], w_up[:, at], preferred_element_type=jnp.float32)
        hidden[:, at] = (jax.nn.silu(gate) * up).astype(jnp.bfloat16)

    out = jnp.dot(hidden[...], w_down[...], preferred_element_type=jnp.float32)
    local_out[...] = out[:rows].astype(jnp.bfloat16)
    remote_out[...] = out[rows:].astype(jnp.bfloat16)


def experts(local, remote, w_gate, w_up, w_down):
    rows, width = local.shape
    units = w_gate.shape[1]
    return pl.pallas_call(
        experts_kernel,
        in_specs=[NEAR] * 5,
        out_specs=[NEAR] * 2,
        out_shape=[jax.ShapeDtypeStruct((rows, width), jnp.bfloat16)] * 2,
        scratch_shapes=[
            pltpu.VMEM((2 * rows, width), jnp.bfloat16),
            pltpu.VMEM((2 * rows, units), jnp.bfloat16),
        ],
        compiler_params=pltpu.CompilerParams(vmem_limit_bytes=20 * MIB),
        cost_estimate=pl.CostEstimate(
            flops=12 * rows * width * units,
            bytes_accessed=8 * rows * width,
            transcendentals=2 * rows * units,
        ),
        name="experts",
    )(local, remote, close(w_gate), close(w_up), close(w_down))


def pile_kernel(*refs):
    blocks, out = refs[:-1], refs[-1]
    out[...] = jnp.concatenate(
        [block[...].astype(jnp.float32) for block in blocks], axis=0
    ).astype(out.dtype)


def pile(blocks):
    rows, width = blocks[0].shape
    return pl.pallas_call(
        pile_kernel,
        in_specs=[NEAR] * len(blocks),
        out_specs=NEAR,
        out_shape=jax.ShapeDtypeStruct((len(blocks) * rows, width), blocks[0].dtype),
        compiler_params=pltpu.CompilerParams(vmem_limit_bytes=(4 + len(blocks)) * MIB),
        name="pile",
    )(*blocks)


def add_kernel(first, second, *outs):
    rows = outs[0].shape[0]
    total = first[...].astype(jnp.float32) + second[...].astype(jnp.float32)
    for at, out in enumerate(outs):
        out[...] = total[at * rows : (at + 1) * rows].astype(out.dtype)


def add_split(first, second, blocks):
    rows, width = first.shape
    each = rows // blocks
    return pl.pallas_call(
        add_kernel,
        in_specs=[NEAR, NEAR],
        out_specs=[NEAR] * blocks,
        out_shape=[jax.ShapeDtypeStruct((each, width), first.dtype)] * blocks,
        compiler_params=pltpu.CompilerParams(vmem_limit_bytes=(6 + blocks) * MIB),
        name="add_split",
    )(first, second)


def total(blocks):
    result = blocks[0][...].astype(jnp.float32)
    for block in blocks[1:]:
        result = result + block[...].astype(jnp.float32)
    return result.astype(jnp.bfloat16)


def total_kernel(*refs):
    refs[-1][...] = total(refs[:-1])


def total_of(blocks):
    return pl.pallas_call(
        total_kernel,
        in_specs=[NEAR] * len(blocks),
        out_specs=NEAR,
        out_shape=jax.ShapeDtypeStruct(blocks[0].shape, blocks[0].dtype),
        compiler_params=pltpu.CompilerParams(vmem_limit_bytes=(4 + len(blocks)) * MIB),
        name="total",
    )(*blocks)


def combine_kernel(place, base, weight, *refs):
    blocks, out = refs[:-1], refs[-1]
    part = jnp.dot(
        weight[place][:, :CAP], total(blocks), preferred_element_type=jnp.float32
    )
    out[...] = (base[...] + part).astype(out.dtype)


def combine(place, base, weight, blocks, result):
    return pl.pallas_call(
        functools.partial(combine_kernel, place),
        in_specs=[NEAR] * (2 + len(blocks)),
        out_specs=NEAR,
        out_shape=result,
        compiler_params=pltpu.CompilerParams(vmem_limit_bytes=(8 + len(blocks)) * MIB),
        name="combine",
    )(close(base), weight, *blocks)


def finish_kernel(parts, base, weight, other, out, held, sems):
    width = base.shape[1] // parts
    copies = []
    for part in range(parts):
        at = pl.ds(part * width, width)
        held[:, at] = (
            base[:, at]
            + jnp.dot(weight[1][:, :CAP], other[:, at], preferred_element_type=jnp.float32)
        ).astype(held.dtype)
        copies.append(pltpu.make_async_copy(held.at[:, at], out.at[:, at], sems.at[part]))
        copies[-1].start()
    for copy in copies:
        copy.wait()


def finish(base, weight, other):
    parts = 4
    return pl.pallas_call(
        functools.partial(finish_kernel, parts),
        in_specs=[NEAR] * 3,
        out_specs=pl.BlockSpec(memory_space=pl.ANY),
        out_shape=jax.ShapeDtypeStruct(base.shape, jnp.bfloat16),
        scratch_shapes=[
            pltpu.VMEM(base.shape, jnp.bfloat16),
            pltpu.SemaphoreType.DMA((parts,)),
        ],
        compiler_params=pltpu.CompilerParams(vmem_limit_bytes=8 * MIB),
        name="finish",
    )(close(base), weight, other)


def shards(
    resid, queries, keys, values, segment_ids, norm_gain, routes, route_gates, w_gate, w_up, w_down
):
    count = lax.axis_size("expert")
    own = lax.axis_index("expert")
    shard_count = count // E_WIN

    place = own % 4

    def moved(block, steps):
        pairs = [(i, i + steps[i % 4]) for i in range(count) if i % 4 in steps]
        return lax.ppermute(block, "expert", [pair for pair in pairs if pair[1] < count])

    across = {0: 3, 1: 3, 2: -1, 3: 3}
    passed = {1: 4, 2: -2}
    beside = {0: 1, 1: 1, 2: 1}

    def swapped(block, mask):
        return lax.ppermute(block, "expert", [(i, i ^ mask) for i in range(count)])

    seg_own = segment_ids.reshape(1, -1)
    beyond = 2 * WIN_DEV + 2
    delta_list = [
        0 * own,
        jnp.where(place == 1, beyond, 3),
        jnp.where(place == 0, 1, jnp.where(place == 1, 3, beyond)),
        jnp.where(place == 0, beyond, 1),
        0 * own + 2,
    ]
    my_expert = own // shard_count
    source = jnp.where(place < 2, 0, jnp.where(place == 2, 1, 2))
    scalars = jnp.stack(
        [jnp.where(own >= delta, delta, beyond) for delta in delta_list] + [my_expert, source]
    ).astype(jnp.int32)

    key_block = bundle(keys, seg_own)
    key_one, value_one = moved(key_block, across), moved(values, across)
    key_three, value_three = moved(key_block, beside), moved(values, beside)
    mine = bring(
        [
            queries, keys, values, seg_own, resid, norm_gain.reshape(1, -1), routes.T,
            route_gates.T,
        ],
        scalars,
    )
    key_two = moved(key_one, passed)
    value_one, mine = lax.optimization_barrier((value_one, mine))
    value_two = moved(value_one, passed)
    key_four = swapped(choose(scalars, [key_two, key_three, key_one]), 1)
    value_four = swapped(choose(scalars, [value_two, value_three, value_one]), 1)

    queries, keys, values, seg_own, resid, gain, routes_held, gates_held = mine
    mixed, keep, send, weight = attention(
        scalars,
        queries,
        [
            keys, values, key_one, value_one, key_two, value_two, key_three, value_three,
            key_four, value_four,
        ],
        seg_own, resid, gain, routes_held, gates_held,
    )
    gate_held, up_held = fetch(w_gate, weight), fetch(w_up, weight)
    partner = [(i, (i + shard_count) % count) for i in range(count)]
    masks = list(range(2, shard_count, 2))[::-1]
    got = lax.ppermute(send, "expert", partner)

    def spread(block):
        return [block] + [swapped(block, mask) for mask in masks]

    def both_cores(blocks):
        local = pile(blocks)
        return local, swapped(local, 1)

    def summed(parts):
        return add_split(parts[0], swapped(parts[1], 1), 1 + len(masks))

    def scattered(blocks):
        moved = [swapped(block, mask) for block, mask in zip(blocks[1:], masks)]
        return [blocks[0]] + moved[::-1]

    early_blocks = spread(keep)
    early_blocks, got, gate_held, up_held = lax.optimization_barrier(
        (early_blocks, got, gate_held, up_held)
    )
    early_rows = both_cores(early_blocks)
    held = [gate_held, up_held, fetch(w_down, early_rows[1])]
    early_parts = experts(*early_rows, *held)
    late_blocks = spread(got)
    late_blocks, early_parts = lax.optimization_barrier((late_blocks, early_parts))
    late_blocks = summed(experts(*both_cores(late_blocks), *held))
    early_blocks = summed(early_parts)
    late_blocks, early_blocks = lax.optimization_barrier((late_blocks, early_blocks))
    late_blocks = scattered(late_blocks)
    late_blocks[:-1], early_blocks = lax.optimization_barrier((late_blocks[:-1], early_blocks))
    early_blocks = scattered(early_blocks)
    back = total_of(late_blocks)
    other = lax.ppermute(back, "expert", partner)
    base = combine(0, mixed, weight, early_blocks, pltpu.VMEM(mixed.shape, jnp.float32))
    return finish(base, weight, other)


def solution(mesh):
    placed = (
        P(("groups", "expert"), None),
        P(("groups", "expert"), None),
        P(("groups", "expert"), None),
        P(("groups", "expert"), None),
        P(("groups", "expert")),
        P(),
        P(("groups", "expert"), None),
        P(("groups", "expert"), None),
        P(None, "expert"),
        P(None, "expert"),
        P("expert", None),
    )
    return jax.shard_map(
        shards, mesh=mesh, in_specs=placed, out_specs=P(("groups", "expert"), None), check_vma=False
    )
```

```python
import functools

import jax
import jax.numpy as jnp
from jax import lax
from jax.experimental import pallas as pl
from jax.experimental.pallas import tpu as pltpu
from jax.sharding import PartitionSpec as P

HEAD_DIM = 128
E_WIN = 2
WIN_DEV = 3
BLOCKS = 5
CAP = 20
SPARE = 16
HEADS_STEP = 32
MASKED = -1e30
MIB = 1024 * 1024


def far(x):
    return pltpu.with_memory_space_constraint(x, pltpu.HBM)


def close(x):
    return pltpu.with_memory_space_constraint(x, pltpu.VMEM)


NEAR = pl.BlockSpec(memory_space=pltpu.VMEM)


def bundle_kernel(keys, segs, out):
    rows, width = keys.shape
    out[:, :width] = keys[...]
    out[:, width:] = jnp.zeros((rows, HEAD_DIM), keys.dtype)
    out[:SPARE, width : width + rows] = jnp.broadcast_to(
        segs[...].astype(jnp.float32), (SPARE, rows)
    ).astype(keys.dtype)


def bundle(keys, segs):
    rows, width = keys.shape
    return pl.pallas_call(
        bundle_kernel,
        in_specs=[NEAR, NEAR],
        out_specs=NEAR,
        out_shape=pltpu.VMEM((rows, width + HEAD_DIM), keys.dtype),
        cost_estimate=pl.CostEstimate(
            flops=0, bytes_accessed=4 * rows * width, transcendentals=0
        ),
        compiler_params=pltpu.CompilerParams(vmem_limit_bytes=6 * MIB),
        name="bundle",
    )(far(keys), far(segs))


def choose_kernel(flags, first, second, third, out):
    for value, block in enumerate((first, second, third)):

        @pl.when(flags[6] == value)
        def _():
            out[...] = block[...]


def choose(flags, blocks):
    return pl.pallas_call(
        choose_kernel,
        in_specs=[pl.BlockSpec(memory_space=pltpu.SMEM)] + [NEAR] * 3,
        out_specs=NEAR,
        out_shape=jax.ShapeDtypeStruct(blocks[0].shape, blocks[0].dtype),
        compiler_params=pltpu.CompilerParams(vmem_limit_bytes=6 * MIB),
        name="choose",
    )(flags, *[close(block) for block in blocks])


def attention_kernel(
    deltas, q, k0, v0, k1, v1, k2, v2, k3, v3, k4, v4, seg0, resid, gain, routes, gates,
    mixed_out, keep_out, send_out, weight_out,
):
    rows, model = q.shape
    keys = BLOCKS * rows
    width = HEADS_STEP * HEAD_DIM

    seg_own = seg0[...].astype(jnp.float32)
    seg_row = jnp.concatenate(
        [seg_own]
        + [block[:SPARE, model:][0:1, :rows].astype(jnp.float32) for block in (k1, k2, k3, k4)],
        axis=1,
    )
    eye = lax.broadcasted_iota(jnp.int32, (rows, rows), 0) == lax.broadcasted_iota(
        jnp.int32, (rows, rows), 1
    )
    seg_col = jnp.sum(jnp.where(eye, seg_own, 0.0), axis=1, keepdims=True)
    lane = lax.broadcasted_iota(jnp.int32, (rows, keys), 1)
    sub = lax.broadcasted_iota(jnp.int32, (rows, keys), 0)
    block = lane // rows
    back = jnp.zeros_like(block)
    for at in range(1, BLOCKS):
        back = jnp.where(block == at, deltas[at], back)
    distance = sub - (lane - block * rows) + back * rows
    allowed = (distance >= 0) & (distance <= WIN_DEV * rows) & (seg_col == seg_row)
    bias = jnp.where(allowed, 0.0, MASKED)
    scale = 1.0 / HEAD_DIM**0.5
    heads = [slice(head * HEAD_DIM, (head + 1) * HEAD_DIM) for head in range(HEADS_STEP)]

    @pl.loop(0, model // width)
    def _(step):
        at = pl.ds(pl.multiple_of(step * width, width), width)
        query = q[:, at]
        key = jnp.concatenate([k0[:, at], k1[:, at], k2[:, at], k3[:, at], k4[:, at]], axis=0)
        value = jnp.concatenate([v0[:, at], v1[:, at], v2[:, at], v3[:, at], v4[:, at]], axis=0)
        scores = jnp.stack(
            [
                lax.dot_general(
                    query[:, cols], key[:, cols], (((1,), (1,)), ((), ())),
                    preferred_element_type=jnp.float32,
                )
                for cols in heads
            ]
        )
        scores = scores * scale + bias[None]
        expo = jnp.exp(scores - jnp.max(scores, axis=2, keepdims=True))
        denom = jnp.sum(expo, axis=2, keepdims=True)
        probs = expo.astype(jnp.bfloat16)
        outs = [
            jnp.dot(probs[head], value[:, cols], preferred_element_type=jnp.float32)
            / denom[head]
            for head, cols in enumerate(heads)
        ]
        mixed_out[:, at] = resid[:, at].astype(jnp.float32) + jnp.concatenate(outs, axis=1)

    mixed = mixed_out[...]
    normed = (
        mixed * lax.rsqrt(jnp.mean(mixed * mixed, axis=1, keepdims=True) + 1e-05) * gain[...]
    ).astype(jnp.bfloat16)
    across = lax.broadcasted_iota(jnp.int32, (rows, rows), 1)
    down = lax.broadcasted_iota(jnp.int32, (rows, rows), 0)
    upper = jnp.where(down < across, 1.0, 0.0).astype(jnp.bfloat16)
    eye = jnp.where(down == across, 1.0, 0.0).astype(jnp.bfloat16)
    slot = lax.broadcasted_iota(jnp.int32, (32, rows), 0)

    def picks(expert):
        hit = routes[...] == expert
        member = jnp.max(jnp.where(hit, 1.0, 0.0), axis=0, keepdims=True)
        weight = jnp.sum(
            jnp.where(hit, gates[...].astype(jnp.float32), 0.0), axis=0, keepdims=True
        )
        rank = jnp.dot(
            jnp.broadcast_to(member, (8, rows)).astype(jnp.bfloat16),
            upper,
            preferred_element_type=jnp.float32,
        )[0:1].astype(jnp.int32)
        return member > 0.5, weight, rank

    def spread(pick, weight):
        return lax.dot_general(
            eye,
            jnp.where(pick, weight, 0.0).astype(jnp.bfloat16),
            (((1,), (1,)), ((), ())),
            preferred_element_type=jnp.float32,
        ).astype(jnp.bfloat16)

    def packed(pick):
        return jnp.dot(
            jnp.where(pick, 1.0, 0.0).astype(jnp.bfloat16),
            normed,
            preferred_element_type=jnp.float32,
        ).astype(jnp.bfloat16)

    for place, out in ((0, keep_out), (1, send_out)):
        member, weight, rank = picks(deltas[5] if place == 0 else 1 - deltas[5])
        pick = (slot == rank) & member
        out[...] = packed(pick)[:CAP]
        weight_out[place] = spread(pick, weight)


def attention(deltas, q, pairs, seg_own, resid, gain, routes, gates):
    rows, width = q.shape
    return pl.pallas_call(
        attention_kernel,
        in_specs=[pl.BlockSpec(memory_space=pltpu.SMEM)] + [NEAR] * (6 + len(pairs)),
        out_specs=[NEAR] * 4,
        out_shape=[
            pltpu.VMEM((rows, width), jnp.float32),
            jax.ShapeDtypeStruct((CAP, width), jnp.bfloat16),
            jax.ShapeDtypeStruct((CAP, width), jnp.bfloat16),
            jax.ShapeDtypeStruct((E_WIN, rows, 32), jnp.bfloat16),
        ],
        compiler_params=pltpu.CompilerParams(vmem_limit_bytes=18 * MIB),
        cost_estimate=pl.CostEstimate(
            flops=4 * rows * BLOCKS * rows * width, bytes_accessed=8 * rows * width * 4,
            transcendentals=rows * BLOCKS * rows * (width // HEAD_DIM),
        ),
        name="attention",
    )(
        deltas, close(q), close(pairs[0]), close(pairs[1]), *pairs[2:], close(seg_own),
        close(resid), close(gain), close(routes), close(gates),
    )


def bring_kernel(count, *refs):
    sources, held, sems = refs[:count], refs[count + 1 : 2 * count + 1], refs[-1]
    copies = [
        pltpu.make_async_copy(source, target, sems.at[at])
        for at, (source, target) in enumerate(zip(sources, held))
    ]
    for copy in copies:
        copy.start()
    for copy in copies:
        copy.wait()


def bring(arrays, after):
    count = len(arrays)
    anywhere = pl.BlockSpec(memory_space=pl.ANY)
    return pl.pallas_call(
        functools.partial(bring_kernel, count),
        in_specs=[anywhere] * (count + 1),
        out_specs=[NEAR] * count,
        out_shape=[pltpu.VMEM(x.shape, x.dtype) for x in arrays],
        scratch_shapes=[pltpu.SemaphoreType.DMA((count,))],
        compiler_params=pltpu.CompilerParams(vmem_limit_bytes=2 * MIB),
        cost_estimate=pl.CostEstimate(
            flops=0, bytes_accessed=4 * sum(x.size for x in arrays), transcendentals=0
        ),
        name="bring",
    )(*[far(x) for x in arrays], after)


def fetch_kernel(parts, source, after, held, sems):
    depth = source.shape[0] // parts
    copies = []
    for part in range(parts):
        at = pl.ds(part * depth, depth)
        copies.append(pltpu.make_async_copy(source.at[at], held.at[at], sems.at[part]))
    for copy in copies:
        copy.start()
    for copy in copies:
        copy.wait()


def fetch(weights, after):
    parts = 4
    anywhere = pl.BlockSpec(memory_space=pl.ANY)
    return pl.pallas_call(
        functools.partial(fetch_kernel, parts),
        in_specs=[anywhere, anywhere],
        out_specs=NEAR,
        out_shape=pltpu.VMEM(weights.shape, weights.dtype),
        scratch_shapes=[pltpu.SemaphoreType.DMA((parts,))],
        compiler_params=pltpu.CompilerParams(vmem_limit_bytes=2 * MIB),
        cost_estimate=pl.CostEstimate(
            flops=0, bytes_accessed=4 * weights.size, transcendentals=0
        ),
        name="fetch",
    )(far(weights), after)


def experts_kernel(local, remote, w_gate, w_up, w_down, local_out, remote_out, x, hidden):
    width, units = w_gate.shape
    tile = min(1024, units)
    rows = local.shape[0]
    x[:rows] = local[...]
    x[rows:] = remote[...]

    @pl.loop(0, units // tile)
    def _(part):
        at = pl.ds(pl.multiple_of(part * tile, tile), tile)
        gate = jnp.dot(x[...], w_gate[:, at], preferred_element_type=jnp.float32)
        up = jnp.dot(x[...], w_up[:, at], preferred_element_type=jnp.float32)
        hidden[:, at] = (jax.nn.silu(gate) * up).astype(jnp.bfloat16)

    out = jnp.dot(hidden[...], w_down[...], preferred_element_type=jnp.float32)
    local_out[...] = out[:rows].astype(jnp.bfloat16)
    remote_out[...] = out[rows:].astype(jnp.bfloat16)


def experts(local, remote, w_gate, w_up, w_down):
    rows, width = local.shape
    units = w_gate.shape[1]
    return pl.pallas_call(
        experts_kernel,
        in_specs=[NEAR] * 5,
        out_specs=[NEAR] * 2,
        out_shape=[jax.ShapeDtypeStruct((rows, width), jnp.bfloat16)] * 2,
        scratch_shapes=[
            pltpu.VMEM((2 * rows, width), jnp.bfloat16),
            pltpu.VMEM((2 * rows, units), jnp.bfloat16),
        ],
        compiler_params=pltpu.CompilerParams(vmem_limit_bytes=20 * MIB),
        cost_estimate=pl.CostEstimate(
            flops=12 * rows * width * units,
            bytes_accessed=8 * rows * width,
            transcendentals=2 * rows * units,
        ),
        name="experts",
    )(local, remote, close(w_gate), close(w_up), close(w_down))


def pile_kernel(*refs):
    blocks, out = refs[:-1], refs[-1]
    out[...] = jnp.concatenate(
        [block[...].astype(jnp.float32) for block in blocks], axis=0
    ).astype(out.dtype)


def pile(blocks):
    rows, width = blocks[0].shape
    return pl.pallas_call(
        pile_kernel,
        in_specs=[NEAR] * len(blocks),
        out_specs=NEAR,
        out_shape=jax.ShapeDtypeStruct((len(blocks) * rows, width), blocks[0].dtype),
        compiler_params=pltpu.CompilerParams(vmem_limit_bytes=(4 + len(blocks)) * MIB),
        name="pile",
    )(*blocks)


def add_kernel(first, second, *outs):
    rows = outs[0].shape[0]
    total = first[...].astype(jnp.float32) + second[...].astype(jnp.float32)
    for at, out in enumerate(outs):
        out[...] = total[at * rows : (at + 1) * rows].astype(out.dtype)


def add_split(first, second, blocks):
    rows, width = first.shape
    each = rows // blocks
    return pl.pallas_call(
        add_kernel,
        in_specs=[NEAR, NEAR],
        out_specs=[NEAR] * blocks,
        out_shape=[jax.ShapeDtypeStruct((each, width), first.dtype)] * blocks,
        compiler_params=pltpu.CompilerParams(vmem_limit_bytes=(6 + blocks) * MIB),
        name="add_split",
    )(first, second)


def total(blocks):
    result = blocks[0][...].astype(jnp.float32)
    for block in blocks[1:]:
        result = result + block[...].astype(jnp.float32)
    return result.astype(jnp.bfloat16)


def total_kernel(*refs):
    refs[-1][...] = total(refs[:-1])


def total_of(blocks):
    return pl.pallas_call(
        total_kernel,
        in_specs=[NEAR] * len(blocks),
        out_specs=NEAR,
        out_shape=jax.ShapeDtypeStruct(blocks[0].shape, blocks[0].dtype),
        compiler_params=pltpu.CompilerParams(vmem_limit_bytes=(4 + len(blocks)) * MIB),
        name="total",
    )(*blocks)


def combine_kernel(place, base, weight, *refs):
    blocks, out = refs[:-1], refs[-1]
    part = jnp.dot(
        weight[place][:, :CAP], total(blocks), preferred_element_type=jnp.float32
    )
    out[...] = (base[...] + part).astype(out.dtype)


def combine(place, base, weight, blocks, result):
    return pl.pallas_call(
        functools.partial(combine_kernel, place),
        in_specs=[NEAR] * (2 + len(blocks)),
        out_specs=NEAR,
        out_shape=result,
        compiler_params=pltpu.CompilerParams(vmem_limit_bytes=(8 + len(blocks)) * MIB),
        name="combine",
    )(close(base), weight, *blocks)


def finish_kernel(parts, base, weight, other, out, held, sems):
    width = base.shape[1] // parts
    copies = []
    for part in range(parts):
        at = pl.ds(part * width, width)
        held[:, at] = (
            base[:, at]
            + jnp.dot(weight[1][:, :CAP], other[:, at], preferred_element_type=jnp.float32)
        ).astype(held.dtype)
        copies.append(pltpu.make_async_copy(held.at[:, at], out.at[:, at], sems.at[part]))
        copies[-1].start()
    for copy in copies:
        copy.wait()


def finish(base, weight, other):
    parts = 4
    return pl.pallas_call(
        functools.partial(finish_kernel, parts),
        in_specs=[NEAR] * 3,
        out_specs=pl.BlockSpec(memory_space=pl.ANY),
        out_shape=jax.ShapeDtypeStruct(base.shape, jnp.bfloat16),
        scratch_shapes=[
            pltpu.VMEM(base.shape, jnp.bfloat16),
            pltpu.SemaphoreType.DMA((parts,)),
        ],
        compiler_params=pltpu.CompilerParams(vmem_limit_bytes=8 * MIB),
        name="finish",
    )(close(base), weight, other)


def shards(
    resid, queries, keys, values, segment_ids, norm_gain, routes, route_gates, w_gate, w_up, w_down
):
    count = lax.axis_size("expert")
    own = lax.axis_index("expert")
    shard_count = count // E_WIN

    place = own % 4

    def moved(block, steps):
        pairs = [(i, i + steps[i % 4]) for i in range(count) if i % 4 in steps]
        return lax.ppermute(block, "expert", [pair for pair in pairs if pair[1] < count])

    across = {0: 3, 1: 3, 2: -1, 3: 3}
    passed = {1: 4, 2: -2}
    beside = {0: 1, 1: 1, 2: 1}

    def swapped(block, mask):
        return lax.ppermute(block, "expert", [(i, i ^ mask) for i in range(count)])

    seg_own = segment_ids.reshape(1, -1)
    beyond = 2 * WIN_DEV + 2
    delta_list = [
        0 * own,
        jnp.where(place == 1, beyond, 3),
        jnp.where(place == 0, 1, jnp.where(place == 1, 3, beyond)),
        jnp.where(place == 0, beyond, 1),
        0 * own + 2,
    ]
    my_expert = own // shard_count
    source = jnp.where(place < 2, 0, jnp.where(place == 2, 1, 2))
    scalars = jnp.stack(
        [jnp.where(own >= delta, delta, beyond) for delta in delta_list] + [my_expert, source]
    ).astype(jnp.int32)

    key_block = bundle(keys, seg_own)
    key_one, value_one = moved(key_block, across), moved(values, across)
    key_three, value_three = moved(key_block, beside), moved(values, beside)
    key_two = moved(key_one, passed)
    mine = bring(
        [
            queries, keys, values, seg_own, resid, norm_gain.reshape(1, -1), routes.T,
            route_gates.T,
        ],
        key_two,
    )
    value_two = moved(value_one, passed)
    key_four = swapped(choose(scalars, [key_two, key_three, key_one]), 1)
    key_four, mine = lax.optimization_barrier((key_four, mine))
    value_four = swapped(choose(scalars, [value_two, value_three, value_one]), 1)

    queries, keys, values, seg_own, resid, gain, routes_held, gates_held = mine
    mixed, keep, send, weight = attention(
        scalars,
        queries,
        [
            keys, values, key_one, value_one, key_two, value_two, key_three, value_three,
            key_four, value_four,
        ],
        seg_own, resid, gain, routes_held, gates_held,
    )
    gate_held, up_held = fetch(w_gate, weight), fetch(w_up, weight)
    partner = [(i, (i + shard_count) % count) for i in range(count)]
    masks = list(range(2, shard_count, 2))[::-1]
    got = lax.ppermute(send, "expert", partner)

    def spread(block):
        return [block] + [swapped(block, mask) for mask in masks]

    def both_cores(blocks):
        local = pile(blocks)
        return local, swapped(local, 1)

    def summed(parts):
        return add_split(parts[0], swapped(parts[1], 1), 1 + len(masks))

    def scattered(blocks):
        moved = [swapped(block, mask) for block, mask in zip(blocks[1:], masks)]
        return [blocks[0]] + moved[::-1]

    early_blocks = spread(keep)
    early_blocks, got, gate_held, up_held = lax.optimization_barrier(
        (early_blocks, got, gate_held, up_held)
    )
    early_rows = both_cores(early_blocks)
    held = [gate_held, up_held, fetch(w_down, early_rows[1])]
    early_parts = experts(*early_rows, *held)
    late_blocks = spread(got)
    late_blocks, early_parts = lax.optimization_barrier((late_blocks, early_parts))
    late_blocks = summed(experts(*both_cores(late_blocks), *held))
    early_blocks = summed(early_parts)
    late_blocks, early_blocks = lax.optimization_barrier((late_blocks, early_blocks))
    late_blocks = scattered(late_blocks)
    late_blocks[:-1], early_blocks = lax.optimization_barrier((late_blocks[:-1], early_blocks))
    early_blocks = scattered(early_blocks)
    back = total_of(late_blocks)
    other = lax.ppermute(back, "expert", partner)
    base = combine(0, mixed, weight, early_blocks, pltpu.VMEM(mixed.shape, jnp.float32))
    return finish(base, weight, other)


def solution(mesh):
    placed = (
        P(("groups", "expert"), None),
        P(("groups", "expert"), None),
        P(("groups", "expert"), None),
        P(("groups", "expert"), None),
        P(("groups", "expert")),
        P(),
        P(("groups", "expert"), None),
        P(("groups", "expert"), None),
        P(None, "expert"),
        P(None, "expert"),
        P("expert", None),
    )
    return jax.shard_map(
        shards, mesh=mesh, in_specs=placed, out_specs=P(("groups", "expert"), None), check_vma=False
    )
```
